32 devices in a mesh: seq: 16 (over z, y, core), ffn: 2 (over x).
Axes of the slice: x: 2, y: 2, z: 4, core: 2. Of those that a mesh axis runs over, the one named last changes fastest.
Arguments:
- tokens: bfloat16 [16384, 1024], P(('seq', 'ffn')), may hold values from -6 to 6
- spots: int32 [32, 128], P(('seq', 'ffn')), may hold values from 0 to 511, as said below
- counts: int32 [32], P(('seq', 'ffn')), may hold values from 42 to 128, as said below
- fill: bfloat16 [32, 128, 1024], P(('seq', 'ffn')), may hold values from -6 to 6
- cot: bfloat16 [32, 128, 1024], P(('seq', 'ffn')), may hold values from -6 to 6
- w_qkv: bfloat16 [1024, 3072], replicated, may hold values from -0.25 to 0.25
- b_q: bfloat16 [1024], replicated, may hold values from -3 to 3
- b_v: bfloat16 [1024], replicated, may hold values from -3 to 3
- w_out: bfloat16 [1024, 1024], replicated, may hold values from -0.375 to 0.375
- b_out: bfloat16 [1024], replicated, may hold values from -3 to 3
- gain_one: bfloat16 [1024], replicated, may hold values from 0.5 to 1.5
- shift_one: bfloat16 [1024], replicated, may hold values from -2 to 2
- w_up: bfloat16 [1024, 4096], P(None, 'ffn'), may hold values from -0.1875 to 0.1875
- b_up: bfloat16 [4096], P('ffn'), may hold values from -3 to 3
- w_down: bfloat16 [4096, 1024], P('ffn'), may hold values from -0.09375 to 0.09375
- b_down: bfloat16 [1024], replicated, may hold values from -3 to 3
- gain_two: bfloat16 [1024], replicated, may hold values from 0.5 to 1.5
- shift_two: bfloat16 [1024], replicated, may hold values from -2 to 2
Outputs:
- output: bfloat16 [16384, 1024], P(('seq', 'ffn'))
- grad_tokens: bfloat16 [16384, 1024], P(('seq', 'ffn'))
- grad_fill: bfloat16 [32, 128, 1024], P(('seq', 'ffn'))
- grad_w_qkv: float32 [1024, 3072], P('seq', 'ffn')
- grad_b_q: float32 [1024], replicated
- grad_b_v: float32 [1024], replicated
- grad_w_out: float32 [1024, 1024], P('seq', 'ffn')
- grad_b_out: float32 [1024], replicated
- grad_gain_one: float32 [1024], replicated
- grad_shift_one: float32 [1024], replicated
- grad_w_up: float32 [1024, 4096], P('seq', 'ffn')
- grad_b_up: float32 [4096], replicated
- grad_w_down: float32 [4096, 1024], P('ffn', 'seq')
- grad_b_down: float32 [1024], replicated
- grad_gain_two: float32 [1024], replicated
- grad_shift_two: float32 [1024], replicated
The draws below stay inside these ranges and needn't reach their ends.
Inputs may be any that keep to these rules, and one draw needn't show every extreme that they name: `spots`: in row s the first counts[s] entries are distinct positions of protein s; the other entries are 0. `counts`: some protein has exactly 128 listed positions and some exactly 42.
All inputs are finite; a program needn't handle non-finite values.
Results may differ from the reference program's by a relative error of at most 0.019.
Values may be sent and summed in bfloat16 or wider, within the bound.
No kernel may reach another device: no remote copies, remote signals or barrier semaphores. Data moves between devices by JAX's collectives and lax.ppermute only.
A program may use at most 192 MiB of HBM per device.

```python
import jax
import jax.numpy as jnp
from jax import lax

D = 1024
H = 16
HD = 64
FF = 4096
L = 512
MAXM = 128
SEQS = 32
TOKENS = 16384


def shared_counts(key):
    drawn = jax.random.randint(key, (SEQS,), MAXM // 3, MAXM + 1)
    top_index = jax.random.randint(jax.random.fold_in(key, 11), (), 0, SEQS)
    least_index = (top_index + 1) % SEQS
    numbers = jnp.arange(SEQS)
    drawn = jnp.where(numbers == top_index, MAXM, drawn)
    drawn = jnp.where(numbers == least_index, MAXM // 3, drawn)
    return drawn.astype(jnp.int32)


def draw_counts(key, part):
    drawn = shared_counts(key)
    return drawn


def draw_spots(key, part):
    drawn = shared_counts(key)
    key = jax.random.fold_in(key, 5)
    keys = jax.random.split(key, SEQS)
    orders = jax.vmap(lambda single: jax.random.permutation(single, L))(keys)[:, :MAXM]
    slot_ids = jnp.arange(MAXM)[None, :]
    return jnp.where(slot_ids < drawn[:, None], orders, 0).astype(jnp.int32)


def spiked(values, rng, source, target, shards_of, factor):
    owner, partner = [(jnp.arange(values.shape[dim]) // (values.shape[dim] // shards_of)).reshape([-1 if axis == dim else 1 for axis in range(values.ndim)]) for dim in (source, target)]
    chosen = jax.random.permutation(rng, shards_of)[partner]
    strong = (owner == chosen) | (owner == (partner + shards_of // 2) % shards_of)
    return jnp.where(strong, factor * values, values)


def steps_of(key, extent, shards, smallest, top_value):
    level, own = 1.0, jax.random.fold_in(key, 6)
    for position, blocks in shards:
        draws = jnp.exp(jax.random.uniform(jax.random.fold_in(own, position), (blocks,), jnp.float32, smallest / len(shards), top_value / len(shards)))
        level = level * jnp.repeat(draws, extent[position] // blocks).reshape([-1 if axis == position else 1 for axis in range(len(extent))])
    return level


def noise(rng, extent, scale, bound, pieces=(), kind=jnp.bfloat16):
    array = scale * jax.random.normal(rng, extent, jnp.float32)
    if pieces:
        array = array * steps_of(rng, extent, pieces, -0.22, 0.18)
    return jnp.clip(array, -bound, bound).astype(kind)


def noise_with(own_key, dims, width, most, pieces, heavy, held_as=jnp.bfloat16):
    values = width * jax.random.normal(own_key, dims, jnp.float32)
    if pieces:
        values = values * steps_of(own_key, dims, pieces, -0.22, 0.18)
    return jnp.clip(spiked(values, jax.random.fold_in(own_key, 3), *heavy), -most, most).astype(held_as)


def setup_inputs(seed: int = 0) -> dict:
    key_of = jax.random.split(jax.random.key(seed), 19)
    tokens = noise_with(key_of[0], (TOKENS, D), 1.0, 6.0, ((0, 32),), (0, 1, 32, 2.75))
    spots = draw_spots(jax.random.fold_in(key_of[18], 71), 0)
    counts = draw_counts(jax.random.fold_in(key_of[18], 71), 0)
    fill = noise(key_of[3], (SEQS, MAXM, D), 1.0, 6.0, ((0, 32),))
    cot = noise_with(key_of[4], (SEQS, MAXM, D), 1.0, 6.0, ((0, 32),), (0, 2, 32, 2.75))
    w_qkv = noise(key_of[5], (D, 3 * D), (D // 2) ** -0.5, 0.25)
    b_q = noise(key_of[6], (D,), 0.5, 3.0)
    b_v = noise(key_of[7], (D,), 0.5, 3.0)
    w_out = noise(key_of[8], (D, D), (D // 4) ** -0.5, 0.375)
    b_out = noise(key_of[9], (D,), 0.5, 3.0)
    gain_one = jnp.clip(1.0 + 0.1 * jax.random.normal(key_of[10], (D,), jnp.float32), 0.5, 1.5).astype(jnp.bfloat16)
    shift_one = noise(key_of[11], (D,), 0.3, 2.0)
    w_up = noise(key_of[12], (D, FF), D ** -0.5, 0.1875, ((1, 2),))
    b_up = noise(key_of[13], (FF,), 0.5, 3.0, ((0, 2),))
    w_down = noise(key_of[14], (FF, D), FF ** -0.5, 0.09375, ((0, 2),))
    b_down = noise(key_of[15], (D,), 0.5, 3.0)
    gain_two = jnp.clip(1.0 + 0.1 * jax.random.normal(key_of[16], (D,), jnp.float32), 0.5, 1.5).astype(jnp.bfloat16)
    shift_two = noise(key_of[17], (D,), 0.3, 2.0)
    return dict(tokens=tokens, spots=spots, counts=counts, fill=fill, cot=cot, w_qkv=w_qkv, b_q=b_q, b_v=b_v, w_out=w_out, b_out=b_out, gain_one=gain_one, shift_one=shift_one, w_up=w_up, b_up=b_up, w_down=w_down, b_down=b_down, gain_two=gain_two, shift_two=shift_two)


@jax.custom_vjp
def low(v):
    return lax.optimization_barrier(v.astype(jnp.bfloat16)).astype(jnp.float32)

@jax.custom_vjp
def low_back(v):
    return v

def low_keep(v):
    return (low(v), None)

def low_pass(kept, grad):
    return (grad,)

def back_keep(v):
    return (v, None)

def back_low(kept, grad):
    return (low(grad),)
low.defvjp(low_keep, low_pass)
low_back.defvjp(back_keep, back_low)
exact_erf_mode = lax.Precision.HIGHEST
epsilon = 1e-12

def layer_norm(value, gain, shift):
    centre = value - lax.optimization_barrier(jnp.mean(value, axis=-1, keepdims=True))
    spread = lax.optimization_barrier(jnp.mean(centre * centre, axis=-1, keepdims=True))
    return centre * lax.rsqrt(spread + epsilon) * gain + shift

def make_placed(spot_rows, count_rows):
    positions = jnp.arange(L, dtype=jnp.int32)
    slot_ids = jnp.arange(MAXM, dtype=jnp.int32)
    hits = (spot_rows[:, :, None] == positions[None, None, :]) & (slot_ids[None, :, None] < count_rows[:, None, None])
    return hits.astype(jnp.float32)

def block(tok_rows, fill_rows, placed_tokens, params):
    w_qkv, b_q, b_v, w_out, b_out, gain_one, shift_one, w_up, b_up, w_down, b_down, gain_two, shift_two = params
    kept = 1.0 - lax.optimization_barrier(jnp.sum(placed_tokens, axis=1))
    x = tok_rows * kept[..., None] + jnp.einsum('gml,gmd->gld', placed_tokens, fill_rows, precision=exact_erf_mode)
    group = x.shape[0]
    qkv = jnp.einsum('gld,de->gle', x, w_qkv, precision=exact_erf_mode) + jnp.concatenate([b_q, jnp.zeros_like(b_q), b_v])
    qkv = low_back(low(qkv))
    query = qkv[..., :D].reshape(group, L, H, HD)
    key_part = qkv[..., D:2 * D].reshape(group, L, H, HD)
    value = qkv[..., 2 * D:].reshape(group, L, H, HD)
    scores = low_back(jnp.einsum('glhe,gmhe->ghlm', query, key_part, precision=exact_erf_mode) * HD ** (-0.5))
    probs = jax.nn.softmax(scores, axis=-1)
    attended = jnp.einsum('ghlm,gmhe->glhe', low(probs), value, precision=exact_erf_mode).reshape(group, L, D)
    attended = low(low_back(attended))
    resid_one = x + low_back(jnp.einsum('gld,de->gle', attended, w_out, precision=exact_erf_mode)) + b_out
    normed_one = layer_norm(resid_one, gain_one, shift_one)
    normed_low = low(normed_one)
    pre = low_back(jnp.einsum('gld,df->glf', normed_low, w_up, precision=exact_erf_mode)) + b_up
    hidden = low(jax.nn.gelu(pre, approximate=False))
    resid_two = normed_one + low_back(jnp.einsum('glf,fd->gld', hidden, w_down, precision=exact_erf_mode)) + b_down
    return layer_norm(resid_two, gain_two, shift_two)

def reference(tokens, spots, counts, fill, cot, w_qkv, b_q, b_v, w_out, b_out, gain_one, shift_one, w_up, b_up, w_down, b_down, gain_two, shift_two):
    params = tuple((item.astype(jnp.float32) for item in (w_qkv, b_q, b_v, w_out, b_out, gain_one, shift_one, w_up, b_up, w_down, b_down, gain_two, shift_two)))
    group_count = 8
    groups = SEQS // group_count
    tok_all = tokens.astype(jnp.float32).reshape(groups, group_count, L, D)
    fill_all = fill.astype(jnp.float32).reshape(groups, group_count, MAXM, D)
    cot_all = cot.astype(jnp.float32).reshape(groups, group_count, MAXM, D)
    spot_all = spots.reshape(groups, group_count, MAXM)
    count_all = counts.reshape(groups, group_count)

    def step(carry, item):
        tok_rows, fill_rows, cot_rows, spot_rows, count_rows = item
        placed_tokens = make_placed(spot_rows, count_rows)

        def listed_rows(a, b, p):
            result = block(a, b, placed_tokens, p)
            picked = jnp.einsum('gml,gld->gmd', placed_tokens, result, precision=exact_erf_mode)
            return (picked, result)
        picked, pull, result = jax.vjp(listed_rows, tok_rows, fill_rows, params, has_aux=True)
        grad_tok, grad_fl, grad_par = pull(cot_rows)
        carry = jax.tree.map(jnp.add, carry, grad_par)
        return (carry, (result.astype(jnp.bfloat16), grad_tok.astype(jnp.bfloat16), grad_fl.astype(jnp.bfloat16)))
    zeros = jax.tree.map(jnp.zeros_like, params)
    sums, (outputs, grad_toks, grad_fills) = lax.scan(step, zeros, (tok_all, fill_all, cot_all, spot_all, count_all))
    g_wqkv, g_bq, g_bv, g_wout, g_bout, g_gone, g_sone, g_wup, g_bup, g_wdown, g_bdown, g_gtwo, g_stwo = sums
    return (outputs.reshape(TOKENS, D), grad_toks.reshape(TOKENS, D), grad_fills.reshape(SEQS, MAXM, D), g_wqkv, g_bq, g_bv, g_wout, g_bout, g_gone, g_sone, g_wup, g_bup, g_wdown, g_bdown, g_gtwo, g_stwo)
```

```python
import functools

import jax
import jax.numpy as jnp
from jax import lax
from jax.experimental import pallas as pl
from jax.experimental.pallas import tpu as pltpu
from jax.sharding import PartitionSpec as P

H = 16
F32 = jnp.float32
LOW = jnp.bfloat16
epsilon = 1e-12
LOG2E = 1.4426950408889634
NT = (((1,), (1,)), ((), ()))
WIDE = 512
STEP = 10**11


def mm(left, right):
    return jnp.dot(left, right, preferred_element_type=F32)


def mm_nt(left, right):
    return lax.dot_general(left, right, NT, preferred_element_type=F32)


def call(body, grid, in_specs, out_specs, out_shape, scratch=(), prefetch=1, mib=48, weight=0):
    return pl.pallas_call(
        body,
        grid_spec=pltpu.PrefetchScalarGridSpec(
            num_scalar_prefetch=prefetch,
            grid=grid,
            in_specs=in_specs,
            out_specs=out_specs,
            scratch_shapes=list(scratch),
        ),
        out_shape=out_shape,
        compiler_params=pltpu.CompilerParams(
            dimension_semantics=("arbitrary",) * len(grid), vmem_limit_bytes=mib << 20
        ),
        cost_estimate=pl.CostEstimate(flops=1 + weight * STEP, bytes_accessed=1, transcendentals=0),
    )


def spec(shape, index):
    return pl.BlockSpec(shape, index)


def shape(dims, dtype):
    return jax.ShapeDtypeStruct(dims, dtype)


def one_hot_rows(sc, spots, first, rows):
    slots = spots.shape[1]
    place = lax.broadcasted_iota(jnp.int32, (rows, slots), 0) + first
    slot = lax.broadcasted_iota(jnp.int32, (rows, slots), 1)
    hit = (place == spots) & (slot < sc[2])
    return jnp.where(hit, 1.0, 0.0)


def store_turned(sc, value, keep_ref, send_ref, first_column, chunk):
    columns = value.shape[1]
    for block in range(0, columns, 128):
        turned = jnp.transpose(value[:, block : block + 128]).astype(LOW)
        for part in range(0, 128, chunk):
            place = ((first_column + block + part) // chunk) ^ sc[0]
            piece = turned[part : part + chunk]
            at = ((place // 2) % 2) * (keep_ref.shape[0] // 2) + place // 4

            @pl.when(place % 2 == 0)
            def _():
                keep_ref[at] = piece

            @pl.when(place % 2 == 1)
            def _():
                send_ref[at] = piece


def qkv_body(chunk, sc, tokens, spots, fill, w, bias, x_out, keep, send, qkv):
    @pl.when(pl.program_id(0) == 0)
    def _():
        placed = one_hot_rows(sc, spots[...], 0, tokens.shape[0])
        kept = 1.0 - jnp.sum(placed, axis=1, keepdims=True)
        x = tokens[...].astype(F32) * kept + mm(placed.astype(LOW), fill[...])
        x_out[...] = x.astype(LOW)
        store_turned(sc, x, keep, send, 0, chunk)

    qkv[...] = (mm(x_out[...], w[...]) + bias[...]).astype(LOW)


def embed_qkv(sc, tokens, spots, fill, w_qkv, bias, n_seq):
    rows, width = tokens.shape
    out = w_qkv.shape[1]
    block = 512
    chunk = width // n_seq
    turned = (n_seq // 2, chunk, rows)
    whole = lambda j, sc: (0, 0)
    return call(
        functools.partial(qkv_body, chunk),
        (out // block,),
        [
            spec((rows, width), whole),
            spec(spots.shape, whole),
            spec(fill.shape, whole),
            spec((width, block), lambda j, sc: (0, j)),
            spec((1, block), lambda j, sc: (0, j)),
        ],
        [
            spec((rows, width), whole),
            spec(turned, lambda j, sc: (0, 0, 0)),
            spec(turned, lambda j, sc: (0, 0, 0)),
            spec((rows, block), lambda j, sc: (0, j)),
        ],
        [shape((rows, width), LOW), shape(turned, LOW), shape(turned, LOW), shape((rows, out), LOW)],
    )(sc, tokens, spots, fill, w_qkv, bias)


def head_masks(width, size, factor):
    lane = lax.broadcasted_iota(jnp.int32, (1, width), 1)
    return [
        jnp.where(lane // size == n, factor, 0.0).astype(LOW) for n in range(width // size)
    ]


def attend_body(chunk, scale, sc, q, k, v, att, keep, send, logs):
    rows, width = q.shape
    size = width // 2
    masks = head_masks(width, size, scale)
    lane = lax.broadcasted_iota(jnp.int32, (1, width), 1)
    mixed, stats = [], []
    for mask in masks:
        scores = mm_nt(q[...] * mask, k[...])
        peak = jnp.max(scores, axis=1, keepdims=True) * LOG2E
        expo = jnp.exp2(scores * LOG2E - peak)
        total = jnp.sum(expo, axis=1, keepdims=True)
        mixed.append(mm(expo.astype(LOW), v[...]) / total)
        stats.append(peak + jnp.log2(total))
    both = jnp.where(lane < size, mixed[0], mixed[1])
    att[...] = both.astype(LOW)
    table = jnp.where(lane == 0, stats[0], stats[1])
    logs[0] = jnp.transpose(table)[0:2]
    place_first = pl.program_id(0) * width
    store_turned(sc, both, keep, send, place_first, chunk)


def attend(sc, qkv, n_seq):
    rows = qkv.shape[0]
    width = qkv.shape[1] // 3
    size = width // H
    pair = 2 * size
    pairs = width // pair
    chunk = width // n_seq
    turned = (n_seq // 2, chunk, rows)
    whole = lambda j, sc: (0, 0, 0)
    return call(
        functools.partial(attend_body, chunk, size ** (-0.5)),
        (pairs,),
        [
            spec((rows, pair), lambda j, sc: (0, j)),
            spec((rows, pair), lambda j, sc: (0, pairs + j)),
            spec((rows, pair), lambda j, sc: (0, 2 * pairs + j)),
        ],
        [
            spec((rows, pair), lambda j, sc: (0, j)),
            spec(turned, whole),
            spec(turned, whole),
            spec((1, 2, rows), lambda j, sc: (j, 0, 0)),
        ],
        [
            shape((rows, width), LOW),
            shape(turned, LOW),
            shape(turned, LOW),
            shape((pairs, 2, rows), F32),
        ],
    )(sc, qkv, qkv, qkv)


def norm_one_body(chunk, sc, att, w, x, b, gain, shift, hat, inv, low, keep, send):
    value = x[...].astype(F32) + mm(att[...], w[...]) + b[...]
    centre = value - jnp.mean(value, axis=-1, keepdims=True)
    spread = jnp.mean(centre * centre, axis=-1, keepdims=True)
    inverse = lax.rsqrt(spread + epsilon)
    scaled = centre * inverse
    hat[...] = scaled
    inv[...] = inverse
    normed = scaled * gain[...] + shift[...]
    low[...] = normed.astype(LOW)
    store_turned(sc, normed, keep, send, 0, chunk)


def norm_one(sc, att, w_out, x, b_out, gain, shift, n_seq):
    rows, width = x.shape
    block = 128
    chunk = width // n_seq
    turned = (n_seq // 2, chunk, rows)
    row = lambda i, sc: (i, 0)
    whole = lambda i, sc: (0, 0)
    vector = spec((1, width), whole)
    return call(
        functools.partial(norm_one_body, chunk),
        (rows // block,),
        [spec((block, width), row), spec((width, width), whole), spec((block, width), row), vector, vector, vector],
        [
            spec((block, width), row),
            spec((block, 1), row),
            spec((block, width), row),
            spec((n_seq // 2, chunk, block), lambda i, sc: (0, 0, i)),
            spec((n_seq // 2, chunk, block), lambda i, sc: (0, 0, i)),
        ],
        [
            shape((rows, width), F32),
            shape((rows, 1), F32),
            shape((rows, width), LOW),
            shape(turned, LOW),
            shape(turned, LOW),
        ],
    )(sc, att, w_out, x, b_out, gain, shift)


TAIL = tuple(0.5 * c for c in (0.254829592, -0.284496736, 1.421413741, -1.453152027, 1.061405429))
TAIL_P = 0.3275911 * 0.7071067811865476


def gelu_both(x):
    t = 1.0 / (1.0 + TAIL_P * jnp.abs(x))
    bell = jnp.exp2(x * x * (-0.5 * LOG2E))
    poly = TAIL[4]
    for c in TAIL[3::-1]:
        poly = poly * t + c
    tail = poly * t * bell
    mass = jnp.where(x < 0.0, tail, 1.0 - tail)
    return x * mass, mass + x * bell * 0.3989422804014327


def ffn_specs(split, width, part):
    if split == "own":
        ups = [spec((width, WIDE), lambda j, sc: (0, j))]
        downs = [spec((WIDE, width), lambda j, sc: (j, 0))]
        return ups, downs, WIDE
    if split == "stack":
        ups = [spec((None, width, part), lambda j, sc: (j, 0, 0))]
        downs = [spec((None, part, width), lambda j, sc: (j, 0, 0))]
        return ups, downs, part
    near = lambda j, sc: (jnp.minimum(j, 2), 0, 0)
    far = lambda j, sc: (0, 0, 0)
    ups = [spec((None, width, part), at) for at in (near, near, far, far)]
    downs = [spec((None, part, width), at) for at in (near, near, far, far)]
    return ups, downs, part


def column_block(split):
    if split == "pairs":
        return lambda j, sc: (0, j ^ ((sc[0] // 2) % 4))
    return lambda j, sc: (0, j)


def for_pieces(split, size, sc, ups, downs, work):
    if split != "pairs":
        work([(ups[0], downs[0], 0)])
        return
    core = sc[0] % 2
    places = [pl.multiple_of(core * size, size), pl.multiple_of((1 - core) * size, size)]
    step = pl.program_id(0)
    pl.when(step < 3)(lambda: work(list(zip(ups[:2], downs[:2], places))))
    pl.when(step == 3)(lambda: work(list(zip(ups[2:], downs[2:], places))))


def ffn_fwd_body(split, size, n, first, sc, *refs):
    low, bias = refs[:2]
    ups, downs = refs[2 : 2 + n], refs[2 + n : 2 + 2 * n]
    rest = refs[2 + 2 * n :]
    start = None
    if not first:
        start, rest = rest[0], rest[1:]
    hidden, slope, total = rest
    @pl.when(pl.program_id(0) == 0)
    def _():
        total[...] = jnp.zeros_like(total) if first else start[...]

    def work(pieces):
        mixed = None
        for up, down, offset in pieces:
            columns = pl.ds(offset, size)
            pre = mm(low[...], up[...]) + bias[:, columns]
            act, grad = gelu_both(pre)
            act = act.astype(LOW)
            hidden[:, columns] = act
            slope[:, columns] = grad.astype(LOW)
            product = mm(act, down[...])
            mixed = product if mixed is None else mixed + product
        total[...] += mixed

    for_pieces(split, size, sc, ups, downs, work)


def ffn_fwd(sc, low, bias, ups, downs, split, start=None):
    rows, width = low.shape
    units = bias.shape[1]
    part = ups[0].shape[-1]
    up_specs, down_specs, size = ffn_specs(split, width, part)
    step = WIDE if split != "stack" else part
    whole = lambda j, sc: (0, 0)
    column = column_block(split)
    total = spec((rows, width), whole)
    first = start is None
    return call(
        functools.partial(ffn_fwd_body, split, size, len(ups), first),
        (units // step,),
        [total, spec((1, step), column)] + up_specs + down_specs + ([] if first else [total]),
        [spec((rows, step), column), spec((rows, step), column), total],
        [shape((rows, units), LOW), shape((rows, units), LOW), shape((rows, width), F32)],
    )(sc, low, bias, *ups, *downs, *([] if first else [start]))


def ffn_bwd_body(split, size, n, first, sc, *refs):
    low, slope = refs[:2]
    ups, downs = refs[2 : 2 + n], refs[2 + n : 2 + 2 * n]
    rest = refs[2 + 2 * n :]
    start = None
    if not first:
        start, rest = rest[0], rest[1:]
    g_low, sums, total = rest
    @pl.when(pl.program_id(0) == 0)
    def _():
        total[...] = jnp.zeros_like(total) if first else start[...]

    def work(pieces):
        mixed = None
        for up, down, offset in pieces:
            columns = pl.ds(offset, size)
            g_pre = mm_nt(low[...], down[...]) * slope[:, columns].astype(F32)
            sums[:, columns] = jnp.sum(g_pre, axis=0, keepdims=True)
            rounded = g_pre.astype(LOW)
            g_low[:, columns] = rounded
            product = mm_nt(rounded, up[...])
            mixed = product if mixed is None else mixed + product
        total[...] += mixed

    for_pieces(split, size, sc, ups, downs, work)


def ffn_bwd(sc, low, slope, ups, downs, split, start=None):
    rows, width = low.shape
    units = slope.shape[1]
    part = ups[0].shape[-1]
    up_specs, down_specs, size = ffn_specs(split, width, part)
    step = WIDE if split != "stack" else part
    whole = lambda j, sc: (0, 0)
    column = column_block(split)
    total = spec((rows, width), whole)
    first = start is None
    return call(
        functools.partial(ffn_bwd_body, split, size, len(ups), first),
        (units // step,),
        [total, spec((rows, step), column)] + up_specs + down_specs + ([] if first else [total]),
        [spec((rows, step), column), spec((1, step), column), total],
        [shape((rows, units), LOW), shape((1, units), F32), shape((rows, width), F32)],
    )(sc, low, slope, *ups, *downs, *([] if first else [start]))


def norm_back(hat, inverse, gain, grad):
    inner = grad * gain
    mean = jnp.mean(inner, axis=-1, keepdims=True)
    along = jnp.mean(inner * hat, axis=-1, keepdims=True)
    return inverse * (inner - mean - hat * along)


def add_sums(sums, rows):
    @pl.when(pl.program_id(0) == 0)
    def _():
        sums[...] = jnp.zeros_like(sums)

    for n, value in enumerate(rows):
        sums[n : n + 1, :] += jnp.sum(value, axis=0, keepdims=True)


def norm_two_body(chunk, sc, mixed, hat_one, gain_one, shift_one, b_down, gain, shift, spots, cot, out, grad, low, keep, send, sums):
    rows = mixed.shape[0]
    value = hat_one[...] * gain_one[...] + shift_one[...] + mixed[...] + b_down[...]
    centre = value - jnp.mean(value, axis=-1, keepdims=True)
    spread = jnp.mean(centre * centre, axis=-1, keepdims=True)
    inverse = lax.rsqrt(spread + epsilon)
    hat = centre * inverse
    out[...] = (hat * gain[...] + shift[...]).astype(LOW)
    placed = one_hot_rows(sc, spots[...], pl.program_id(0) * rows, rows)
    out_grad = mm(placed.astype(LOW), cot[...])
    result = norm_back(hat, inverse, gain[...], out_grad)
    grad[...] = result
    low[...] = result.astype(LOW)
    store_turned(sc, result, keep, send, 0, chunk)
    add_sums(sums, (out_grad * hat, out_grad, result))


def norm_two(sc, mixed, hat_one, gain_one, shift_one, b_down, gain, shift, spots, cot, n_seq):
    rows, width = mixed.shape
    block = 128
    chunk = width // n_seq
    turned = (n_seq // 2, chunk, rows)
    row = lambda i, sc: (i, 0)
    whole = lambda i, sc: (0, 0)
    vector = spec((1, width), whole)
    tile = spec((block, width), row)
    return call(
        functools.partial(norm_two_body, chunk),
        (rows // block,),
        [tile, tile, vector, vector, vector, vector, vector, spec(spots.shape, whole), spec(cot.shape, whole)],
        [
            tile,
            tile,
            tile,
            spec((n_seq // 2, chunk, block), lambda i, sc: (0, 0, i)),
            spec((n_seq // 2, chunk, block), lambda i, sc: (0, 0, i)),
            spec((8, width), whole),
        ],
        [
            shape((rows, width), LOW),
            shape((rows, width), F32),
            shape((rows, width), LOW),
            shape(turned, LOW),
            shape(turned, LOW),
            shape((8, width), F32),
        ],
        weight=1,
    )(sc, mixed, hat_one, gain_one, shift_one, b_down, gain, shift, spots, cot)


def norm_one_back_body(sc, grad_two, ffn, hat, inv, gain, w, grad, low, g_att, sums):
    g_normed = grad_two[...] + ffn[...]
    result = norm_back(hat[...], inv[...], gain[...], g_normed)
    grad[...] = result
    rounded = result.astype(LOW)
    low[...] = rounded
    g_att[...] = mm_nt(rounded, w[...]).astype(LOW)
    add_sums(sums, (g_normed * hat[...], g_normed, result))


def norm_one_back(sc, grad_two, ffn, hat, inv, gain, w_out):
    rows, width = hat.shape
    block = 128
    row = lambda i, sc: (i, 0)
    whole = lambda i, sc: (0, 0)
    tile = spec((block, width), row)
    return call(
        norm_one_back_body,
        (rows // block,),
        [tile, tile, tile, spec((block, 1), row), spec((1, width), whole), spec((width, width), whole)],
        [tile, tile, tile, spec((8, width), whole)],
        [shape((rows, width), F32), shape((rows, width), LOW), shape((rows, width), LOW), shape((8, width), F32)],
    )(sc, grad_two, ffn, hat, inv, gain, w_out)


def attend_back_body(scale, sc, q, k, v, att, g_att, logs, g_qkv, sums):
    rows, width = q.shape
    size = width // 2
    k_all, v_all = k[...], v[...]
    ones = head_masks(width, size, 1.0)
    halves = head_masks(width, size, scale)
    inner = jnp.transpose(att[...].astype(F32) * g_att[...].astype(F32))
    k_turned = jnp.transpose(k_all.astype(F32) * scale).astype(LOW)
    g_v = g_k = None
    g_q = []
    for n in range(2):
        q_one = q[...] * halves[n]
        g_one = g_att[...] * ones[n]
        scores = mm_nt(k_all, q_one)
        probs = jnp.exp2(scores * LOG2E - logs[0, n : n + 1, :])
        g_probs = mm_nt(v_all, g_one)
        level = jnp.sum(inner[n * size : (n + 1) * size], axis=0, keepdims=True)
        g_scores = (probs * (g_probs - level)).astype(LOW)
        part_v = mm(probs.astype(LOW), g_one)
        part_k = mm(g_scores, q_one)
        g_v = part_v if g_v is None else g_v + part_v
        g_k = part_k if g_k is None else g_k + part_k
        g_q.append(mm(k_turned[n * size : (n + 1) * size], g_scores))
    query = jnp.transpose(jnp.concatenate(g_q, axis=0)).astype(LOW)
    value = g_v.astype(LOW)
    g_qkv[0] = query
    g_qkv[1] = g_k.astype(LOW)
    g_qkv[2] = value
    sums[0:1, :] = jnp.sum(query.astype(F32), axis=0, keepdims=True)
    sums[1:2, :] = jnp.sum(value.astype(F32), axis=0, keepdims=True)


def attend_back(sc, qkv, att, g_att, logs):
    rows, width = att.shape
    size = width // H
    pair = 2 * size
    pairs = width // pair
    tile = spec((rows, pair), lambda j, sc: (0, j))
    return call(
        functools.partial(attend_back_body, size ** (-0.5)),
        (pairs,),
        [
            tile,
            spec((rows, pair), lambda j, sc: (0, pairs + j)),
            spec((rows, pair), lambda j, sc: (0, 2 * pairs + j)),
            tile,
            tile,
            spec((1, 2, rows), lambda j, sc: (j, 0, 0)),
        ],
        [spec((3, rows, pair), lambda j, sc: (0, 0, j)), spec((2, pair), lambda j, sc: (0, j))],
        [shape((3, rows, width), LOW), shape((2, width), F32)],
    )(sc, qkv, qkv, qkv, att, g_att, logs)


def token_grads_body(sc, g_qkv, w, base, spots, spots_column, tokens_out, fill_out, total):
    rows = base.shape[0]
    width = base.shape[1]
    step = pl.program_id(0)
    grad = base[...]
    for n in range(3):
        grad = grad + mm_nt(g_qkv[n], w[:, n * width : (n + 1) * width])
    placed = one_hot_rows(sc, spots[...], step * rows, rows)
    kept = 1.0 - jnp.sum(placed, axis=1, keepdims=True)
    tokens_out[...] = (grad * kept).astype(LOW)
    slots = spots_column.shape[0]
    place = lax.broadcasted_iota(jnp.int32, (slots, rows), 1) + step * rows
    slot = lax.broadcasted_iota(jnp.int32, (slots, rows), 0)
    hit = (place == spots_column[...]) & (slot < sc[2])
    picked = mm(jnp.where(hit, 1.0, 0.0).astype(LOW), grad.astype(LOW))

    @pl.when(step == 0)
    def _():
        total[...] = picked

    @pl.when(step > 0)
    def _():
        total[...] += picked

    fill_out[...] = total[...].astype(LOW)


def token_grads(sc, g_qkv, w_qkv, base, spots, slots):
    rows, width = base.shape
    block = 128
    row = lambda i, sc: (i, 0)
    whole = lambda i, sc: (0, 0)
    tile = spec((block, width), row)
    return call(
        token_grads_body,
        (rows // block,),
        [
            spec((3, block, width), lambda i, sc: (0, i, 0)),
            spec(w_qkv.shape, whole),
            tile,
            spec(spots.shape, whole),
            spec((slots, 1), whole),
        ],
        [tile, spec((slots, width), whole)],
        [shape((rows, width), LOW), shape((slots, width), LOW)],
        scratch=[pltpu.VMEM((slots, width), F32)],
    )(sc, g_qkv, w_qkv, base, spots, spots.reshape(slots, 1))


def weight_body(counts, kinds, lefts, sc, *refs):
    used = 2 * (1 + max(lefts))
    left_refs, ins = refs[:used], refs[used : used + 2 * len(counts)]
    outs = list(refs[used + 2 * len(counts) :])
    slots = {}
    for kind, copies in (("halved", 2), ("whole", 1)):
        if kind in kinds:
            slots[kind], outs = outs[:copies], outs[copies:]
    step = pl.program_id(0)
    first = 0
    for n, (count, kind, at) in enumerate(zip(counts, kinds, lefts)):
        left, left_other = left_refs[2 * at : 2 * at + 2]
        mine, other = ins[2 * n], ins[2 * n + 1]

        def work(left=left, left_other=left_other, mine=mine, other=other, kind=kind):
            places, _, depth = left.shape
            rows_of = lambda ref: ref[...].reshape(-1, depth)
            total = mm(rows_of(left), mine[...]) + mm(rows_of(left_other), other[...])
            total = total.astype(LOW).reshape(places, -1, total.shape[-1])
            if kind == "whole":
                slots[kind][0][...] = total
            else:
                slots[kind][0][...] = total[: places // 2]
                slots[kind][1][...] = total[places // 2 :]

        if len(counts) == 1:
            work()
        else:
            pl.when((step >= first) & (step < first + count))(work)
        first += count


def weight_grad(sc, lefts, segments):
    places, chunk, depth = lefts[0][0].shape
    left_spec = spec((places, chunk, depth), lambda j, sc: (0, 0, 0))
    in_specs = [left_spec] * (2 * len(lefts))
    operands = [value for pair in lefts for value in pair]
    first = 0
    for mine, other, count, index, kind, matrix in segments:
        def at(j, sc, first=first, count=count, index=index):
            return index(jnp.clip(j - first, 0, count - 1), sc)

        block = (depth, WIDE) if mine.ndim == 2 else (None, depth, WIDE)
        in_specs += [spec(block, at), spec(block, at)]
        operands += [mine, other]
        first += count
    blocks = first
    out_specs, out_shapes = [], []
    done = 0
    for kind in ("halved", "whole"):
        count = sum(item[2] for item in segments if item[4] == kind)
        if count:
            kept = places if kind == "whole" else places // 2
            at = lambda j, sc, done=done, count=count: (jnp.clip(j - done, 0, count - 1), 0, 0, 0)
            copies = 1 if kind == "whole" else 2
            out_specs += [spec((None, kept, chunk, WIDE), at)] * copies
            out_shapes += [shape((count, kept, chunk, WIDE), LOW)] * copies
            done += count
    pick = lambda n: tuple(item[n] for item in segments)
    return call(
        functools.partial(weight_body, pick(2), pick(4), pick(5)),
        (blocks,),
        in_specs,
        out_specs,
        out_shapes,
    )(sc, *operands)


def add_body(count, sc, *refs):
    for n in range(count):
        keep, got = refs[2 * n], refs[2 * n + 1]
        left, sent = refs[2 * count + 2 * n], refs[2 * count + 2 * n + 1]
        total = (keep[...].astype(F32) + got[...].astype(F32)).astype(LOW)
        left[...] = total[:, :, 0]
        sent[...] = total[:, :, 1]


def add_halves(sc, items):
    tile = WIDE // 2
    in_specs, out_specs, out_shapes, operands = [], [], [], []
    for keep, got, dims in items:
        for value in (keep, got):
            operands.append(value.reshape(dims + (WIDE,)))
            in_specs.append(spec(dims + (tile,), lambda j, sc: (0, 0, 0, 0, j)))
        half = dims[:2] + dims[3:]
        out_specs += [spec(half + (tile,), lambda j, sc: (0, 0, 0, j))] * 2
        out_shapes += [shape(half + (WIDE,), LOW)] * 2
    found = call(functools.partial(add_body, len(items)), (WIDE // tile,), in_specs, out_specs, out_shapes, weight=1)(
        sc, *operands
    )
    return [(found[2 * n], found[2 * n + 1]) for n in range(len(items))]


def last_body(plan, sc, *refs):
    ins = len(plan) * 2
    places = {}
    for n, (blocks, targets) in enumerate(plan):
        keep, got = refs[2 * n], refs[2 * n + 1]
        for block, (target, turned) in zip(range(blocks), targets):
            out = refs[ins + target]
            at = places.get(target, 0)
            total = keep[block].astype(F32) + got[block].astype(F32)
            if turned:
                out[at : at + WIDE, :] = jnp.transpose(total)
            else:
                out[:, at : at + WIDE] = total
            places[target] = at + WIDE


def add_last(sc, items, outs):
    whole = lambda n: (lambda j, sc: (0,) * n)
    operands = [value for item in items for value in item[:2]]
    plan = tuple((item[0].shape[0], item[2]) for item in items)
    return call(
        functools.partial(last_body, plan),
        (1,),
        [spec(value.shape, whole(3)) for value in operands],
        [spec(dims, whole(2)) for dims in outs],
        [shape(dims, F32) for dims in outs],
        weight=1,
    )(sc, *operands)


def stack_body(sc, *refs):
    count = len(refs) - 2
    out, sems = refs[count], refs[count + 1]
    copies = [pltpu.make_async_copy(refs[n], out.at[n], sems.at[n]) for n in range(count)]
    for copy in copies:
        copy.start()
    for copy in copies:
        copy.wait()


def stack(sc, *values):
    anywhere = pl.BlockSpec(memory_space=pl.ANY)
    return call(
        stack_body,
        (1,),
        [anywhere] * len(values),
        anywhere,
        shape((len(values),) + values[0].shape, LOW),
        scratch=[pltpu.SemaphoreType.DMA((len(values),))],
        weight=1,
    )(sc, *values)


def swap(value, axis, bit):
    size = lax.axis_size(axis)
    return lax.ppermute(value, axis, [(n, n ^ bit) for n in range(size)])


def halves(value, bits, step):
    shards, blocks, places, chunk, wide = value.shape
    axis, bit = step
    if axis == "ffn":
        return value[: shards // 2], value[shards // 2 :], bits
    at = bits.index(bit)
    low = 1 << (len(bits) - 1 - at)
    parts = value.reshape(shards, blocks, places // (2 * low), 2, low, chunk, wide)
    dims = (shards, blocks, places // 2, chunk, wide)
    return (
        parts[:, :, :, 0].reshape(dims),
        parts[:, :, :, 1].reshape(dims),
        bits[:at] + bits[at + 1 :],
    )


class Line:
    def __init__(self):
        self.last = None

    def put(self, *values):
        if self.last is None:
            return values if len(values) > 1 else values[0]
        tied = lax.optimization_barrier(values + (self.last,))[:-1]
        return tied if len(values) > 1 else tied[0]

    def mark(self, value):
        self.last = value


class Stream:
    def __init__(self, line, bits, steps, whole=None, keep=None, send=None):
        self.line, self.bits, self.steps = line, list(bits), list(steps)
        if keep is None:
            keep, send, self.bits = halves(whole, self.bits, self.steps[0])
        elif self.steps[0][0] == "seq":
            self.bits.remove(self.steps[0][1])
        self.post(keep, send)

    def post(self, keep, send):
        self.keep = keep
        self.got = swap(send, *self.steps.pop(0))

    def advance(self):
        keep, got = self.line.put(self.keep, self.got)
        if self.steps:
            step = self.steps[0]
            keep_a, send_a, left = halves(keep, self.bits, step)
            keep_b, send_b, left = halves(got, self.bits, step)
            self.bits = left
            add = lambda a, b: (a.astype(F32) + b.astype(F32)).astype(LOW)
            send = add(send_a, send_b)
            keep = add(keep_a, keep_b)
            self.line.mark(keep)
            self.post(keep, send)
            return None
        total = keep.astype(F32) + got.astype(F32)
        self.line.mark(total)
        return total

    def finish(self):
        while True:
            total = self.advance()
            if total is not None:
                return total


class Streams:
    def __init__(self, sc, line, items):
        self.sc, self.line, self.items = sc, line, []
        for keep, send, bits, steps in items:
            axis, bit = steps[0]
            bits = [b for b in bits if axis != "seq" or b != bit]
            self.items.append([keep, swap(send, axis, bit), keep.shape, bits, list(steps[1:])])

    def advance(self):
        work = []
        tied = self.line.put(*[value for item in self.items for value in item[:2]])
        for n, (_, _, dims, bits, steps) in enumerate(self.items):
            shards, blocks, places, chunk, _ = dims
            axis, bit = steps[0]
            if axis == "ffn":
                split = (1, 1, 2, dims[0] // 2 * blocks * places * chunk)
                left = (shards // 2, blocks, places, chunk, WIDE)
            else:
                at = bits.index(bit)
                low = 1 << (len(bits) - 1 - at)
                split = (shards * blocks, places // (2 * low), 2, low * chunk)
                left = (shards, blocks, places // 2, chunk, WIDE)
                bits.remove(bit)
            work.append((tied[2 * n], tied[2 * n + 1], split, left))
        found = add_halves(self.sc, [item[:3] for item in work])
        self.line.mark(found[0][0])
        for n, (keep, send) in enumerate(found):
            left = work[n][3]
            axis, bit = self.items[n][4].pop(0)
            self.items[n][:3] = [keep.reshape(left), swap(send.reshape(left), axis, bit), left]

    def finish(self, targets, outs):
        tied = self.line.put(*[value for item in self.items for value in item[:2]])
        flat = lambda v: v.reshape((-1,) + v.shape[3:])
        items = [(flat(tied[2 * n]), flat(tied[2 * n + 1]), targets[n]) for n in range(len(self.items))]
        found = add_last(self.sc, items, outs)
        self.line.mark(found[0])
        return found


def all_sum(line, value, n_seq, n_ffn):
    for axis, size in (("seq", n_seq), ("ffn", n_ffn)):
        for bit in bits_of(size):
            value = value + line.put(swap(value, axis, bit))
            line.mark(value)
            yield value


def bits_of(size):
    found = []
    bit = 1
    while bit < size:
        found.append(bit)
        bit *= 2
    return found


def columns_of(found):
    found = found.reshape((-1,) + found.shape[3:])
    return jnp.transpose(found, (1, 0, 2)).reshape(found.shape[1], -1)


def on_device(
    tokens,
    spots,
    counts,
    fill,
    cot,
    w_qkv,
    b_q,
    b_v,
    w_out,
    b_out,
    gain_one,
    shift_one,
    w_up,
    b_up,
    w_down,
    b_down,
    gain_two,
    shift_two,
):
    n_seq, n_ffn = lax.axis_size("seq"), lax.axis_size("ffn")
    seq, ffn = lax.axis_index("seq"), lax.axis_index("ffn")
    rows, width = tokens.shape
    slots = spots.shape[1]
    units = w_up.shape[1]
    sc = jnp.stack([seq.astype(jnp.int32), ffn.astype(jnp.int32), counts[0]])
    fill, cot = fill[0], cot[0]
    vector = lambda v: v.astype(F32).reshape(1, -1)
    gain_a, shift_a, gain_b, shift_b = (vector(v) for v in (gain_one, shift_one, gain_two, shift_two))
    bias_qkv = vector(jnp.concatenate([b_q, jnp.zeros_like(b_q), b_v]))

    order = ffn ^ jnp.arange(n_ffn)
    line = Line()
    pairs = n_ffn == 2
    if pairs:
        split = "pairs"
        size = units // 8
        core, near = seq % 2, (seq // 2) % 4

        def cut(away):
            place = (near ^ away) * 2 + core
            up = lax.dynamic_slice(w_up, (0, place * size), (width, size))
            down = lax.dynamic_slice(w_down, (place * size, 0), (size, width))
            return up, down

        up_own, down_own = cut(0)
        up_own = swap(up_own, "ffn", 1)
        down_own = swap(down_own, "ffn", 1)
        b_other = swap(b_up, "ffn", 1)
    else:
        split = "stack"
        ups = (jnp.take(lax.all_gather(w_up, "ffn"), order[1:], axis=0),)
        downs = (jnp.take(lax.all_gather(w_down, "ffn"), order[1:], axis=0),)
        b_other = jnp.take(lax.all_gather(b_up, "ffn"), order[1:], axis=0)

    x, x_keep, x_send, qkv = embed_qkv(sc, tokens, spots, fill, w_qkv, bias_qkv, n_seq)
    line.mark(qkv)
    x_get = swap(x_send, "seq", 1)
    if pairs:
        up_own = line.put(up_own)
        up_y, up_z = swap(up_own, "seq", 2), swap(up_own, "seq", 4)
        up_far, down_far = cut(3)
        up_far = swap(line.put(up_far), "ffn", 1)
        down_far = swap(line.put(down_far), "ffn", 1)
    att, att_keep, att_send, logs = attend(sc, line.put(qkv), n_seq)
    line.mark(att)
    att_get = swap(att_send, "seq", 1)
    if pairs:
        up_near = stack(sc, *line.put(up_own, up_y, up_z))
        line.mark(up_near)
        up_near_other = swap(up_near, "seq", 1)
        down_own = line.put(down_own)
        down_y, down_z = swap(down_own, "seq", 2), swap(down_own, "seq", 4)
    hat, inv, low, n_keep, n_send = norm_one(sc, line.put(att), w_out, x, vector(b_out), gain_a, shift_a, n_seq)
    line.mark(low)
    n_get = swap(n_send, "seq", 1)
    hid_own, slope_own, total = ffn_fwd(sc, line.put(low), vector(b_up), (w_up,), (w_down,), "own")
    line.mark(hid_own)
    hid_own_get = swap(hid_own, "seq", 1)
    if pairs:
        down_near = stack(sc, *line.put(down_own, down_y, down_z))
        line.mark(down_near)
        down_near_other = swap(down_near, "seq", 1)
        up_far = line.put(up_far)[None]
        up_far_other = swap(up_far, "seq", 1)
        down_far = line.put(down_far)[None]
        down_far_other = swap(down_far, "seq", 1)
        ups = (up_near, up_near_other, up_far, up_far_other)
        downs = (down_near, down_near_other, down_far, down_far_other)
    hid_oth, slope_oth, total = ffn_fwd(sc, line.put(low), vector(b_other), ups, downs, split, total)
    line.mark(hid_oth)
    hid_oth_get = swap(hid_oth, "seq", 1)

    output, g_two, g_down, d_keep, d_send, sums_two = norm_two(
        sc, line.put(total), hat, gain_a, shift_a, vector(b_down), gain_b, shift_b, spots, cot, n_seq
    )
    line.mark(g_down)
    d_get = swap(d_send, "seq", 1)

    found_bits = bits_of(n_seq)
    seq_bits = [2] + found_bits[2:][::-1]
    ffn_steps = [("ffn", b) for b in bits_of(n_ffn)[::-1]]
    z_steps = [("seq", b) for b in found_bits[2:]]
    y_step = [("seq", 2)]
    x_first = ffn_steps + z_steps + y_step
    y_first = y_step + z_steps + ffn_steps
    per = units // WIDE
    half = per // 2
    shards = lambda v, n: v.reshape((n, -1) + v.shape[1:])
    column = lambda start: (lambda b, sc: (0, start + b))

    def big_first(left, oth, oth_get):
        mine, right = left
        (send,) = weight_grad(sc, [(line.put(mine), right)], [(oth, oth_get, half, column(0), "whole", 0)])
        line.mark(send)
        return shards(send, 1)

    def big_rest(left, own, own_get, oth, oth_get, send):
        mine, right = left
        keep_b, send_b, keep = weight_grad(
            sc, [(line.put(mine), right)],
            [
                (own, own_get, per - half, column(half), "halved", 0),
                (oth, oth_get, per - half, column(half), "halved", 0),
                (own, own_get, half, column(0), "whole", 0),
            ],
        )
        line.mark(keep)
        return Streams(sc, line, [
            (shards(keep, 1), send, seq_bits, x_first),
            (shards(keep_b, 2), shards(send_b, 2), seq_bits, y_first),
        ])

    def big_whole(left, own, own_get, oth, oth_get):
        n_oth = oth.shape[1] // WIDE
        mine, right = left
        (whole,) = weight_grad(
            sc, [(line.put(mine), right)],
            [(own, own_get, per, column(0), "whole", 0), (oth, oth_get, n_oth, column(0), "whole", 0)],
        )
        line.mark(whole)
        return Stream(line, seq_bits, x_first, whole=shards(whole, n_ffn))

    d_left, n_left = (d_keep, d_get), (n_keep, n_get)
    if pairs:
        d_first = big_first(d_left, hid_oth, hid_oth_get)
        downs_sum = big_rest(d_left, hid_own, hid_own_get, hid_oth, hid_oth_get, d_first)
    else:
        down_a = big_whole(d_left, hid_own, hid_own_get, hid_oth, hid_oth_get)

    gp_oth, bs_oth, g_total = ffn_bwd(sc, line.put(g_down), slope_oth, ups, downs, split)
    line.mark(gp_oth)
    gp_oth_get = swap(gp_oth, "seq", 1)
    gp_own, bs_own, g_total = ffn_bwd(sc, line.put(g_down), slope_own, (w_up,), (w_down,), "own", g_total)
    line.mark(gp_own)
    gp_own_get = swap(gp_own, "seq", 1)

    if pairs:
        downs_sum.advance()
        u_first = big_first(n_left, gp_oth, gp_oth_get)
        ups_sum = big_rest(n_left, gp_own, gp_own_get, gp_oth, gp_oth_get, u_first)
    else:
        up_a = big_whole(n_left, gp_own, gp_own_get, gp_oth, gp_oth_get)
    b_up_sums = jnp.concatenate([bs_own.reshape(1, units), bs_oth.reshape(n_ffn - 1, units)])
    b_up_sums = jnp.take(b_up_sums, order, axis=0).reshape(-1)

    g_one, g_att_low, g_att, sums_one = norm_one_back(sc, line.put(g_two), g_total, hat, inv, gain_a, w_out)
    line.mark(g_att)
    g_att_get = swap(g_att_low, "seq", 1)
    if pairs:
        downs_sum.advance()

    def narrow(mine, other, first, count, kind, matrix):
        per_row = mine.shape[-1] // WIDE
        blocks = per_row * (mine.shape[0] if mine.ndim == 3 else 1)
        each = blocks // n_ffn

        def index(b, sc):
            block = ((b // count) ^ sc[1]) * each + first + b % count
            return (0, block) if mine.ndim == 2 else (block // per_row, 0, block % per_row)

        return (mine, other, n_ffn * count, index, kind, matrix)

    def narrow_whole(left, mine, other):
        per_row = mine.shape[-1] // WIDE
        blocks = per_row * (mine.shape[0] if mine.ndim == 3 else 1)
        index = (lambda b, sc: (0, b)) if mine.ndim == 2 else (lambda b, sc: (b // per_row, 0, b % per_row))
        (whole,) = weight_grad(sc, [(line.put(left[0]), left[1])], [(mine, other, blocks, index, "whole", 0)])
        line.mark(whole)
        places, chunk = whole.shape[1:3]
        share = blocks * WIDE // n_ffn
        whole = jnp.transpose(whole, (1, 2, 0, 3)).reshape(places, chunk, n_ffn, share)
        whole = jnp.take(jnp.transpose(whole, (2, 0, 1, 3)), order, axis=0)[:, None]
        return Stream(line, seq_bits, x_first, whole=whole)

    g_qkv, sums_att = attend_back(sc, line.put(qkv), att, g_att, logs)
    line.mark(g_qkv)
    g_qkv_get = swap(g_qkv, "seq", 1)
    sums = jnp.concatenate([sums_two[:3].reshape(-1), sums_one[:3].reshape(-1), b_up_sums, sums_att.reshape(-1)])
    summing = all_sum(line, sums, n_seq, n_ffn)
    if pairs:
        ups_sum.advance()
        downs_sum.advance()
    grad_tokens, grad_fill = token_grads(sc, line.put(g_qkv), w_qkv, g_one, spots, slots)
    line.mark(grad_tokens)
    chunk = width // n_seq
    if pairs:
        keep_b, send_b, both = weight_grad(
            sc, [(line.put(x_keep), x_get), (att_keep, att_get)],
            [
                narrow(g_qkv, g_qkv_get, 2, 1, "halved", 0),
                narrow(g_att_low, g_att_get, 0, 1, "halved", 1),
                narrow(g_qkv, g_qkv_get, 0, 2, "whole", 0),
            ],
        )
        line.mark(keep_b)
        both = shards(both, 2)
        joint = lambda v: shards(v, 2).reshape(2, 2, 1, *v.shape[1:])
        by_shard = lambda v: jnp.swapaxes(joint(v), 0, 1).reshape(2, 2, *v.shape[1:])
        tail = Streams(sc, line, [
            (both[:1], both[1:], seq_bits, ffn_steps + y_step + z_steps),
            (by_shard(keep_b), by_shard(send_b), seq_bits, y_step + ffn_steps + z_steps),
        ])
        ups_sum.advance()
        (grad_down,) = downs_sum.finish([((0, True),) * 2] * 2, [(units, chunk)])
        next(summing)
        ups_sum.advance()
        next(summing)
        tail.advance()
        next(summing)
        (grad_up,) = ups_sum.finish([((0, False),) * 2] * 2, [(chunk, units)])
        next(summing)
        tail.advance()
        (*_, total_sums) = summing
        tail.advance()
        grad_qkv, grad_out = tail.finish(
            [((0, False), (0, False)), ((0, False), (1, False))], [(chunk, 3 * WIDE), (chunk, WIDE)]
        )
    else:
        out = narrow_whole((att_keep, att_get), g_att_low, g_att_get)
        qkv_a = narrow_whole((x_keep, x_get), g_qkv, g_qkv_get)
        (*_, total_sums) = summing
        grad_down, grad_up = columns_of(down_a.finish()).T, columns_of(up_a.finish())
        grad_out, grad_qkv = columns_of(out.finish()), columns_of(qkv_a.finish())

    part = lambda v, n: v[n * width : (n + 1) * width]
    return (
        output,
        grad_tokens,
        grad_fill[None],
        grad_qkv,
        total_sums[-2 * width : -width],
        total_sums[-width:],
        grad_out,
        part(total_sums, 5),
        part(total_sums, 3),
        part(total_sums, 4),
        grad_up,
        total_sums[6 * width : -2 * width],
        grad_down,
        part(total_sums, 2),
        part(total_sums, 0),
        part(total_sums, 1),
    )


def solution(mesh):
    rows = ("seq", "ffn")
    in_specs = (
        P(rows, None),
        P(rows, None),
        P(rows),
        P(rows, None, None),
        P(rows, None, None),
        P(),
        P(),
        P(),
        P(),
        P(),
        P(),
        P(),
        P(None, "ffn"),
        P("ffn"),
        P("ffn", None),
        P(),
        P(),
        P(),
    )
    out_specs = (
        P(rows, None),
        P(rows, None),
        P(rows, None, None),
        P("seq", "ffn"),
        P(),
        P(),
        P("seq", "ffn"),
        P(),
        P(),
        P(),
        P("seq", "ffn"),
        P(),
        P("ffn", "seq"),
        P(),
        P(),
        P(),
    )
    return jax.shard_map(on_device, mesh=mesh, in_specs=in_specs, out_specs=out_specs, check_vma=False)
```

```python
import functools

import jax
import jax.numpy as jnp
from jax import lax
from jax.experimental import pallas as pl
from jax.experimental.pallas import tpu as pltpu
from jax.sharding import PartitionSpec as P

H = 16
F32 = jnp.float32
LOW = jnp.bfloat16
epsilon = 1e-12
LOG2E = 1.4426950408889634
NT = (((1,), (1,)), ((), ()))
WIDE = 512
SEQUENCE = ("gD", "B", "N", "gU", "A", "D", "T", "U", "P", "G", "H", "D", "S", "Q", "U", "S", "D", "Q", "U", "eD", "S", "Q", "S", "S", "eU", "eQ")
STEP = 3 * 10**10


def mm(left, right):
    return jnp.dot(left, right, preferred_element_type=F32)


def mm_nt(left, right):
    return lax.dot_general(left, right, NT, preferred_element_type=F32)


def call(body, grid, in_specs, out_specs, out_shape, scratch=(), prefetch=1, mib=32, weight=0):
    return pl.pallas_call(
        body,
        grid_spec=pltpu.PrefetchScalarGridSpec(
            num_scalar_prefetch=prefetch,
            grid=grid,
            in_specs=in_specs,
            out_specs=out_specs,
            scratch_shapes=list(scratch),
        ),
        out_shape=out_shape,
        compiler_params=pltpu.CompilerParams(
            dimension_semantics=("arbitrary",) * len(grid), vmem_limit_bytes=mib << 20
        ),
        cost_estimate=pl.CostEstimate(flops=int(1 + weight * STEP), bytes_accessed=1, transcendentals=0),
    )


def far(dims, dtype):
    return pltpu.HBM(dims, dtype)


def in_hbm(*values):
    return [pltpu.with_memory_space_constraint(value, pltpu.HBM) for value in values]


def spec(shape, index):
    return pl.BlockSpec(shape, index)


def shape(dims, dtype):
    return jax.ShapeDtypeStruct(dims, dtype)


def one_hot_rows(sc, spots, first, rows):
    slots = spots.shape[1]
    place = lax.broadcasted_iota(jnp.int32, (rows, slots), 0) + first
    slot = lax.broadcasted_iota(jnp.int32, (rows, slots), 1)
    hit = (place == spots) & (slot < sc[2])
    return jnp.where(hit, 1.0, 0.0)


def store_turned(sc, value, keep_ref, send_ref, first_column, chunk):
    columns = value.shape[1]
    for block in range(0, columns, 128):
        turned = jnp.transpose(value[:, block : block + 128]).astype(LOW)
        for part in range(0, 128, chunk):
            place = ((first_column + block + part) // chunk) ^ sc[0]
            piece = turned[part : part + chunk]
            at = ((place // 2) % 2) * (keep_ref.shape[0] // 2) + place // 4

            @pl.when(place % 2 == 0)
            def _():
                keep_ref[at] = piece

            @pl.when(place % 2 == 1)
            def _():
                send_ref[at] = piece


def qkv_body(chunk, sc, tokens, spots, fill, w, bias, x_out, keep, send, qkv):
    @pl.when(pl.program_id(0) == 0)
    def _():
        placed = one_hot_rows(sc, spots[...], 0, tokens.shape[0])
        kept = 1.0 - jnp.sum(placed, axis=1, keepdims=True)
        x = tokens[...].astype(F32) * kept + mm(placed.astype(LOW), fill[...])
        x_out[...] = x.astype(LOW)
        store_turned(sc, x, keep, send, 0, chunk)

    qkv[...] = (mm(x_out[...], w[...]) + bias[...]).astype(LOW)


def embed_qkv(sc, tokens, spots, fill, w_qkv, bias, n_seq):
    rows, width = tokens.shape
    out = w_qkv.shape[1]
    block = 512
    chunk = width // n_seq
    turned = (n_seq // 2, chunk, rows)
    whole = lambda j, sc: (0, 0)
    return call(
        functools.partial(qkv_body, chunk),
        (out // block,),
        [
            spec((rows, width), whole),
            spec(spots.shape, whole),
            spec(fill.shape, whole),
            spec((width, block), lambda j, sc: (0, j)),
            spec((1, block), lambda j, sc: (0, j)),
        ],
        [
            spec((rows, width), whole),
            spec(turned, lambda j, sc: (0, 0, 0)),
            spec(turned, lambda j, sc: (0, 0, 0)),
            spec((rows, block), lambda j, sc: (0, j)),
        ],
        [shape((rows, width), LOW), far(turned, LOW), far(turned, LOW), shape((rows, out), LOW)],
        weight=1,
    )(sc, tokens, spots, fill, w_qkv, bias)


def head_masks(width, size, factor):
    lane = lax.broadcasted_iota(jnp.int32, (1, width), 1)
    return [jnp.where(lane // size == n, factor, 0.0).astype(LOW) for n in range(width // size)]


def attend_body(chunk, size, scale, sc, q, k, v, att, keep, send, logs):
    rows, width = q.shape
    pair = 2 * size
    masks = head_masks(pair, size, scale)
    lane = lax.broadcasted_iota(jnp.int32, (1, pair), 1)
    place_first = pl.program_id(0) * width
    for first in range(0, width, pair):
        columns = slice(first, first + pair)
        mixed, stats = [], []
        for mask in masks:
            scores = mm_nt(q[:, columns] * mask, k[:, columns])
            peak = jnp.max(scores, axis=1, keepdims=True) * LOG2E
            expo = jnp.exp2(scores * LOG2E - peak)
            total = jnp.sum(expo, axis=1, keepdims=True)
            mixed.append(mm(expo.astype(LOW), v[:, columns]) * (1.0 / total))
            stats.append(peak + jnp.log2(total))
        both = jnp.where(lane < size, mixed[0], mixed[1])
        att[:, columns] = both.astype(LOW)
        logs[:, columns] = jnp.where(lane < size, stats[0], stats[1])
        store_turned(sc, both, keep, send, place_first + first, chunk)


def attend(sc, qkv, n_seq):
    rows = qkv.shape[0]
    width = qkv.shape[1] // 3
    size = width // H
    block = 4 * size
    steps = width // block
    chunk = width // n_seq
    turned = (n_seq // 2, chunk, rows)
    whole = lambda j, sc: (0, 0, 0)
    tile = spec((rows, block), lambda j, sc: (0, j))
    return call(
        functools.partial(attend_body, chunk, size, size ** (-0.5)),
        (steps,),
        [
            tile,
            spec((rows, block), lambda j, sc: (0, steps + j)),
            spec((rows, block), lambda j, sc: (0, 2 * steps + j)),
        ],
        [tile, spec(turned, whole), spec(turned, whole), tile],
        [shape((rows, width), LOW), far(turned, LOW), far(turned, LOW), shape((rows, width), F32)],
        weight=1,
    )(sc, qkv, qkv, qkv)


def norm_one_body(chunk, sc, att, w, x, b, gain, shift, hat, inv, low, keep, send):
    value = x[...].astype(F32) + mm(att[...], w[...]) + b[...]
    centre = value - jnp.mean(value, axis=-1, keepdims=True)
    spread = jnp.mean(centre * centre, axis=-1, keepdims=True)
    inverse = lax.rsqrt(spread + epsilon)
    scaled = centre * inverse
    hat[...] = scaled
    inv[...] = inverse
    normed = scaled * gain[...] + shift[...]
    low[...] = normed.astype(LOW)
    store_turned(sc, normed, keep, send, 0, chunk)


def norm_one(sc, att, w_out, x, b_out, gain, shift, n_seq):
    rows, width = x.shape
    block = 256
    chunk = width // n_seq
    turned = (n_seq // 2, chunk, rows)
    row = lambda i, sc: (i, 0)
    whole = lambda i, sc: (0, 0)
    vector = spec((1, width), whole)
    return call(
        functools.partial(norm_one_body, chunk),
        (rows // block,),
        [spec((block, width), row), spec((width, width), whole), spec((block, width), row), vector, vector, vector],
        [
            spec((block, width), row),
            spec((block, 1), row),
            spec((block, width), row),
            spec((n_seq // 2, chunk, block), lambda i, sc: (0, 0, i)),
            spec((n_seq // 2, chunk, block), lambda i, sc: (0, 0, i)),
        ],
        [
            far((rows, width), F32),
            shape((rows, 1), F32),
            shape((rows, width), LOW),
            far(turned, LOW),
            far(turned, LOW),
        ],
        weight=1,
    )(sc, att, w_out, x, b_out, gain, shift)


TAIL = tuple(0.5 * c for c in (0.254829592, -0.284496736, 1.421413741, -1.453152027, 1.061405429))
TAIL_P = 0.3275911 * 0.7071067811865476


def gelu_both(x):
    t = 1.0 / (1.0 + TAIL_P * jnp.abs(x))
    bell = jnp.exp2(x * x * (-0.5 * LOG2E))
    poly = TAIL[4]
    for c in TAIL[3::-1]:
        poly = poly * t + c
    tail = poly * t * bell
    mass = jnp.where(x < 0.0, tail, 1.0 - tail)
    return x * mass, mass + x * bell * 0.3989422804014327


def ffn_specs(split, width, part):
    if split == "own":
        ups = [spec((width, WIDE), lambda j, sc: (0, j))]
        downs = [spec((WIDE, width), lambda j, sc: (j, 0))]
        return ups, downs, WIDE
    if split == "stack":
        ups = [spec((None, width, part), lambda j, sc: (j, 0, 0))]
        downs = [spec((None, part, width), lambda j, sc: (j, 0, 0))]
        return ups, downs, part
    near = lambda j, sc: (jnp.minimum(j, 2), 0, 0)
    far = lambda j, sc: (0, 0, 0)
    ups = [spec((None, width, part), at) for at in (near, near, far, far)]
    downs = [spec((None, part, width), at) for at in (near, near, far, far)]
    return ups, downs, part


def column_block(split):
    if split == "pairs":
        return lambda j, sc: (0, j ^ ((sc[0] // 2) % 4))
    return lambda j, sc: (0, j)


def for_pieces(split, size, sc, ups, downs, work):
    if split != "pairs":
        work([(ups[0], downs[0], 0)])
        return
    core = sc[0] % 2
    places = [pl.multiple_of(core * size, size), pl.multiple_of((1 - core) * size, size)]
    step = pl.program_id(0)
    pl.when(step < 3)(lambda: work(list(zip(ups[:2], downs[:2], places))))
    pl.when(step == 3)(lambda: work(list(zip(ups[2:], downs[2:], places))))


def ffn_fwd_body(split, size, n, first, sc, *refs):
    low, bias = refs[:2]
    ups, downs = refs[2 : 2 + n], refs[2 + n : 2 + 2 * n]
    rest = refs[2 + 2 * n :]
    start = None
    if not first:
        start, rest = rest[0], rest[1:]
    hidden, slope, total = rest
    @pl.when(pl.program_id(0) == 0)
    def _():
        total[...] = jnp.zeros_like(total) if first else start[...]

    def work(pieces):
        mixed = None
        for up, down, offset in pieces:
            columns = pl.ds(offset, size)
            pre = mm(low[...], up[...]) + bias[:, columns]
            act, grad = gelu_both(pre)
            act = act.astype(LOW)
            hidden[:, columns] = act
            slope[:, columns] = grad.astype(LOW)
            product = mm(act, down[...])
            mixed = product if mixed is None else mixed + product
        total[...] += mixed

    for_pieces(split, size, sc, ups, downs, work)


def ffn_fwd(sc, low, bias, ups, downs, split, start=None):
    rows, width = low.shape
    units = bias.shape[1]
    part = ups[0].shape[-1]
    up_specs, down_specs, size = ffn_specs(split, width, part)
    step = WIDE if split != "stack" else part
    whole = lambda j, sc: (0, 0)
    column = column_block(split)
    total = spec((rows, width), whole)
    first = start is None
    return call(
        functools.partial(ffn_fwd_body, split, size, len(ups), first),
        (units // step,),
        [total, spec((1, step), column)] + up_specs + down_specs + ([] if first else [total]),
        [spec((rows, step), column), spec((rows, step), column), total],
        [shape((rows, units), LOW), shape((rows, units), LOW), shape((rows, width), F32)],
        weight=1,
    )(sc, low, bias, *ups, *downs, *([] if first else [start]))


def ffn_bwd_body(split, size, n, first, sc, *refs):
    low, slope = refs[:2]
    ups, downs = refs[2 : 2 + n], refs[2 + n : 2 + 2 * n]
    rest = refs[2 + 2 * n :]
    start = None
    if not first:
        start, rest = rest[0], rest[1:]
    g_low, sums, total = rest
    @pl.when(pl.program_id(0) == 0)
    def _():
        total[...] = jnp.zeros_like(total) if first else start[...]

    def work(pieces):
        mixed = None
        for up, down, offset in pieces:
            columns = pl.ds(offset, size)
            g_pre = mm_nt(low[...], down[...]) * slope[:, columns].astype(F32)
            sums[:, columns] = jnp.sum(g_pre, axis=0, keepdims=True)
            rounded = g_pre.astype(LOW)
            g_low[:, columns] = rounded
            product = mm_nt(rounded, up[...])
            mixed = product if mixed is None else mixed + product
        total[...] += mixed

    for_pieces(split, size, sc, ups, downs, work)


def ffn_bwd(sc, low, slope, ups, downs, split, start=None):
    rows, width = low.shape
    units = slope.shape[1]
    part = ups[0].shape[-1]
    up_specs, down_specs, size = ffn_specs(split, width, part)
    step = WIDE if split != "stack" else part
    whole = lambda j, sc: (0, 0)
    column = column_block(split)
    total = spec((rows, width), whole)
    first = start is None
    return call(
        functools.partial(ffn_bwd_body, split, size, len(ups), first),
        (units // step,),
        [total, spec((rows, step), column)] + up_specs + down_specs + ([] if first else [total]),
        [spec((rows, step), column), spec((1, step), column), total],
        [shape((rows, units), LOW), shape((1, units), F32), shape((rows, width), F32)],
    )(sc, low, slope, *ups, *downs, *([] if first else [start]))


def ffn_both_body(size, sc, low, slope_oth, slope_own, *refs):
    ups, downs, (up, down) = refs[:4], refs[4:8], refs[8:10]
    g_oth, g_own, sums_oth, sums_own, total = refs[10:]
    core = sc[0] % 2
    places = [pl.multiple_of(core * size, size), pl.multiple_of((1 - core) * size, size)]
    step = pl.program_id(0)

    def work(pieces, slope, g_low, sums):
        mixed = None
        for up_ref, down_ref, offset, span in pieces:
            columns = pl.ds(offset, span)
            g_pre = mm_nt(low[...], down_ref[...]) * slope[:, columns].astype(F32)
            sums[:, columns] = jnp.sum(g_pre, axis=0, keepdims=True)
            rounded = g_pre.astype(LOW)
            g_low[:, columns] = rounded
            product = mm_nt(rounded, up_ref[...])
            mixed = product if mixed is None else mixed + product

        @pl.when(step == 0)
        def _():
            total[...] = mixed

        @pl.when(step > 0)
        def _():
            total[...] += mixed

    other = lambda group: [(u, d, place, size) for u, d, place in zip(ups[group], downs[group], places)]
    pl.when(step < 3)(lambda: work(other(slice(0, 2)), slope_oth, g_oth, sums_oth))
    pl.when(step == 3)(lambda: work(other(slice(2, 4)), slope_oth, g_oth, sums_oth))
    pl.when(step > 3)(lambda: work([(up, down, 0, 2 * size)], slope_own, g_own, sums_own))


def ffn_both(sc, low, slope_oth, slope_own, ups, downs, up, down):
    rows, width = low.shape
    units = slope_own.shape[1]
    part = ups[0].shape[-1]
    wide = 2 * part
    steps = units // wide
    whole = lambda j, sc: (0, 0)
    near = lambda j, sc: (jnp.minimum(j, 2), 0, 0)
    away = lambda j, sc: (0, 0, 0)
    oth = lambda j, sc: (0, jnp.minimum(j, 3) ^ ((sc[0] // 2) % 4))
    own = lambda j, sc: (0, jnp.maximum(j - 4, 0))
    own_row = lambda j, sc: (jnp.maximum(j - 4, 0), 0)
    return call(
        functools.partial(ffn_both_body, part),
        (4 + steps,),
        [spec((rows, width), whole), spec((rows, wide), oth), spec((rows, wide), own)]
        + [spec((None, width, part), at) for at in (near, near, away, away)]
        + [spec((None, part, width), at) for at in (near, near, away, away)]
        + [spec((width, wide), own), spec((wide, width), own_row)],
        [spec((rows, wide), oth), spec((rows, wide), own), spec((1, wide), oth), spec((1, wide), own), spec((rows, width), whole)],
        [far((rows, units), LOW), far((rows, units), LOW), shape((1, units), F32), shape((1, units), F32), shape((rows, width), F32)],
        weight=0,
    )(sc, low, slope_oth, slope_own, *ups, *downs, up, down)


def norm_back(hat, inverse, gain, grad):
    inner = grad * gain
    mean = jnp.mean(inner, axis=-1, keepdims=True)
    along = jnp.mean(inner * hat, axis=-1, keepdims=True)
    return inverse * (inner - mean - hat * along)


def add_sums(sums, rows):
    @pl.when(pl.program_id(0) == 0)
    def _():
        sums[...] = jnp.zeros_like(sums)

    for n, value in enumerate(rows):
        sums[n : n + 1, :] += jnp.sum(value, axis=0, keepdims=True)


def norm_two_body(chunk, sc, mixed, hat_one, gain_one, shift_one, b_down, gain, shift, spots, cot, out, grad, low, keep, send, sums):
    rows = mixed.shape[0]
    value = hat_one[...] * gain_one[...] + shift_one[...] + mixed[...] + b_down[...]
    centre = value - jnp.mean(value, axis=-1, keepdims=True)
    spread = jnp.mean(centre * centre, axis=-1, keepdims=True)
    inverse = lax.rsqrt(spread + epsilon)
    hat = centre * inverse
    out[...] = (hat * gain[...] + shift[...]).astype(LOW)
    placed = one_hot_rows(sc, spots[...], pl.program_id(0) * rows, rows)
    out_grad = mm(placed.astype(LOW), cot[...])
    result = norm_back(hat, inverse, gain[...], out_grad)
    grad[...] = result
    low[...] = result.astype(LOW)
    store_turned(sc, result, keep, send, 0, chunk)
    add_sums(sums, (out_grad * hat, out_grad, result))


def norm_two(sc, mixed, hat_one, gain_one, shift_one, b_down, gain, shift, spots, cot, n_seq):
    rows, width = mixed.shape
    block = 256
    chunk = width // n_seq
    turned = (n_seq // 2, chunk, rows)
    row = lambda i, sc: (i, 0)
    whole = lambda i, sc: (0, 0)
    vector = spec((1, width), whole)
    tile = spec((block, width), row)
    return call(
        functools.partial(norm_two_body, chunk),
        (rows // block,),
        [tile, tile, vector, vector, vector, vector, vector, spec(spots.shape, whole), spec(cot.shape, whole)],
        [
            tile,
            tile,
            tile,
            spec((n_seq // 2, chunk, block), lambda i, sc: (0, 0, i)),
            spec((n_seq // 2, chunk, block), lambda i, sc: (0, 0, i)),
            spec((8, width), whole),
        ],
        [
            shape((rows, width), LOW),
            shape((rows, width), F32),
            shape((rows, width), LOW),
            far(turned, LOW),
            far(turned, LOW),
            shape((8, width), F32),
        ],
        weight=1,
    )(sc, mixed, hat_one, gain_one, shift_one, b_down, gain, shift, spots, cot)


def norm_one_back_body(sc, grad_two, ffn, hat, inv, gain, w, grad, low, g_att, sums):
    g_normed = grad_two[...] + ffn[...]
    result = norm_back(hat[...], inv[...], gain[...], g_normed)
    grad[...] = result
    rounded = result.astype(LOW)
    low[...] = rounded
    g_att[...] = mm_nt(rounded, w[...]).astype(LOW)
    add_sums(sums, (g_normed * hat[...], g_normed, result))


def norm_one_back(sc, grad_two, ffn, hat, inv, gain, w_out):
    rows, width = hat.shape
    block = 256
    row = lambda i, sc: (i, 0)
    whole = lambda i, sc: (0, 0)
    tile = spec((block, width), row)
    return call(
        norm_one_back_body,
        (rows // block,),
        [tile, tile, tile, spec((block, 1), row), spec((1, width), whole), spec((width, width), whole)],
        [tile, tile, tile, spec((8, width), whole)],
        [shape((rows, width), F32), shape((rows, width), LOW), shape((rows, width), LOW), shape((8, width), F32)],
        weight=0,
    )(sc, grad_two, ffn, hat, inv, gain, w_out)


def mm_tn(left, right):
    return lax.dot_general(left, right, (((0,), (0,)), ((), ())), preferred_element_type=F32)


def attend_back_body(size, scale, sc, q, k, v, att, g_att, logs, g_qkv, sums):
    rows, width = q.shape
    pair = 2 * size
    ones = head_masks(pair, size, 1.0)
    halves = head_masks(pair, size, scale)
    lane = lax.broadcasted_iota(jnp.int32, (1, pair), 1)
    for first in range(0, width, pair):
        columns = slice(first, first + pair)
        q_pair, k_pair, v_pair, g_pair = q[:, columns], k[:, columns], v[:, columns], g_att[:, columns]
        q_scaled = q_pair * jnp.asarray(scale, LOW)
        k_scaled = k_pair * jnp.asarray(scale, LOW)
        product = att[:, columns].astype(F32) * g_pair.astype(F32)
        log_pair = logs[:, columns]
        turned_v, turned_k, g_q = [], [], []
        for n in range(2):
            rows_of = slice(n * size, (n + 1) * size)
            scores = mm_nt(q_pair * halves[n], k_pair)
            probs = jnp.exp2(scores * LOG2E - log_pair[:, n * size : n * size + 1])
            g_probs = mm_nt(g_pair * ones[n], v_pair)
            level = jnp.sum(jnp.where(lane // size == n, product, 0.0), axis=1, keepdims=True)
            g_scores = (probs * (g_probs - level)).astype(LOW)
            turned_v.append(mm_tn(g_pair, probs.astype(LOW))[rows_of])
            turned_k.append(mm_tn(q_scaled, g_scores)[rows_of])
            g_q.append(mm(g_scores, k_scaled))
        query = jnp.where(lane < size, g_q[0], g_q[1]).astype(LOW)
        value = jnp.transpose(jnp.concatenate(turned_v, axis=0)).astype(LOW)
        g_qkv[0, :, columns] = query
        g_qkv[1, :, columns] = jnp.transpose(jnp.concatenate(turned_k, axis=0)).astype(LOW)
        g_qkv[2, :, columns] = value
        sums[0:1, columns] = jnp.sum(query.astype(F32), axis=0, keepdims=True)
        sums[1:2, columns] = jnp.sum(value.astype(F32), axis=0, keepdims=True)


def attend_back(sc, qkv, att, g_att, logs):
    rows, width = att.shape
    size = width // H
    block = 4 * size
    steps = width // block
    tile = spec((rows, block), lambda j, sc: (0, j))
    return call(
        functools.partial(attend_back_body, size, size ** (-0.5)),
        (steps,),
        [
            tile,
            spec((rows, block), lambda j, sc: (0, steps + j)),
            spec((rows, block), lambda j, sc: (0, 2 * steps + j)),
            tile,
            tile,
            tile,
        ],
        [spec((3, rows, block), lambda j, sc: (0, 0, j)), spec((2, block), lambda j, sc: (0, j))],
        [far((3, rows, width), LOW), shape((2, width), F32)],
        weight=0,
    )(sc, qkv, qkv, qkv, att, g_att, logs)


def token_grads_body(sc, g_qkv, w, base, spots, spots_column, tokens_out, fill_out):
    rows = base.shape[0]
    width = g_qkv.shape[2]
    grad = base[...]
    for n in range(3):
        grad = grad + mm_nt(g_qkv[n], w[:, n * width : (n + 1) * width])
    placed = one_hot_rows(sc, spots[...], 0, rows)
    kept = 1.0 - jnp.sum(placed, axis=1, keepdims=True)
    tokens_out[...] = (grad * kept).astype(LOW)
    slots = spots_column.shape[0]
    place = lax.broadcasted_iota(jnp.int32, (slots, rows), 1)
    slot = lax.broadcasted_iota(jnp.int32, (slots, rows), 0)
    hit = (place == spots_column[...]) & (slot < sc[2])
    fill_out[...] = mm(jnp.where(hit, 1.0, 0.0).astype(LOW), grad.astype(LOW)).astype(LOW)


def token_grads(sc, g_qkv, w_qkv, base, spots, slots):
    rows, width = base.shape
    block = 512
    column = lambda i, sc: (0, i)
    whole = lambda i, sc: (0, 0)
    tile = spec((rows, block), column)
    return call(
        token_grads_body,
        (width // block,),
        [
            spec(g_qkv.shape, lambda i, sc: (0, 0, 0)),
            spec((block, w_qkv.shape[1]), lambda i, sc: (i, 0)),
            tile,
            spec(spots.shape, whole),
            spec((slots, 1), whole),
        ],
        [tile, spec((slots, block), column)],
        [shape((rows, width), LOW), shape((slots, width), LOW)],
        weight=0,
    )(sc, g_qkv, w_qkv, base, spots, spots.reshape(slots, 1))


def weight_body(plan, lefts, sc, *refs):
    left_refs, refs = refs[: 2 * lefts], refs[2 * lefts :]
    ins, outs = refs[: 2 * len(plan)], refs[2 * len(plan) :]
    step = pl.program_id(0)
    first = 0
    for n, (count, matrix, targets) in enumerate(plan):
        left, left_other = left_refs[2 * matrix : 2 * matrix + 2]
        mine, other = ins[2 * n], ins[2 * n + 1]

        def work(left=left, left_other=left_other, mine=mine, other=other, targets=targets):
            places, _, depth = left.shape
            rows_of = lambda ref: ref[...].reshape(-1, depth)
            total = mm(rows_of(left), mine[...]) + mm(rows_of(left_other), other[...])
            total = total.astype(LOW).reshape(places, -1, total.shape[-1])
            share = places // len(targets)
            for part, target in enumerate(targets):
                outs[target][...] = total[part * share : (part + 1) * share]

        if len(plan) == 1:
            work()
        else:
            pl.when((step >= first) & (step < first + count))(work)
        first += count


def weight_grad(sc, lefts, segments):
    places, chunk, depth = lefts[0][0].shape
    left_spec = spec((places, chunk, depth), lambda j, sc: (0, 0, 0))
    in_specs = [left_spec] * (2 * len(lefts))
    operands = [value for pair in lefts for value in pair]
    spans, plan, first = {}, [], 0
    for mine, other, count, index, matrix, names in segments:
        def at(j, sc, first=first, count=count, index=index):
            return index(jnp.clip(j - first, 0, count - 1), sc)

        block = (depth, WIDE) if mine.ndim == 2 else (None, depth, WIDE)
        in_specs += [spec(block, at), spec(block, at)]
        operands += [mine, other]
        for name in names:
            begin = spans.setdefault(name, [first, first, places // len(names)])
            begin[1] = first + count
        first += count
    order = list(spans)
    for _, _, count, _, matrix, names in segments:
        plan.append((count, matrix, tuple(order.index(name) for name in names)))
    out_specs, out_shapes = [], []
    for begin, end, kept in spans.values():
        at = lambda j, sc, begin=begin, end=end: (jnp.clip(j, begin, end - 1) - begin, 0, 0)
        out_specs.append(spec((kept, chunk, WIDE), at))
        out_shapes.append(far(((end - begin) * kept, chunk, WIDE), LOW))
    found = call(
        functools.partial(weight_body, tuple(plan), len(lefts)),
        (first,),
        in_specs,
        out_specs,
        out_shapes,
        weight=0,
    )(sc, *operands)
    return dict(zip(order, found))


def add_body(count, plan, sc, *refs):
    outs = refs[2 * count :]
    for source, start, (outer, inner), target, place in plan:
        span = pl.ds(start, outer * 2 * inner)
        total = refs[2 * source][span].astype(F32) + refs[2 * source + 1][span].astype(F32)
        total = total.astype(LOW).reshape((outer, 2, inner) + total.shape[1:])
        for half in range(2):
            part = total[:, half]
            outs[2 * target + half][pl.ds(place, outer * inner)] = part.reshape((outer * inner,) + part.shape[2:])


def add_halves(sc, arrays, plan, sizes):
    tile = WIDE // 2
    chunk = arrays[0][0].shape[1]
    column = lambda j, sc: (0, 0, j)
    operands = [value for pair in arrays for value in pair]
    found = call(
        functools.partial(add_body, len(arrays), tuple(plan)),
        (WIDE // tile,),
        [spec(value.shape[:2] + (tile,), column) for value in operands],
        [spec((size, chunk, tile), column) for size in sizes for _ in range(2)],
        [far((size, chunk, WIDE), LOW) for size in sizes for _ in range(2)],
        weight=0,
    )(sc, *operands)
    return [(found[2 * n], found[2 * n + 1]) for n in range(len(sizes))]


def last_body(count, plan, sc, *refs):
    for source, place, target, at, turned in plan:
        total = refs[2 * source][place].astype(F32) + refs[2 * source + 1][place].astype(F32)
        out = refs[2 * count + target]
        if turned:
            out[at : at + WIDE, :] = jnp.transpose(total)
        else:
            out[:, at : at + WIDE] = total


def add_last(sc, arrays, plan, outs):
    whole = lambda n: (lambda j, sc: (0,) * n)
    operands = [value for pair in arrays for value in pair]
    return call(
        functools.partial(last_body, len(arrays), tuple(plan)),
        (1,),
        [spec(value.shape, whole(3)) for value in operands],
        [spec(dims, whole(2)) for dims in outs],
        [shape(dims, F32) for dims in outs],
    )(sc, *operands)


def stack_body(sc, *refs):
    out = refs[-1]
    for n, ref in enumerate(refs[:-1]):
        out[n] = ref[...]


def stack(sc, *values):
    rows, columns = values[0].shape
    steps = 2
    return call(
        stack_body,
        (steps,),
        [spec((rows // steps, columns), lambda j, sc: (j, 0))] * len(values),
        spec((len(values), rows // steps, columns), lambda j, sc: (0, j, 0)),
        far((len(values),) + values[0].shape, LOW),
        weight=1,
    )(sc, *values)


def swap(value, axis, bit):
    size = lax.axis_size(axis)
    return lax.ppermute(value, axis, [(n, n ^ bit) for n in range(size)])


def halves(value, bits, step):
    shards, blocks, places, chunk, wide = value.shape
    axis, bit = step
    if axis == "ffn":
        return value[: shards // 2], value[shards // 2 :], bits
    at = bits.index(bit)
    low = 1 << (len(bits) - 1 - at)
    parts = value.reshape(shards, blocks, places // (2 * low), 2, low, chunk, wide)
    dims = (shards, blocks, places // 2, chunk, wide)
    return (
        parts[:, :, :, 0].reshape(dims),
        parts[:, :, :, 1].reshape(dims),
        bits[:at] + bits[at + 1 :],
    )


class Line:
    def __init__(self):
        self.last = ()

    def put(self, *values):
        if self.last:
            values = lax.optimization_barrier(self.last + values)[len(self.last) :]
        return values if len(values) > 1 else values[0]

    def mark(self, value):
        self.last = (value,)

    def need(self, *values):
        self.last += values


class Stream:
    def __init__(self, line, bits, steps, whole=None, keep=None, send=None):
        self.line, self.bits, self.steps = line, list(bits), list(steps)
        if keep is None:
            keep, send, self.bits = halves(whole, self.bits, self.steps[0])
        elif self.steps[0][0] == "seq":
            self.bits.remove(self.steps[0][1])
        self.post(keep, send)

    def post(self, keep, send):
        self.keep = keep
        self.got = swap(send, *self.steps.pop(0))

    def advance(self):
        keep, got = self.line.put(self.keep, self.got)
        if self.steps:
            step = self.steps[0]
            keep_a, send_a, left = halves(keep, self.bits, step)
            keep_b, send_b, left = halves(got, self.bits, step)
            self.bits = left
            add = lambda a, b: (a.astype(F32) + b.astype(F32)).astype(LOW)
            send = add(send_a, send_b)
            keep = add(keep_a, keep_b)
            self.line.mark(keep)
            self.post(keep, send)
            return None
        total = keep.astype(F32) + got.astype(F32)
        self.line.mark(total)
        return total

    def finish(self):
        while True:
            total = self.advance()
            if total is not None:
                return total


class Group:
    def __init__(self, sc, line, parts):
        self.sc, self.line = sc, line
        self.arrays = []
        self.parts = []
        for n, (axes, keep, send, step) in enumerate(parts):
            self.arrays.append((keep, swap(send, *step)))
            self.parts.append((n, 0, list(axes)))

    def tied(self):
        flat = self.line.put(*[value for pair in self.arrays for value in pair])
        return [(flat[2 * n], flat[2 * n + 1]) for n in range(len(self.arrays))]

    def advance(self, *steps):
        steps = steps * len(self.parts) if len(steps) == 1 else steps
        order = list(dict.fromkeys(steps))
        plan, sizes, parts = [], [0] * len(order), []
        for (array, start, axes), step in zip(self.parts, steps):
            at = [name for name, _ in axes].index(step)
            outer = inner = 1
            for _, size in axes[:at]:
                outer *= size
            for _, size in axes[at + 1 :]:
                inner *= size
            target = order.index(step)
            plan.append((array, start, (outer, inner), target, sizes[target]))
            parts.append((target, sizes[target], axes[:at] + axes[at + 1 :]))
            sizes[target] += outer * inner
        found = add_halves(self.sc, self.tied(), plan, sizes)
        self.line.mark(found[0][0])
        self.arrays = [(keep, swap(send, *step)) for (keep, send), step in zip(found, order)]
        self.parts = parts

    def finish(self, targets, outs):
        plan = []
        for (array, start, _), places in zip(self.parts, targets):
            for n, place in enumerate(places):
                plan.append((array, start + n) + place)
        found = add_last(self.sc, self.tied(), plan, outs)
        self.line.mark(found[0])
        return found


def pack_body(sc, two, one, own, other, att, out):
    out[...] = jnp.zeros_like(out)
    out[0:3, :] = two[0:3, :]
    out[3:6, :] = one[0:3, :]
    width = out.shape[1]
    count = own.shape[1] // width
    for n in range(count):
        columns = slice(n * width, (n + 1) * width)
        first = sc[1] == 0
        out[6 + n : 7 + n, :] = jnp.where(first, own[:, columns], other[:, columns])
        out[6 + count + n : 7 + count + n, :] = jnp.where(first, other[:, columns], own[:, columns])
    out[6 + 2 * count : 8 + 2 * count, :] = att[...]


def pack(sc, *values):
    width = values[0].shape[1]
    rows = 8 + 2 * values[2].shape[1] // width
    rows += -rows % 8
    whole = lambda j, sc: (0, 0)
    return call(
        pack_body,
        (1,),
        [spec(v.shape, whole) for v in values],
        spec((rows, width), whole),
        far((rows, width), F32),
        weight=1,
    )(sc, *values)


def cut_body(sc, *refs):
    for ref, out in zip(refs[:4], refs[4:]):
        out[...] = ref[...]


def cut(sc, w_up, w_down):
    width, units = w_up.shape
    part = units // 8
    steps = 2
    place = lambda sc, away: (((sc[0] // 2) % 4) ^ away) * 2 + sc[0] % 2
    ups = [spec((width // steps, part), lambda j, sc, n=n: (j, place(sc, n))) for n in (0, 3)]
    downs = [spec((part // steps, width), lambda j, sc, n=n: (place(sc, n) * steps + j, 0)) for n in (0, 3)]
    row = lambda j, sc: (j, 0)
    return call(
        cut_body,
        (steps,),
        ups + downs,
        [spec((width // steps, part), row)] * 2 + [spec((part // steps, width), row)] * 2,
        [far((width, part), LOW)] * 2 + [far((part, width), LOW)] * 2,
        weight=1,
    )(sc, w_up, w_up, w_down, w_down)


def all_sum(line, value, n_seq, n_ffn):
    for axis, size in (("seq", n_seq), ("ffn", n_ffn)):
        for bit in bits_of(size):
            value = value + line.put(swap(value, axis, bit))
            line.mark(value)
            yield value


def bits_of(size):
    found = []
    bit = 1
    while bit < size:
        found.append(bit)
        bit *= 2
    return found


def columns_of(found):
    found = found.reshape((-1,) + found.shape[3:])
    return jnp.transpose(found, (1, 0, 2)).reshape(found.shape[1], -1)


def on_device(
    tokens,
    spots,
    counts,
    fill,
    cot,
    w_qkv,
    b_q,
    b_v,
    w_out,
    b_out,
    gain_one,
    shift_one,
    w_up,
    b_up,
    w_down,
    b_down,
    gain_two,
    shift_two,
):
    n_seq, n_ffn = lax.axis_size("seq"), lax.axis_size("ffn")
    seq, ffn = lax.axis_index("seq"), lax.axis_index("ffn")
    rows, width = tokens.shape
    slots = spots.shape[1]
    units = w_up.shape[1]
    sc = jnp.stack([seq.astype(jnp.int32), ffn.astype(jnp.int32), counts[0]])
    fill, cot = fill[0], cot[0]
    vector = lambda v: v.astype(F32).reshape(1, -1)
    gain_a, shift_a, gain_b, shift_b = (vector(v) for v in (gain_one, shift_one, gain_two, shift_two))
    bias_qkv = vector(jnp.concatenate([b_q, jnp.zeros_like(b_q), b_v]))

    order = ffn ^ jnp.arange(n_ffn)
    line = Line()
    pairs = n_ffn == 2
    if pairs:
        split = "pairs"
        w_up, w_down, w_qkv = in_hbm(w_up, w_down, w_qkv)
        up_own, up_far, down_own, down_far = cut(sc, w_up, w_down)
        up_own = swap(up_own, "ffn", 1)
        b_other = swap(b_up, "ffn", 1)
        down_own = swap(down_own, "ffn", 1)
        up_far = swap(up_far, "ffn", 1)
        down_far = swap(down_far, "ffn", 1)
    else:
        split = "stack"
        ups = (jnp.take(lax.all_gather(w_up, "ffn"), order[1:], axis=0),)
        downs = (jnp.take(lax.all_gather(w_down, "ffn"), order[1:], axis=0),)
        b_other = jnp.take(lax.all_gather(b_up, "ffn"), order[1:], axis=0)

    x, x_keep, x_send, qkv = embed_qkv(sc, tokens, spots, fill, w_qkv, bias_qkv, n_seq)
    line.mark(qkv)
    if pairs:
        line.need(up_own, b_other)
        up_y, up_z = swap(line.put(up_own), "seq", 2), swap(line.put(up_own), "seq", 4)
    att, att_keep, att_send, logs = attend(sc, line.put(qkv), n_seq)
    line.mark(att)
    if pairs:
        up_near = stack(sc, *line.put(up_own, up_y, up_z))
        line.mark(up_near)
        line.need(down_own)
        down_y, down_z = swap(line.put(down_own), "seq", 2), swap(line.put(down_own), "seq", 4)
        up_near_other = swap(up_near, "seq", 1)
    hat, inv, low, n_keep, n_send = norm_one(sc, line.put(att), w_out, x, vector(b_out), gain_a, shift_a, n_seq)
    line.mark(low)
    if pairs:
        line.need(up_near_other, up_far)
    x_get = swap(line.put(x_send), "seq", 1)
    att_get = swap(line.put(att_send), "seq", 1)
    hid_own, slope_own, total = ffn_fwd(sc, line.put(low), vector(b_up), (w_up,), (w_down,), "own")
    line.mark(hid_own)
    if pairs:
        line.need(x_get, att_get, down_far)
        up_far, down_far = line.put(up_far)[None], line.put(down_far)[None]
        up_far_other, down_far_other = swap(up_far, "seq", 1), swap(down_far, "seq", 1)
        down_near = stack(sc, *line.put(down_own, down_y, down_z))
        line.mark(down_near)
        down_near_other = swap(down_near, "seq", 1)
        ups = (up_near, up_near_other, up_far, up_far_other)
        downs = (down_near, down_near_other, down_far, down_far_other)
    n_get = swap(line.put(n_send), "seq", 1)
    hid_own_get = swap(line.put(hid_own), "seq", 1)
    hid_oth, slope_oth, total = ffn_fwd(sc, line.put(low), vector(b_other), ups, downs, split, total)
    line.mark(hid_oth)
    line.need(n_get)
    hid_oth_get = swap(hid_oth, "seq", 1)

    output, g_two, g_down, d_keep, d_send, sums_two = norm_two(
        sc, line.put(total), hat, gain_a, shift_a, vector(b_down), gain_b, shift_b, spots, cot, n_seq
    )
    line.mark(g_down)
    line.need(hid_own_get, hid_oth_get)
    d_get = swap(d_send, "seq", 1)

    found_bits = bits_of(n_seq)
    seq_bits = [2] + found_bits[2:][::-1]
    x_step = ("ffn", 1)
    y_step = ("seq", 2)
    z_steps = [("seq", b) for b in found_bits[2:]]
    x_first = [("ffn", b) for b in bits_of(n_ffn)[::-1]] + z_steps + [y_step]
    z_axes = [(step, 2) for step in z_steps[::-1]]
    per = units // WIDE
    half = per // 2
    chunk = width // n_seq
    shards = lambda v, n, places: v.reshape(n, -1, places, chunk, WIDE)
    column = lambda start: (lambda b, sc: (0, start + b))
    d_left, n_left = (d_keep, d_get), (n_keep, n_get)

    def streams(found, blocks_a, blocks_b):
        a = [("block", blocks_a), (y_step, 2)] + z_axes
        b = [(x_step, 2), ("block", blocks_b)] + z_axes
        return Group(sc, line, [
            (a, found["keep_a"], found["send_a"], x_step),
            (b, found["keep_b"], found["send_b"], y_step),
        ])

    def big(left, own, own_get, oth, oth_get):
        left = (line.put(left[0]), left[1])
        found = weight_grad(sc, [left], [
            (oth, oth_get, half, column(0), 0, ("send_a",)),
            (own, own_get, per - half, column(half), 0, ("keep_b", "send_b")),
            (oth, oth_get, per - half, column(half), 0, ("keep_b", "send_b")),
            (own, own_get, half, column(0), 0, ("keep_a",)),
        ])
        line.mark(found["keep_a"])
        return streams(found, half, per - half)

    def big_whole(left, own, own_get, oth, oth_get):
        n_oth = oth.shape[1] // WIDE
        left = (line.put(left[0]), left[1])
        found = weight_grad(sc, [left], [
            (own, own_get, per, column(0), 0, ("all",)), (oth, oth_get, n_oth, column(0), 0, ("all",))
        ])["all"]
        line.mark(found)
        return Stream(line, seq_bits, x_first, whole=shards(found, n_ffn, n_seq // 2))

    def narrow(mine, other, first, count, matrix, names):
        per_row = mine.shape[-1] // WIDE
        each = per_row * (mine.shape[0] if mine.ndim == 3 else 1) // n_ffn

        def segment(shard):
            def index(b, sc):
                block = (shard ^ sc[1]) * each + first + b
                return (0, block) if mine.ndim == 2 else (block // per_row, 0, block % per_row)

            return (mine, other, count, index, matrix, names)

        return segment

    def narrow_whole(left, mine, other):
        per_row = mine.shape[-1] // WIDE
        blocks = per_row * (mine.shape[0] if mine.ndim == 3 else 1)
        index = (lambda b, sc: (0, b)) if mine.ndim == 2 else (lambda b, sc: (b // per_row, 0, b % per_row))
        whole = weight_grad(sc, [(line.put(left[0]), left[1])], [(mine, other, blocks, index, 0, ("all",))])["all"]
        line.mark(whole)
        share = blocks * WIDE // n_ffn
        whole = whole.reshape(blocks, n_seq // 2, chunk, WIDE)
        whole = jnp.transpose(whole, (1, 2, 0, 3)).reshape(n_seq // 2, chunk, n_ffn, share)
        whole = jnp.take(jnp.transpose(whole, (2, 0, 1, 3)), order, axis=0)[:, None]
        return Stream(line, seq_bits, x_first, whole=whole)

    ways = {} if not pairs else {"z": [(z_steps[0],), (z_steps[1],), (y_step, x_step)], "y": [(y_step, x_step), (z_steps[0],), (z_steps[1],)]}
    way_d, way_u = list(ways.get("z", ())), list(ways.get("z", ()))
    if pairs:
        held = in_hbm(*ups, *downs)
        ups, downs = held[:4], held[4:]
    columns = lambda count, first, target=0, turned=False: [
        (target, (first + n) * WIDE, turned) for n in range(count)
    ]
    if pairs:
        ops = {}

        def wg_d():
            ops["D"] = big(d_left, hid_own, hid_own_get, hid_oth, hid_oth_get)

        def ffn_back():
            gp_oth, gp_own, bs_oth, bs_own, total = ffn_both(
                sc, line.put(g_down), slope_oth, slope_own, ups, downs, w_up, w_down
            )
            line.mark(gp_own)
            ops["gp"] = (gp_own, swap(gp_own, "seq", 1), gp_oth, swap(gp_oth, "seq", 1))
            ops["bs"] = (bs_own, bs_oth)
            ops["total"] = total

        def norm_back_one():
            ops["one"] = norm_one_back(sc, line.put(g_two), ops["total"], hat, inv, gain_a, w_out)
            line.mark(ops["one"][2])
            ops["low"] = (ops["one"][1], swap(ops["one"][1], "seq", 1))

        def wg_u():
            line.need(ops["gp"][1], ops["gp"][3])
            ops["U"] = big(n_left, *ops["gp"])

        def back():
            g_qkv, sums_att = attend_back(sc, line.put(qkv), att, ops["one"][2], logs)
            line.mark(g_qkv)
            ops["qkv"] = (g_qkv, swap(g_qkv, "seq", 1))
            ops["sums_att"] = sums_att

        def wg_q():
            q = ops["qkv"]
            lefts = [(line.put(x_keep), x_get), (att_keep, att_get)]
            q_a = narrow(*q, 0, 2, 0, ("send_a",))
            q_b = narrow(*q, 2, 1, 0, ("keep_b", "send_b"))
            o_b = narrow(*ops["low"], 0, 1, 1, ("keep_b", "send_b"))
            ops["found"] = weight_grad(sc, lefts, [q_a(1), q_b(0), o_b(0), q_b(1), o_b(1)])
            line.mark(ops["found"]["keep_b"])

        def wg_q_rest():
            q_keep = narrow(*ops["qkv"], 0, 2, 0, ("keep_a",))
            found = dict(ops["found"])
            found.update(weight_grad(sc, [(line.put(x_keep), x_get)], [q_keep(0)]))
            line.mark(found["keep_a"])
            ops["Q"] = streams(found, 2, 2)

        def tokens_back():
            ops["tokens"] = token_grads(sc, line.put(ops["qkv"][0]), w_qkv, ops["one"][0], spots, slots)
            line.mark(ops["tokens"][0])

        def sums_start():
            bs_own, bs_oth = ops["bs"]
            ops["sums"] = pack(line.put(sc), sums_two, ops["one"][3], bs_own, bs_oth, ops["sums_att"])
            line.mark(ops["sums"])
            ops["sum_steps"] = [("seq", b) for b in bits_of(n_seq)] + [("ffn", b) for b in bits_of(n_ffn)]
            sums_post()

        def sums_post():
            step = ops["sum_steps"].pop(0)
            ops["got"] = swap(line.put(ops["sums"]), *step)

        def sums_add():
            mine, got = line.put(ops["sums"], ops["got"])
            ops["sums"] = mine + got
            line.mark(ops["sums"])
            if ops["sum_steps"]:
                sums_post()

        def step_of(name, way):
            return lambda: ops[name].advance(*way.pop(0))

        def end_d():
            ops["down"] = ops["D"].finish(
                [columns(half, 0, turned=True), columns(per - half, half, turned=True)], [(units, chunk)]
            )

        def end_u():
            ops["up"] = ops["U"].finish([columns(half, 0), columns(per - half, half)], [(chunk, units)])

        def end_q():
            ops["last"] = ops["Q"].finish(
                [columns(2, 0), columns(1, 2) + columns(1, 0, 1)], [(chunk, 3 * WIDE), (chunk, WIDE)]
            )

        way_q = [(y_step, x_step), (z_steps[0],), (z_steps[1],)]
        steps = {
            "gD": wg_d, "B": ffn_back, "N": norm_back_one, "gU": wg_u, "A": back, "G": wg_q, "H": wg_q_rest,
            "T": tokens_back, "P": sums_start, "S": sums_add, "D": step_of("D", way_d), "U": step_of("U", way_u),
            "Q": step_of("Q", way_q), "eD": end_d, "eU": end_u, "eQ": end_q,
        }
        for name in SEQUENCE:
            steps[name]()
        grad_tokens, grad_fill = ops["tokens"]
        (grad_down,), (grad_up,) = ops["down"], ops["up"]
        grad_qkv, grad_out = ops["last"]
        total_sums = ops["sums"].reshape(-1)
    else:
        down_a = big_whole(d_left, hid_own, hid_own_get, hid_oth, hid_oth_get)
        gp_oth, bs_oth, g_total = ffn_bwd(sc, line.put(g_down), slope_oth, ups, downs, split)
        line.mark(gp_oth)
        gp_oth_get = swap(gp_oth, "seq", 1)
        gp_own, bs_own, g_total = ffn_bwd(sc, line.put(g_down), slope_own, (w_up,), (w_down,), "own", g_total)
        line.mark(gp_own)
        gp_own_get = swap(gp_own, "seq", 1)
        g_one, g_att_low, g_att, sums_one = norm_one_back(sc, line.put(g_two), g_total, hat, inv, gain_a, w_out)
        line.mark(g_att)
        g_att_get = swap(g_att_low, "seq", 1)
        up_a = big_whole(n_left, gp_own, gp_own_get, gp_oth, gp_oth_get)
        g_qkv, sums_att = attend_back(sc, line.put(qkv), att, g_att, logs)
        line.mark(g_qkv)
        g_qkv_get = swap(g_qkv, "seq", 1)
        b_up_sums = jnp.concatenate([bs_own.reshape(1, units), bs_oth.reshape(n_ffn - 1, units)])
        b_up_sums = jnp.take(b_up_sums, order, axis=0).reshape(-1)
        sums = jnp.concatenate(
            [sums_two[:3].reshape(-1), sums_one[:3].reshape(-1), b_up_sums, sums_att.reshape(-1)]
        )
        grad_tokens, grad_fill = token_grads(sc, line.put(g_qkv), w_qkv, g_one, spots, slots)
        line.mark(grad_tokens)
        out = narrow_whole((att_keep, att_get), g_att_low, g_att_get)
        qkv_a = narrow_whole((x_keep, x_get), g_qkv, g_qkv_get)
        (*_, total_sums) = all_sum(line, sums, n_seq, n_ffn)
        grad_down, grad_up = columns_of(down_a.finish()).T, columns_of(up_a.finish())
        grad_out, grad_qkv = columns_of(out.finish()), columns_of(qkv_a.finish())
    hidden_units = n_ffn * units

    part = lambda v, n: v[n * width : (n + 1) * width]
    return (
        output,
        grad_tokens,
        grad_fill[None],
        grad_qkv,
        total_sums[6 * width + hidden_units : 7 * width + hidden_units],
        total_sums[7 * width + hidden_units : 8 * width + hidden_units],
        grad_out,
        part(total_sums, 5),
        part(total_sums, 3),
        part(total_sums, 4),
        grad_up,
        total_sums[6 * width : 6 * width + hidden_units],
        grad_down,
        part(total_sums, 2),
        part(total_sums, 0),
        part(total_sums, 1),
    )


def solution(mesh):
    rows = ("seq", "ffn")
    in_specs = (
        P(rows, None),
        P(rows, None),
        P(rows),
        P(rows, None, None),
        P(rows, None, None),
        P(),
        P(),
        P(),
        P(),
        P(),
        P(),
        P(),
        P(None, "ffn"),
        P("ffn"),
        P("ffn", None),
        P(),
        P(),
        P(),
    )
    out_specs = (
        P(rows, None),
        P(rows, None),
        P(rows, None, None),
        P("seq", "ffn"),
        P(),
        P(),
        P("seq", "ffn"),
        P(),
        P(),
        P(),
        P("seq", "ffn"),
        P(),
        P("ffn", "seq"),
        P(),
        P(),
        P(),
    )
    return jax.shard_map(on_device, mesh=mesh, in_specs=in_specs, out_specs=out_specs, check_vma=False)
```

```python
import functools

import jax
import jax.numpy as jnp
from jax import lax
from jax.experimental import pallas as pl
from jax.experimental.pallas import tpu as pltpu
from jax.sharding import PartitionSpec as P

H = 16
F32 = jnp.float32
LOW = jnp.bfloat16
epsilon = 1e-12
LOG2E = 1.4426950408889634
NT = (((1,), (1,)), ((), ()))
WIDE = 512
SEQUENCE = ("gD", "B", "N", "D!", "gU", "A", "P", "D", "S", "U!", "S", "G", "S", "H", "D", "T", "Q", "S", "U", "S", "Q", "eD", "U", "Q", "eU", "eQ")
STEP = 3 * 10**10


def mm(left, right):
    return jnp.dot(left, right, preferred_element_type=F32)


def mm_nt(left, right):
    return lax.dot_general(left, right, NT, preferred_element_type=F32)


def call(body, grid, in_specs, out_specs, out_shape, scratch=(), prefetch=1, mib=32, weight=0):
    return pl.pallas_call(
        body,
        grid_spec=pltpu.PrefetchScalarGridSpec(
            num_scalar_prefetch=prefetch,
            grid=grid,
            in_specs=in_specs,
            out_specs=out_specs,
            scratch_shapes=list(scratch),
        ),
        out_shape=out_shape,
        compiler_params=pltpu.CompilerParams(
            dimension_semantics=("arbitrary",) * len(grid), vmem_limit_bytes=mib << 20
        ),
        cost_estimate=pl.CostEstimate(flops=int(1 + weight * STEP), bytes_accessed=1, transcendentals=0),
    )


def far(dims, dtype):
    return pltpu.HBM(dims, dtype)


def in_hbm(*values):
    return [pltpu.with_memory_space_constraint(value, pltpu.HBM) for value in values]


def spec(shape, index):
    return pl.BlockSpec(shape, index)


def shape(dims, dtype):
    return jax.ShapeDtypeStruct(dims, dtype)


def one_hot_rows(sc, spots, first, rows):
    slots = spots.shape[1]
    place = lax.broadcasted_iota(jnp.int32, (rows, slots), 0) + first
    slot = lax.broadcasted_iota(jnp.int32, (rows, slots), 1)
    hit = (place == spots) & (slot < sc[2])
    return jnp.where(hit, 1.0, 0.0)


def store_turned(sc, value, keep_ref, send_ref, first_column, chunk):
    columns = value.shape[1]
    for block in range(0, columns, 128):
        turned = jnp.transpose(value[:, block : block + 128]).astype(LOW)
        for part in range(0, 128, chunk):
            place = ((first_column + block + part) // chunk) ^ sc[0]
            piece = turned[part : part + chunk]
            at = ((place // 2) % 2) * (keep_ref.shape[0] // 2) + place // 4

            @pl.when(place % 2 == 0)
            def _():
                keep_ref[at] = piece

            @pl.when(place % 2 == 1)
            def _():
                send_ref[at] = piece


def qkv_body(chunk, sc, tokens, spots, fill, w, bias, x_out, keep, send, qkv):
    @pl.when(pl.program_id(0) == 0)
    def _():
        placed = one_hot_rows(sc, spots[...], 0, tokens.shape[0])
        kept = 1.0 - jnp.sum(placed, axis=1, keepdims=True)
        x = tokens[...].astype(F32) * kept + mm(placed.astype(LOW), fill[...])
        x_out[...] = x.astype(LOW)
        store_turned(sc, x, keep, send, 0, chunk)

    qkv[...] = (mm(x_out[...], w[...]) + bias[...]).astype(LOW)


def embed_qkv(sc, tokens, spots, fill, w_qkv, bias, n_seq):
    rows, width = tokens.shape
    out = w_qkv.shape[1]
    block = 512
    chunk = width // n_seq
    turned = (n_seq // 2, chunk, rows)
    whole = lambda j, sc: (0, 0)
    return call(
        functools.partial(qkv_body, chunk),
        (out // block,),
        [
            spec((rows, width), whole),
            spec(spots.shape, whole),
            spec(fill.shape, whole),
            spec((width, block), lambda j, sc: (0, j)),
            spec((1, block), lambda j, sc: (0, j)),
        ],
        [
            spec((rows, width), whole),
            spec(turned, lambda j, sc: (0, 0, 0)),
            spec(turned, lambda j, sc: (0, 0, 0)),
            spec((rows, block), lambda j, sc: (0, j)),
        ],
        [shape((rows, width), LOW), far(turned, LOW), far(turned, LOW), shape((rows, out), LOW)],
        weight=1,
    )(sc, tokens, spots, fill, w_qkv, bias)


def head_masks(width, size, factor):
    lane = lax.broadcasted_iota(jnp.int32, (1, width), 1)
    return [jnp.where(lane // size == n, factor, 0.0).astype(LOW) for n in range(width // size)]


def attend_body(chunk, size, scale, sc, q, k, v, att, keep, send, logs):
    rows, width = q.shape
    pair = 2 * size
    masks = head_masks(pair, size, scale)
    lane = lax.broadcasted_iota(jnp.int32, (1, pair), 1)
    place_first = pl.program_id(0) * width
    for first in range(0, width, pair):
        columns = slice(first, first + pair)
        mixed, stats = [], []
        for mask in masks:
            scores = mm_nt(q[:, columns] * mask, k[:, columns])
            peak = jnp.max(scores, axis=1, keepdims=True) * LOG2E
            expo = jnp.exp2(scores * LOG2E - peak)
            total = jnp.sum(expo, axis=1, keepdims=True)
            mixed.append(mm(expo.astype(LOW), v[:, columns]) * (1.0 / total))
            stats.append(peak + jnp.log2(total))
        both = jnp.where(lane < size, mixed[0], mixed[1])
        att[:, columns] = both.astype(LOW)
        logs[:, columns] = jnp.where(lane < size, stats[0], stats[1])
        store_turned(sc, both, keep, send, place_first + first, chunk)


def attend(sc, qkv, n_seq):
    rows = qkv.shape[0]
    width = qkv.shape[1] // 3
    size = width // H
    block = 4 * size
    steps = width // block
    chunk = width // n_seq
    turned = (n_seq // 2, chunk, rows)
    whole = lambda j, sc: (0, 0, 0)
    tile = spec((rows, block), lambda j, sc: (0, j))
    return call(
        functools.partial(attend_body, chunk, size, size ** (-0.5)),
        (steps,),
        [
            tile,
            spec((rows, block), lambda j, sc: (0, steps + j)),
            spec((rows, block), lambda j, sc: (0, 2 * steps + j)),
        ],
        [tile, spec(turned, whole), spec(turned, whole), tile],
        [shape((rows, width), LOW), far(turned, LOW), far(turned, LOW), shape((rows, width), F32)],
        weight=1,
    )(sc, qkv, qkv, qkv)


def norm_one_body(chunk, sc, att, w, x, b, gain, shift, hat, inv, low, keep, send):
    value = x[...].astype(F32) + mm(att[...], w[...]) + b[...]
    centre = value - jnp.mean(value, axis=-1, keepdims=True)
    spread = jnp.mean(centre * centre, axis=-1, keepdims=True)
    inverse = lax.rsqrt(spread + epsilon)
    scaled = centre * inverse
    hat[...] = scaled
    inv[...] = inverse
    normed = scaled * gain[...] + shift[...]
    low[...] = normed.astype(LOW)
    store_turned(sc, normed, keep, send, 0, chunk)


def norm_one(sc, att, w_out, x, b_out, gain, shift, n_seq):
    rows, width = x.shape
    block = 512
    chunk = width // n_seq
    turned = (n_seq // 2, chunk, rows)
    row = lambda i, sc: (i, 0)
    whole = lambda i, sc: (0, 0)
    vector = spec((1, width), whole)
    return call(
        functools.partial(norm_one_body, chunk),
        (rows // block,),
        [spec((block, width), row), spec((width, width), whole), spec((block, width), row), vector, vector, vector],
        [
            spec((block, width), row),
            spec((block, 1), row),
            spec((block, width), row),
            spec((n_seq // 2, chunk, block), lambda i, sc: (0, 0, i)),
            spec((n_seq // 2, chunk, block), lambda i, sc: (0, 0, i)),
        ],
        [
            far((rows, width), F32),
            shape((rows, 1), F32),
            shape((rows, width), LOW),
            far(turned, LOW),
            far(turned, LOW),
        ],
        weight=1,
    )(sc, att, w_out, x, b_out, gain, shift)


TAIL = tuple(0.5 * c for c in (0.254829592, -0.284496736, 1.421413741, -1.453152027, 1.061405429))
TAIL_P = 0.3275911 * 0.7071067811865476


def gelu_both(x):
    t = 1.0 / (1.0 + TAIL_P * jnp.abs(x))
    bell = jnp.exp2(x * x * (-0.5 * LOG2E))
    poly = TAIL[4]
    for c in TAIL[3::-1]:
        poly = poly * t + c
    tail = poly * t * bell
    mass = jnp.where(x < 0.0, tail, 1.0 - tail)
    return x * mass, mass + x * bell * 0.3989422804014327


def ffn_specs(split, width, part):
    if split == "own":
        ups = [spec((width, WIDE), lambda j, sc: (0, j))]
        downs = [spec((WIDE, width), lambda j, sc: (j, 0))]
        return ups, downs, WIDE
    if split == "stack":
        ups = [spec((None, width, part), lambda j, sc: (j, 0, 0))]
        downs = [spec((None, part, width), lambda j, sc: (j, 0, 0))]
        return ups, downs, part
    near = lambda j, sc: (jnp.minimum(j, 2), 0, 0)
    far = lambda j, sc: (0, 0, 0)
    ups = [spec((None, width, part), at) for at in (near, near, far, far)]
    downs = [spec((None, part, width), at) for at in (near, near, far, far)]
    return ups, downs, part


def column_block(split):
    if split == "pairs":
        return lambda j, sc: (0, j ^ ((sc[0] // 2) % 4))
    return lambda j, sc: (0, j)


def for_pieces(split, size, sc, ups, downs, work):
    if split != "pairs":
        work([(ups[0], downs[0], 0)])
        return
    core = sc[0] % 2
    places = [pl.multiple_of(core * size, size), pl.multiple_of((1 - core) * size, size)]
    step = pl.program_id(0)
    pl.when(step < 3)(lambda: work(list(zip(ups[:2], downs[:2], places))))
    pl.when(step == 3)(lambda: work(list(zip(ups[2:], downs[2:], places))))


def ffn_fwd_body(split, size, n, first, sc, *refs):
    low, bias = refs[:2]
    ups, downs = refs[2 : 2 + n], refs[2 + n : 2 + 2 * n]
    rest = refs[2 + 2 * n :]
    start = None
    if not first:
        start, rest = rest[0], rest[1:]
    hidden, slope, total = rest
    @pl.when(pl.program_id(0) == 0)
    def _():
        total[...] = jnp.zeros_like(total) if first else start[...]

    def work(pieces):
        mixed = None
        for up, down, offset in pieces:
            columns = pl.ds(offset, size)
            pre = mm(low[...], up[...]) + bias[:, columns]
            act, grad = gelu_both(pre)
            act = act.astype(LOW)
            hidden[:, columns] = act
            slope[:, columns] = grad.astype(LOW)
            product = mm(act, down[...])
            mixed = product if mixed is None else mixed + product
        total[...] += mixed

    for_pieces(split, size, sc, ups, downs, work)


def ffn_fwd(sc, low, bias, ups, downs, split, start=None):
    rows, width = low.shape
    units = bias.shape[1]
    part = ups[0].shape[-1]
    up_specs, down_specs, size = ffn_specs(split, width, part)
    step = WIDE if split != "stack" else part
    whole = lambda j, sc: (0, 0)
    column = column_block(split)
    total = spec((rows, width), whole)
    first = start is None
    return call(
        functools.partial(ffn_fwd_body, split, size, len(ups), first),
        (units // step,),
        [total, spec((1, step), column)] + up_specs + down_specs + ([] if first else [total]),
        [spec((rows, step), column), spec((rows, step), column), total],
        [shape((rows, units), LOW), shape((rows, units), LOW), shape((rows, width), F32)],
        weight=1,
    )(sc, low, bias, *ups, *downs, *([] if first else [start]))


def ffn_bwd_body(split, size, n, first, sc, *refs):
    low, slope = refs[:2]
    ups, downs = refs[2 : 2 + n], refs[2 + n : 2 + 2 * n]
    rest = refs[2 + 2 * n :]
    start = None
    if not first:
        start, rest = rest[0], rest[1:]
    g_low, sums, total = rest
    @pl.when(pl.program_id(0) == 0)
    def _():
        total[...] = jnp.zeros_like(total) if first else start[...]

    def work(pieces):
        mixed = None
        for up, down, offset in pieces:
            columns = pl.ds(offset, size)
            g_pre = mm_nt(low[...], down[...]) * slope[:, columns].astype(F32)
            sums[:, columns] = jnp.sum(g_pre, axis=0, keepdims=True)
            rounded = g_pre.astype(LOW)
            g_low[:, columns] = rounded
            product = mm_nt(rounded, up[...])
            mixed = product if mixed is None else mixed + product
        total[...] += mixed

    for_pieces(split, size, sc, ups, downs, work)


def ffn_bwd(sc, low, slope, ups, downs, split, start=None):
    rows, width = low.shape
    units = slope.shape[1]
    part = ups[0].shape[-1]
    up_specs, down_specs, size = ffn_specs(split, width, part)
    step = WIDE if split != "stack" else part
    whole = lambda j, sc: (0, 0)
    column = column_block(split)
    total = spec((rows, width), whole)
    first = start is None
    return call(
        functools.partial(ffn_bwd_body, split, size, len(ups), first),
        (units // step,),
        [total, spec((rows, step), column)] + up_specs + down_specs + ([] if first else [total]),
        [spec((rows, step), column), spec((1, step), column), total],
        [shape((rows, units), LOW), shape((1, units), F32), shape((rows, width), F32)],
    )(sc, low, slope, *ups, *downs, *([] if first else [start]))


def ffn_both_body(size, sc, low, slope_oth, slope_own, *refs):
    ups, downs, (up, down) = refs[:4], refs[4:8], refs[8:10]
    g_oth, g_own, sums_oth, sums_own, total = refs[10:]
    core = sc[0] % 2
    places = [pl.multiple_of(core * size, size), pl.multiple_of((1 - core) * size, size)]
    step = pl.program_id(0)

    def work(pieces, slope, g_low, sums):
        mixed = None
        for up_ref, down_ref, offset, span in pieces:
            columns = pl.ds(offset, span)
            g_pre = mm_nt(low[...], down_ref[...]) * slope[:, columns].astype(F32)
            sums[:, columns] = jnp.sum(g_pre, axis=0, keepdims=True)
            rounded = g_pre.astype(LOW)
            g_low[:, columns] = rounded
            product = mm_nt(rounded, up_ref[...])
            mixed = product if mixed is None else mixed + product

        @pl.when(step == 0)
        def _():
            total[...] = mixed

        @pl.when(step > 0)
        def _():
            total[...] += mixed

    other = lambda group: [(u, d, place, size) for u, d, place in zip(ups[group], downs[group], places)]
    pl.when(step < 3)(lambda: work(other(slice(0, 2)), slope_oth, g_oth, sums_oth))
    pl.when(step == 3)(lambda: work(other(slice(2, 4)), slope_oth, g_oth, sums_oth))
    pl.when(step > 3)(lambda: work([(up, down, 0, 2 * size)], slope_own, g_own, sums_own))


def ffn_both(sc, low, slope_oth, slope_own, ups, downs, up, down):
    rows, width = low.shape
    units = slope_own.shape[1]
    part = ups[0].shape[-1]
    wide = 2 * part
    steps = units // wide
    whole = lambda j, sc: (0, 0)
    near = lambda j, sc: (jnp.minimum(j, 2), 0, 0)
    away = lambda j, sc: (0, 0, 0)
    oth = lambda j, sc: (0, jnp.minimum(j, 3) ^ ((sc[0] // 2) % 4))
    own = lambda j, sc: (0, jnp.maximum(j - 4, 0))
    own_row = lambda j, sc: (jnp.maximum(j - 4, 0), 0)
    return call(
        functools.partial(ffn_both_body, part),
        (4 + steps,),
        [spec((rows, width), whole), spec((rows, wide), oth), spec((rows, wide), own)]
        + [spec((None, width, part), at) for at in (near, near, away, away)]
        + [spec((None, part, width), at) for at in (near, near, away, away)]
        + [spec((width, wide), own), spec((wide, width), own_row)],
        [spec((rows, wide), oth), spec((rows, wide), own), spec((1, wide), oth), spec((1, wide), own), spec((rows, width), whole)],
        [far((rows, units), LOW), far((rows, units), LOW), shape((1, units), F32), shape((1, units), F32), shape((rows, width), F32)],
        weight=0,
    )(sc, low, slope_oth, slope_own, *ups, *downs, up, down)


def norm_back(hat, inverse, gain, grad):
    inner = grad * gain
    mean = jnp.mean(inner, axis=-1, keepdims=True)
    along = jnp.mean(inner * hat, axis=-1, keepdims=True)
    return inverse * (inner - mean - hat * along)


def add_sums(sums, rows):
    @pl.when(pl.program_id(0) == 0)
    def _():
        sums[...] = jnp.zeros_like(sums)

    for n, value in enumerate(rows):
        sums[n : n + 1, :] += jnp.sum(value, axis=0, keepdims=True)


def norm_two_body(chunk, sc, mixed, hat_one, gain_one, shift_one, b_down, gain, shift, spots, cot, out, grad, low, keep, send, sums):
    rows = mixed.shape[0]
    value = hat_one[...] * gain_one[...] + shift_one[...] + mixed[...] + b_down[...]
    centre = value - jnp.mean(value, axis=-1, keepdims=True)
    spread = jnp.mean(centre * centre, axis=-1, keepdims=True)
    inverse = lax.rsqrt(spread + epsilon)
    hat = centre * inverse
    out[...] = (hat * gain[...] + shift[...]).astype(LOW)
    placed = one_hot_rows(sc, spots[...], pl.program_id(0) * rows, rows)
    out_grad = mm(placed.astype(LOW), cot[...])
    result = norm_back(hat, inverse, gain[...], out_grad)
    grad[...] = result
    low[...] = result.astype(LOW)
    store_turned(sc, result, keep, send, 0, chunk)
    add_sums(sums, (out_grad * hat, out_grad, result))


def norm_two(sc, mixed, hat_one, gain_one, shift_one, b_down, gain, shift, spots, cot, n_seq):
    rows, width = mixed.shape
    block = 512
    chunk = width // n_seq
    turned = (n_seq // 2, chunk, rows)
    row = lambda i, sc: (i, 0)
    whole = lambda i, sc: (0, 0)
    vector = spec((1, width), whole)
    tile = spec((block, width), row)
    return call(
        functools.partial(norm_two_body, chunk),
        (rows // block,),
        [tile, tile, vector, vector, vector, vector, vector, spec(spots.shape, whole), spec(cot.shape, whole)],
        [
            tile,
            tile,
            tile,
            spec((n_seq // 2, chunk, block), lambda i, sc: (0, 0, i)),
            spec((n_seq // 2, chunk, block), lambda i, sc: (0, 0, i)),
            spec((8, width), whole),
        ],
        [
            shape((rows, width), LOW),
            shape((rows, width), F32),
            shape((rows, width), LOW),
            far(turned, LOW),
            far(turned, LOW),
            shape((8, width), F32),
        ],
        weight=1,
    )(sc, mixed, hat_one, gain_one, shift_one, b_down, gain, shift, spots, cot)


def norm_one_back_body(sc, grad_two, ffn, hat, inv, gain, w, grad, low, g_att, sums):
    g_normed = grad_two[...] + ffn[...]
    result = norm_back(hat[...], inv[...], gain[...], g_normed)
    grad[...] = result
    rounded = result.astype(LOW)
    low[...] = rounded
    g_att[...] = mm_nt(rounded, w[...]).astype(LOW)
    add_sums(sums, (g_normed * hat[...], g_normed, result))


def norm_one_back(sc, grad_two, ffn, hat, inv, gain, w_out):
    rows, width = hat.shape
    block = 512
    row = lambda i, sc: (i, 0)
    whole = lambda i, sc: (0, 0)
    tile = spec((block, width), row)
    return call(
        norm_one_back_body,
        (rows // block,),
        [tile, tile, tile, spec((block, 1), row), spec((1, width), whole), spec((width, width), whole)],
        [tile, tile, tile, spec((8, width), whole)],
        [shape((rows, width), F32), shape((rows, width), LOW), shape((rows, width), LOW), shape((8, width), F32)],
        weight=0,
    )(sc, grad_two, ffn, hat, inv, gain, w_out)


def mm_tn(left, right):
    return lax.dot_general(left, right, (((0,), (0,)), ((), ())), preferred_element_type=F32)


def attend_back_body(size, scale, sc, q, k, v, att, g_att, logs, g_qkv, sums):
    rows, width = q.shape
    pair = 2 * size
    ones = head_masks(pair, size, 1.0)
    halves = head_masks(pair, size, scale)
    lane = lax.broadcasted_iota(jnp.int32, (1, pair), 1)
    for first in range(0, width, pair):
        columns = slice(first, first + pair)
        q_pair, k_pair, v_pair, g_pair = q[:, columns], k[:, columns], v[:, columns], g_att[:, columns]
        q_scaled = q_pair * jnp.asarray(scale, LOW)
        k_scaled = k_pair * jnp.asarray(scale, LOW)
        product = att[:, columns].astype(F32) * g_pair.astype(F32)
        log_pair = logs[:, columns]
        turned_v, turned_k, g_q = [], [], []
        for n in range(2):
            rows_of = slice(n * size, (n + 1) * size)
            scores = mm_nt(q_pair * halves[n], k_pair)
            probs = jnp.exp2(scores * LOG2E - log_pair[:, n * size : n * size + 1])
            g_probs = mm_nt(g_pair * ones[n], v_pair)
            level = jnp.sum(jnp.where(lane // size == n, product, 0.0), axis=1, keepdims=True)
            g_scores = (probs * (g_probs - level)).astype(LOW)
            turned_v.append(mm_tn(g_pair, probs.astype(LOW))[rows_of])
            turned_k.append(mm_tn(q_scaled, g_scores)[rows_of])
            g_q.append(mm(g_scores, k_scaled))
        query = jnp.where(lane < size, g_q[0], g_q[1]).astype(LOW)
        value = jnp.transpose(jnp.concatenate(turned_v, axis=0)).astype(LOW)
        g_qkv[0, :, columns] = query
        g_qkv[1, :, columns] = jnp.transpose(jnp.concatenate(turned_k, axis=0)).astype(LOW)
        g_qkv[2, :, columns] = value
        sums[0:1, columns] = jnp.sum(query.astype(F32), axis=0, keepdims=True)
        sums[1:2, columns] = jnp.sum(value.astype(F32), axis=0, keepdims=True)


def attend_back(sc, qkv, att, g_att, logs):
    rows, width = att.shape
    size = width // H
    block = 4 * size
    steps = width // block
    tile = spec((rows, block), lambda j, sc: (0, j))
    return call(
        functools.partial(attend_back_body, size, size ** (-0.5)),
        (steps,),
        [
            tile,
            spec((rows, block), lambda j, sc: (0, steps + j)),
            spec((rows, block), lambda j, sc: (0, 2 * steps + j)),
            tile,
            tile,
            tile,
        ],
        [spec((3, rows, block), lambda j, sc: (0, 0, j)), spec((2, block), lambda j, sc: (0, j))],
        [far((3, rows, width), LOW), shape((2, width), F32)],
        weight=0,
    )(sc, qkv, qkv, qkv, att, g_att, logs)


def token_grads_body(sc, g_qkv, w, base, spots, spots_column, tokens_out, fill_out):
    rows = base.shape[0]
    width = g_qkv.shape[2]
    grad = base[...]
    for n in range(3):
        grad = grad + mm_nt(g_qkv[n], w[:, n * width : (n + 1) * width])
    placed = one_hot_rows(sc, spots[...], 0, rows)
    kept = 1.0 - jnp.sum(placed, axis=1, keepdims=True)
    tokens_out[...] = (grad * kept).astype(LOW)
    slots = spots_column.shape[0]
    place = lax.broadcasted_iota(jnp.int32, (slots, rows), 1)
    slot = lax.broadcasted_iota(jnp.int32, (slots, rows), 0)
    hit = (place == spots_column[...]) & (slot < sc[2])
    fill_out[...] = mm(jnp.where(hit, 1.0, 0.0).astype(LOW), grad.astype(LOW)).astype(LOW)


def token_grads(sc, g_qkv, w_qkv, base, spots, slots):
    rows, width = base.shape
    block = 512
    column = lambda i, sc: (0, i)
    whole = lambda i, sc: (0, 0)
    tile = spec((rows, block), column)
    return call(
        token_grads_body,
        (width // block,),
        [
            spec(g_qkv.shape, lambda i, sc: (0, 0, 0)),
            spec((block, w_qkv.shape[1]), lambda i, sc: (i, 0)),
            tile,
            spec(spots.shape, whole),
            spec((slots, 1), whole),
        ],
        [tile, spec((slots, block), column)],
        [shape((rows, width), LOW), shape((slots, width), LOW)],
        weight=0.35,
    )(sc, g_qkv, w_qkv, base, spots, spots.reshape(slots, 1))


def weight_body(plan, lefts, sc, *refs):
    left_refs, refs = refs[: 2 * lefts], refs[2 * lefts :]
    ins, outs = refs[: 2 * len(plan)], refs[2 * len(plan) :]
    step = pl.program_id(0)
    first = 0
    for n, (count, matrix, targets) in enumerate(plan):
        left, left_other = left_refs[2 * matrix : 2 * matrix + 2]
        mine, other = ins[2 * n], ins[2 * n + 1]

        def work(left=left, left_other=left_other, mine=mine, other=other, targets=targets):
            places, _, depth = left.shape
            rows_of = lambda ref: ref[...].reshape(-1, depth)
            total = mm(rows_of(left), mine[...]) + mm(rows_of(left_other), other[...])
            total = total.astype(LOW).reshape(places, -1, total.shape[-1])
            share = places // len(targets)
            for part, target in enumerate(targets):
                outs[target][...] = total[part * share : (part + 1) * share]

        if len(plan) == 1:
            work()
        else:
            pl.when((step >= first) & (step < first + count))(work)
        first += count


def weight_grad(sc, lefts, segments):
    places, chunk, depth = lefts[0][0].shape
    left_spec = spec((places, chunk, depth), lambda j, sc: (0, 0, 0))
    in_specs = [left_spec] * (2 * len(lefts))
    operands = [value for pair in lefts for value in pair]
    spans, plan, first = {}, [], 0
    for mine, other, count, index, matrix, names in segments:
        def at(j, sc, first=first, count=count, index=index):
            return index(jnp.clip(j - first, 0, count - 1), sc)

        block = (depth, WIDE) if mine.ndim == 2 else (None, depth, WIDE)
        in_specs += [spec(block, at), spec(block, at)]
        operands += [mine, other]
        for name in names:
            begin = spans.setdefault(name, [first, first, places // len(names)])
            begin[1] = first + count
        first += count
    order = list(spans)
    for _, _, count, _, matrix, names in segments:
        plan.append((count, matrix, tuple(order.index(name) for name in names)))
    out_specs, out_shapes = [], []
    for begin, end, kept in spans.values():
        at = lambda j, sc, begin=begin, end=end: (jnp.clip(j, begin, end - 1) - begin, 0, 0)
        out_specs.append(spec((kept, chunk, WIDE), at))
        out_shapes.append(far(((end - begin) * kept, chunk, WIDE), LOW))
    found = call(
        functools.partial(weight_body, tuple(plan), len(lefts)),
        (first,),
        in_specs,
        out_specs,
        out_shapes,
        weight=0,
    )(sc, *operands)
    return dict(zip(order, found))


def add_body(count, plan, sc, *refs):
    outs = refs[2 * count :]
    for source, start, (outer, inner), target, place in plan:
        span = pl.ds(start, outer * 2 * inner)
        total = refs[2 * source][span].astype(F32) + refs[2 * source + 1][span].astype(F32)
        total = total.astype(LOW).reshape((outer, 2, inner) + total.shape[1:])
        for half in range(2):
            part = total[:, half]
            outs[2 * target + half][pl.ds(place, outer * inner)] = part.reshape((outer * inner,) + part.shape[2:])


def add_halves(sc, arrays, plan, sizes, weight):
    tile = WIDE // 2
    chunk = arrays[0][0].shape[1]
    column = lambda j, sc: (0, 0, j)
    operands = [value for pair in arrays for value in pair]
    found = call(
        functools.partial(add_body, len(arrays), tuple(plan)),
        (WIDE // tile,),
        [spec(value.shape[:2] + (tile,), column) for value in operands],
        [spec((size, chunk, tile), column) for size in sizes for _ in range(2)],
        [far((size, chunk, WIDE), LOW) for size in sizes for _ in range(2)],
        weight=weight,
    )(sc, *operands)
    return [(found[2 * n], found[2 * n + 1]) for n in range(len(sizes))]


def last_body(count, plan, sc, *refs):
    for source, place, target, at, turned in plan:
        total = refs[2 * source][place].astype(F32) + refs[2 * source + 1][place].astype(F32)
        out = refs[2 * count + target]
        if turned:
            out[at : at + WIDE, :] = jnp.transpose(total)
        else:
            out[:, at : at + WIDE] = total


def add_last(sc, arrays, plan, outs):
    whole = lambda n: (lambda j, sc: (0,) * n)
    operands = [value for pair in arrays for value in pair]
    return call(
        functools.partial(last_body, len(arrays), tuple(plan)),
        (1,),
        [spec(value.shape, whole(3)) for value in operands],
        [spec(dims, whole(2)) for dims in outs],
        [shape(dims, F32) for dims in outs],
    )(sc, *operands)


def stack_body(sc, *refs):
    out = refs[-1]
    for n, ref in enumerate(refs[:-1]):
        out[n] = ref[...]


def stack(sc, *values):
    rows, columns = values[0].shape
    steps = 2
    return call(
        stack_body,
        (steps,),
        [spec((rows // steps, columns), lambda j, sc: (j, 0))] * len(values),
        spec((len(values), rows // steps, columns), lambda j, sc: (0, j, 0)),
        far((len(values),) + values[0].shape, LOW),
        weight=1,
    )(sc, *values)


def swap(value, axis, bit):
    size = lax.axis_size(axis)
    return lax.ppermute(value, axis, [(n, n ^ bit) for n in range(size)])


def halves(value, bits, step):
    shards, blocks, places, chunk, wide = value.shape
    axis, bit = step
    if axis == "ffn":
        return value[: shards // 2], value[shards // 2 :], bits
    at = bits.index(bit)
    low = 1 << (len(bits) - 1 - at)
    parts = value.reshape(shards, blocks, places // (2 * low), 2, low, chunk, wide)
    dims = (shards, blocks, places // 2, chunk, wide)
    return (
        parts[:, :, :, 0].reshape(dims),
        parts[:, :, :, 1].reshape(dims),
        bits[:at] + bits[at + 1 :],
    )


class Line:
    def __init__(self):
        self.last = ()

    def put(self, *values):
        if self.last:
            values = lax.optimization_barrier(self.last + values)[len(self.last) :]
        return values if len(values) > 1 else values[0]

    def mark(self, value):
        self.last = (value,)

    def need(self, *values):
        self.last += values


class Stream:
    def __init__(self, line, bits, steps, whole=None, keep=None, send=None):
        self.line, self.bits, self.steps = line, list(bits), list(steps)
        if keep is None:
            keep, send, self.bits = halves(whole, self.bits, self.steps[0])
        elif self.steps[0][0] == "seq":
            self.bits.remove(self.steps[0][1])
        self.post(keep, send)

    def post(self, keep, send):
        self.keep = keep
        self.got = swap(send, *self.steps.pop(0))

    def advance(self):
        keep, got = self.line.put(self.keep, self.got)
        if self.steps:
            step = self.steps[0]
            keep_a, send_a, left = halves(keep, self.bits, step)
            keep_b, send_b, left = halves(got, self.bits, step)
            self.bits = left
            add = lambda a, b: (a.astype(F32) + b.astype(F32)).astype(LOW)
            send = add(send_a, send_b)
            keep = add(keep_a, keep_b)
            self.line.mark(keep)
            self.post(keep, send)
            return None
        total = keep.astype(F32) + got.astype(F32)
        self.line.mark(total)
        return total

    def finish(self):
        while True:
            total = self.advance()
            if total is not None:
                return total


class Group:
    def __init__(self, sc, line, parts):
        self.sc, self.line = sc, line
        self.arrays = []
        self.parts = []
        for n, (axes, keep, send, step) in enumerate(parts):
            self.arrays.append((keep, swap(send, *step)))
            self.parts.append((n, 0, list(axes)))

    def tied(self):
        flat = self.line.put(*[value for pair in self.arrays for value in pair])
        return [(flat[2 * n], flat[2 * n + 1]) for n in range(len(self.arrays))]

    def advance(self, *steps, weight=0):
        steps = steps * len(self.parts) if len(steps) == 1 else steps
        order = list(dict.fromkeys(steps))
        plan, sizes, parts = [], [0] * len(order), []
        for (array, start, axes), step in zip(self.parts, steps):
            at = [name for name, _ in axes].index(step)
            outer = inner = 1
            for _, size in axes[:at]:
                outer *= size
            for _, size in axes[at + 1 :]:
                inner *= size
            target = order.index(step)
            plan.append((array, start, (outer, inner), target, sizes[target]))
            parts.append((target, sizes[target], axes[:at] + axes[at + 1 :]))
            sizes[target] += outer * inner
        found = add_halves(self.sc, self.tied(), plan, sizes, weight)
        self.line.mark(found[0][0])
        self.arrays = [(keep, swap(send, *step)) for (keep, send), step in zip(found, order)]
        self.parts = parts

    def finish(self, targets, outs):
        plan = []
        for (array, start, _), places in zip(self.parts, targets):
            for n, place in enumerate(places):
                plan.append((array, start + n) + place)
        found = add_last(self.sc, self.tied(), plan, outs)
        self.line.mark(found[0])
        return found


def pack_body(sc, two, one, own, other, att, out):
    out[...] = jnp.zeros_like(out)
    out[0:3, :] = two[0:3, :]
    out[3:6, :] = one[0:3, :]
    width = out.shape[1]
    count = own.shape[1] // width
    for n in range(count):
        columns = slice(n * width, (n + 1) * width)
        first = sc[1] == 0
        out[6 + n : 7 + n, :] = jnp.where(first, own[:, columns], other[:, columns])
        out[6 + count + n : 7 + count + n, :] = jnp.where(first, other[:, columns], own[:, columns])
    out[6 + 2 * count : 8 + 2 * count, :] = att[...]


def pack(sc, *values):
    width = values[0].shape[1]
    rows = 8 + 2 * values[2].shape[1] // width
    rows += -rows % 8
    whole = lambda j, sc: (0, 0)
    return call(
        pack_body,
        (1,),
        [spec(v.shape, whole) for v in values],
        spec((rows, width), whole),
        far((rows, width), F32),
        weight=0,
    )(sc, *values)


def cut_body(sc, *refs):
    for ref, out in zip(refs[:4], refs[4:]):
        out[...] = ref[...]


def cut(sc, w_up, w_down):
    width, units = w_up.shape
    part = units // 8
    steps = 2
    place = lambda sc, away: (((sc[0] // 2) % 4) ^ away) * 2 + sc[0] % 2
    ups = [spec((width // steps, part), lambda j, sc, n=n: (j, place(sc, n))) for n in (0, 3)]
    downs = [spec((part // steps, width), lambda j, sc, n=n: (place(sc, n) * steps + j, 0)) for n in (0, 3)]
    row = lambda j, sc: (j, 0)
    return call(
        cut_body,
        (steps,),
        ups + downs,
        [spec((width // steps, part), row)] * 2 + [spec((part // steps, width), row)] * 2,
        [far((width, part), LOW)] * 2 + [far((part, width), LOW)] * 2,
        weight=1,
    )(sc, w_up, w_up, w_down, w_down)


def all_sum(line, value, n_seq, n_ffn):
    for axis, size in (("seq", n_seq), ("ffn", n_ffn)):
        for bit in bits_of(size):
            value = value + line.put(swap(value, axis, bit))
            line.mark(value)
            yield value


def bits_of(size):
    found = []
    bit = 1
    while bit < size:
        found.append(bit)
        bit *= 2
    return found


def columns_of(found):
    found = found.reshape((-1,) + found.shape[3:])
    return jnp.transpose(found, (1, 0, 2)).reshape(found.shape[1], -1)


def on_device(
    tokens,
    spots,
    counts,
    fill,
    cot,
    w_qkv,
    b_q,
    b_v,
    w_out,
    b_out,
    gain_one,
    shift_one,
    w_up,
    b_up,
    w_down,
    b_down,
    gain_two,
    shift_two,
):
    n_seq, n_ffn = lax.axis_size("seq"), lax.axis_size("ffn")
    seq, ffn = lax.axis_index("seq"), lax.axis_index("ffn")
    rows, width = tokens.shape
    slots = spots.shape[1]
    units = w_up.shape[1]
    sc = jnp.stack([seq.astype(jnp.int32), ffn.astype(jnp.int32), counts[0]])
    fill, cot = fill[0], cot[0]
    vector = lambda v: v.astype(F32).reshape(1, -1)
    gain_a, shift_a, gain_b, shift_b = (vector(v) for v in (gain_one, shift_one, gain_two, shift_two))
    bias_qkv = vector(jnp.concatenate([b_q, jnp.zeros_like(b_q), b_v]))

    order = ffn ^ jnp.arange(n_ffn)
    line = Line()
    pairs = n_ffn == 2
    if pairs:
        split = "pairs"
        w_up, w_down, w_qkv = in_hbm(w_up, w_down, w_qkv)
        up_own, up_far, down_own, down_far = cut(sc, w_up, w_down)
        up_own = swap(up_own, "ffn", 1)
        b_other = swap(b_up, "ffn", 1)
        down_own = swap(down_own, "ffn", 1)
        up_far = swap(up_far, "ffn", 1)
        down_far = swap(down_far, "ffn", 1)
    else:
        split = "stack"
        ups = (jnp.take(lax.all_gather(w_up, "ffn"), order[1:], axis=0),)
        downs = (jnp.take(lax.all_gather(w_down, "ffn"), order[1:], axis=0),)
        b_other = jnp.take(lax.all_gather(b_up, "ffn"), order[1:], axis=0)

    x, x_keep, x_send, qkv = embed_qkv(sc, tokens, spots, fill, w_qkv, bias_qkv, n_seq)
    line.mark(qkv)
    if pairs:
        line.need(up_own, b_other)
        up_y, up_z = swap(line.put(up_own), "seq", 2), swap(line.put(up_own), "seq", 4)
    att, att_keep, att_send, logs = attend(sc, line.put(qkv), n_seq)
    line.mark(att)
    if pairs:
        up_near = stack(sc, *line.put(up_own, up_y, up_z))
        line.mark(up_near)
        line.need(down_own)
        down_y, down_z = swap(line.put(down_own), "seq", 2), swap(line.put(down_own), "seq", 4)
        up_near_other = swap(up_near, "seq", 1)
    hat, inv, low, n_keep, n_send = norm_one(sc, line.put(att), w_out, x, vector(b_out), gain_a, shift_a, n_seq)
    line.mark(low)
    if pairs:
        line.need(up_near_other, up_far)
    x_get = swap(line.put(x_send), "seq", 1)
    att_get = swap(line.put(att_send), "seq", 1)
    hid_own, slope_own, total = ffn_fwd(sc, line.put(low), vector(b_up), (w_up,), (w_down,), "own")
    line.mark(hid_own)
    if pairs:
        line.need(x_get, att_get, down_far)
        up_far, down_far = line.put(up_far)[None], line.put(down_far)[None]
        up_far_other, down_far_other = swap(up_far, "seq", 1), swap(down_far, "seq", 1)
        down_near = stack(sc, *line.put(down_own, down_y, down_z))
        line.mark(down_near)
        down_near_other = swap(down_near, "seq", 1)
        ups = (up_near, up_near_other, up_far, up_far_other)
        downs = (down_near, down_near_other, down_far, down_far_other)
    n_get = swap(line.put(n_send), "seq", 1)
    hid_own_get = swap(line.put(hid_own), "seq", 1)
    hid_oth, slope_oth, total = ffn_fwd(sc, line.put(low), vector(b_other), ups, downs, split, total)
    line.mark(hid_oth)
    line.need(n_get)
    hid_oth_get = swap(hid_oth, "seq", 1)

    output, g_two, g_down, d_keep, d_send, sums_two = norm_two(
        sc, line.put(total), hat, gain_a, shift_a, vector(b_down), gain_b, shift_b, spots, cot, n_seq
    )
    line.mark(g_down)
    line.need(hid_own_get, hid_oth_get)
    d_get = swap(d_send, "seq", 1)

    found_bits = bits_of(n_seq)
    seq_bits = [2] + found_bits[2:][::-1]
    x_step = ("ffn", 1)
    y_step = ("seq", 2)
    z_steps = [("seq", b) for b in found_bits[2:]]
    x_first = [("ffn", b) for b in bits_of(n_ffn)[::-1]] + z_steps + [y_step]
    z_axes = [(step, 2) for step in z_steps[::-1]]
    per = units // WIDE
    half = per // 2
    chunk = width // n_seq
    shards = lambda v, n, places: v.reshape(n, -1, places, chunk, WIDE)
    column = lambda start: (lambda b, sc: (0, start + b))
    d_left, n_left = (d_keep, d_get), (n_keep, n_get)

    def streams(found, blocks_a, blocks_b):
        a = [("block", blocks_a), (y_step, 2)] + z_axes
        b = [(x_step, 2), ("block", blocks_b)] + z_axes
        return Group(sc, line, [
            (a, found["keep_a"], found["send_a"], x_step),
            (b, found["keep_b"], found["send_b"], y_step),
        ])

    def big(left, own, own_get, oth, oth_get):
        left = (line.put(left[0]), left[1])
        found = weight_grad(sc, [left], [
            (oth, oth_get, half, column(0), 0, ("send_a",)),
            (own, own_get, per - half, column(half), 0, ("keep_b", "send_b")),
            (oth, oth_get, per - half, column(half), 0, ("keep_b", "send_b")),
            (own, own_get, half, column(0), 0, ("keep_a",)),
        ])
        line.mark(found["keep_a"])
        return streams(found, half, per - half)

    def big_whole(left, own, own_get, oth, oth_get):
        n_oth = oth.shape[1] // WIDE
        left = (line.put(left[0]), left[1])
        found = weight_grad(sc, [left], [
            (own, own_get, per, column(0), 0, ("all",)), (oth, oth_get, n_oth, column(0), 0, ("all",))
        ])["all"]
        line.mark(found)
        return Stream(line, seq_bits, x_first, whole=shards(found, n_ffn, n_seq // 2))

    def narrow(mine, other, first, count, matrix, names):
        per_row = mine.shape[-1] // WIDE
        each = per_row * (mine.shape[0] if mine.ndim == 3 else 1) // n_ffn

        def segment(shard):
            def index(b, sc):
                block = (shard ^ sc[1]) * each + first + b
                return (0, block) if mine.ndim == 2 else (block // per_row, 0, block % per_row)

            return (mine, other, count, index, matrix, names)

        return segment

    def narrow_whole(left, mine, other):
        per_row = mine.shape[-1] // WIDE
        blocks = per_row * (mine.shape[0] if mine.ndim == 3 else 1)
        index = (lambda b, sc: (0, b)) if mine.ndim == 2 else (lambda b, sc: (b // per_row, 0, b % per_row))
        whole = weight_grad(sc, [(line.put(left[0]), left[1])], [(mine, other, blocks, index, 0, ("all",))])["all"]
        line.mark(whole)
        share = blocks * WIDE // n_ffn
        whole = whole.reshape(blocks, n_seq // 2, chunk, WIDE)
        whole = jnp.transpose(whole, (1, 2, 0, 3)).reshape(n_seq // 2, chunk, n_ffn, share)
        whole = jnp.take(jnp.transpose(whole, (2, 0, 1, 3)), order, axis=0)[:, None]
        return Stream(line, seq_bits, x_first, whole=whole)

    ways = {} if not pairs else {"z": [(z_steps[0],), (z_steps[1],), (y_step, x_step)], "y": [(y_step, x_step), (z_steps[0],), (z_steps[1],)]}
    way_d, way_u = list(ways.get("z", ())), list(ways.get("z", ()))
    if pairs:
        held = in_hbm(*ups, *downs)
        ups, downs = held[:4], held[4:]
    columns = lambda count, first, target=0, turned=False: [
        (target, (first + n) * WIDE, turned) for n in range(count)
    ]
    if pairs:
        ops = {}

        def wg_d():
            ops["D"] = big(d_left, hid_own, hid_own_get, hid_oth, hid_oth_get)

        def ffn_back():
            gp_oth, gp_own, bs_oth, bs_own, total = ffn_both(
                sc, line.put(g_down), slope_oth, slope_own, ups, downs, w_up, w_down
            )
            line.mark(gp_own)
            ops["gp"] = (gp_own, swap(gp_own, "seq", 1), gp_oth, swap(gp_oth, "seq", 1))
            ops["bs"] = (bs_own, bs_oth)
            ops["total"] = total

        def norm_back_one():
            ops["one"] = norm_one_back(sc, line.put(g_two), ops["total"], hat, inv, gain_a, w_out)
            line.mark(ops["one"][2])
            ops["low"] = (ops["one"][1], swap(ops["one"][1], "seq", 1))

        def wg_u():
            line.need(ops["gp"][1], ops["gp"][3])
            ops["U"] = big(n_left, *ops["gp"])
            line.need(ops["low"][1])

        def back():
            g_qkv, sums_att = attend_back(sc, line.put(qkv), att, ops["one"][2], logs)
            line.mark(g_qkv)
            ops["qkv"] = (g_qkv, swap(g_qkv, "seq", 1))
            ops["sums_att"] = sums_att

        def wg_q():
            q = ops["qkv"]
            lefts = [(line.put(x_keep), x_get), (att_keep, att_get)]
            q_a = narrow(*q, 0, 2, 0, ("send_a",))
            q_b = narrow(*q, 2, 1, 0, ("keep_b", "send_b"))
            o_b = narrow(*ops["low"], 0, 1, 1, ("keep_b", "send_b"))
            ops["found"] = weight_grad(sc, lefts, [q_a(1), q_b(0), o_b(0), q_b(1), o_b(1)])
            line.mark(ops["found"]["keep_b"])

        def wg_q_rest():
            q_keep = narrow(*ops["qkv"], 0, 2, 0, ("keep_a",))
            found = dict(ops["found"])
            found.update(weight_grad(sc, [(line.put(x_keep), x_get)], [q_keep(0)]))
            line.mark(found["keep_a"])
            ops["Q"] = streams(found, 2, 2)

        def tokens_back():
            ops["tokens"] = token_grads(sc, line.put(ops["qkv"][0]), w_qkv, ops["one"][0], spots, slots)
            line.mark(ops["tokens"][0])

        def sums_start():
            bs_own, bs_oth = ops["bs"]
            ops["sums"] = pack(line.put(sc), sums_two, ops["one"][3], bs_own, bs_oth, ops["sums_att"])
            line.mark(ops["sums"])
            ops["sum_steps"] = [("seq", 1), ("seq", 2), ("ffn", 1)] + [("seq", b) for b in bits_of(n_seq)[2:]]
            sums_post()

        def sums_post():
            step = ops["sum_steps"].pop(0)
            ops["got"] = swap(line.put(ops["sums"]), *step)

        def sums_add():
            mine, got = line.put(ops["sums"], ops["got"])
            ops["sums"] = mine + got
            line.mark(ops["sums"])
            if ops["sum_steps"]:
                sums_post()

        def step_of(name, way, weight=0):
            return lambda: ops[name].advance(*way.pop(0), weight=weight)

        def end_d():
            ops["down"] = ops["D"].finish(
                [columns(half, 0, turned=True), columns(per - half, half, turned=True)], [(units, chunk)]
            )

        def end_u():
            ops["up"] = ops["U"].finish([columns(half, 0), columns(per - half, half)], [(chunk, units)])

        def end_q():
            ops["last"] = ops["Q"].finish(
                [columns(2, 0), columns(1, 2) + columns(1, 0, 1)], [(chunk, 3 * WIDE), (chunk, WIDE)]
            )

        way_q = [(y_step, x_step), (z_steps[0],), (z_steps[1],)]
        steps = {
            "gD": wg_d, "B": ffn_back, "N": norm_back_one, "gU": wg_u, "A": back, "G": wg_q, "H": wg_q_rest,
            "T": tokens_back, "P": sums_start, "S": sums_add, "D": step_of("D", way_d), "D!": step_of("D", way_d, 0.5), "U!": step_of("U", way_u, 1), "U": step_of("U", way_u),
            "Q": step_of("Q", way_q), "eD": end_d, "eU": end_u, "eQ": end_q,
        }
        for name in SEQUENCE:
            steps[name]()
        grad_tokens, grad_fill = ops["tokens"]
        (grad_down,), (grad_up,) = ops["down"], ops["up"]
        grad_qkv, grad_out = ops["last"]
        total_sums = ops["sums"].reshape(-1)
    else:
        down_a = big_whole(d_left, hid_own, hid_own_get, hid_oth, hid_oth_get)
        gp_oth, bs_oth, g_total = ffn_bwd(sc, line.put(g_down), slope_oth, ups, downs, split)
        line.mark(gp_oth)
        gp_oth_get = swap(gp_oth, "seq", 1)
        gp_own, bs_own, g_total = ffn_bwd(sc, line.put(g_down), slope_own, (w_up,), (w_down,), "own", g_total)
        line.mark(gp_own)
        gp_own_get = swap(gp_own, "seq", 1)
        g_one, g_att_low, g_att, sums_one = norm_one_back(sc, line.put(g_two), g_total, hat, inv, gain_a, w_out)
        line.mark(g_att)
        g_att_get = swap(g_att_low, "seq", 1)
        up_a = big_whole(n_left, gp_own, gp_own_get, gp_oth, gp_oth_get)
        g_qkv, sums_att = attend_back(sc, line.put(qkv), att, g_att, logs)
        line.mark(g_qkv)
        g_qkv_get = swap(g_qkv, "seq", 1)
        b_up_sums = jnp.concatenate([bs_own.reshape(1, units), bs_oth.reshape(n_ffn - 1, units)])
        b_up_sums = jnp.take(b_up_sums, order, axis=0).reshape(-1)
        sums = jnp.concatenate(
            [sums_two[:3].reshape(-1), sums_one[:3].reshape(-1), b_up_sums, sums_att.reshape(-1)]
        )
        grad_tokens, grad_fill = token_grads(sc, line.put(g_qkv), w_qkv, g_one, spots, slots)
        line.mark(grad_tokens)
        out = narrow_whole((att_keep, att_get), g_att_low, g_att_get)
        qkv_a = narrow_whole((x_keep, x_get), g_qkv, g_qkv_get)
        (*_, total_sums) = all_sum(line, sums, n_seq, n_ffn)
        grad_down, grad_up = columns_of(down_a.finish()).T, columns_of(up_a.finish())
        grad_out, grad_qkv = columns_of(out.finish()), columns_of(qkv_a.finish())
    hidden_units = n_ffn * units

    part = lambda v, n: v[n * width : (n + 1) * width]
    return (
        output,
        grad_tokens,
        grad_fill[None],
        grad_qkv,
        total_sums[6 * width + hidden_units : 7 * width + hidden_units],
        total_sums[7 * width + hidden_units : 8 * width + hidden_units],
        grad_out,
        part(total_sums, 5),
        part(total_sums, 3),
        part(total_sums, 4),
        grad_up,
        total_sums[6 * width : 6 * width + hidden_units],
        grad_down,
        part(total_sums, 2),
        part(total_sums, 0),
        part(total_sums, 1),
    )


def solution(mesh):
    rows = ("seq", "ffn")
    in_specs = (
        P(rows, None),
        P(rows, None),
        P(rows),
        P(rows, None, None),
        P(rows, None, None),
        P(),
        P(),
        P(),
        P(),
        P(),
        P(),
        P(),
        P(None, "ffn"),
        P("ffn"),
        P("ffn", None),
        P(),
        P(),
        P(),
    )
    out_specs = (
        P(rows, None),
        P(rows, None),
        P(rows, None, None),
        P("seq", "ffn"),
        P(),
        P(),
        P("seq", "ffn"),
        P(),
        P(),
        P(),
        P("seq", "ffn"),
        P(),
        P("ffn", "seq"),
        P(),
        P(),
        P(),
    )
    return jax.shard_map(on_device, mesh=mesh, in_specs=in_specs, out_specs=out_specs, check_vma=False)
```

```python
import functools

import jax
import jax.numpy as jnp
from jax import lax
from jax.experimental import pallas as pl
from jax.experimental.pallas import tpu as pltpu
from jax.sharding import PartitionSpec as P

H = 16
F32 = jnp.float32
LOW = jnp.bfloat16
epsilon = 1e-12
LOG2E = 1.4426950408889634
NT = (((1,), (1,)), ((), ()))
WIDE = 512
SEQUENCE = ("gD", "B", "N", "D!", "gU", "A", "P", "D", "S", "U!", "S", "G", "S", "H", "D", "T", "Q", "U", "S", "Q", "eD", "U", "S", "Q", "eU", "eQ")
STEP = 3 * 10**10


def mm(left, right):
    return jnp.dot(left, right, preferred_element_type=F32)


def mm_nt(left, right):
    return lax.dot_general(left, right, NT, preferred_element_type=F32)


def call(body, grid, in_specs, out_specs, out_shape, scratch=(), prefetch=1, mib=32, weight=0):
    return pl.pallas_call(
        body,
        grid_spec=pltpu.PrefetchScalarGridSpec(
            num_scalar_prefetch=prefetch,
            grid=grid,
            in_specs=in_specs,
            out_specs=out_specs,
            scratch_shapes=list(scratch),
        ),
        out_shape=out_shape,
        compiler_params=pltpu.CompilerParams(
            dimension_semantics=("arbitrary",) * len(grid), vmem_limit_bytes=mib << 20
        ),
        cost_estimate=pl.CostEstimate(flops=int(1 + weight * STEP), bytes_accessed=1, transcendentals=0),
    )


def far(dims, dtype):
    return pltpu.HBM(dims, dtype)


def in_hbm(*values):
    return [pltpu.with_memory_space_constraint(value, pltpu.HBM) for value in values]


def spec(shape, index):
    return pl.BlockSpec(shape, index)


def shape(dims, dtype):
    return jax.ShapeDtypeStruct(dims, dtype)


def one_hot_rows(sc, spots, first, rows):
    slots = spots.shape[1]
    place = lax.broadcasted_iota(jnp.int32, (rows, slots), 0) + first
    slot = lax.broadcasted_iota(jnp.int32, (rows, slots), 1)
    hit = (place == spots) & (slot < sc[2])
    return jnp.where(hit, 1.0, 0.0)


def store_turned(sc, value, keep_ref, send_ref, first_column, chunk):
    columns = value.shape[1]
    for block in range(0, columns, 128):
        turned = jnp.transpose(value[:, block : block + 128]).astype(LOW)
        for part in range(0, 128, chunk):
            place = ((first_column + block + part) // chunk) ^ sc[0]
            piece = turned[part : part + chunk]
            at = ((place // 2) % 2) * (keep_ref.shape[0] // 2) + place // 4

            @pl.when(place % 2 == 0)
            def _():
                keep_ref[at] = piece

            @pl.when(place % 2 == 1)
            def _():
                send_ref[at] = piece


def qkv_body(chunk, sc, tokens, spots, fill, w, bias, x_out, keep, send, qkv):
    @pl.when(pl.program_id(0) == 0)
    def _():
        placed = one_hot_rows(sc, spots[...], 0, tokens.shape[0])
        kept = 1.0 - jnp.sum(placed, axis=1, keepdims=True)
        x = tokens[...].astype(F32) * kept + mm(placed.astype(LOW), fill[...])
        x_out[...] = x.astype(LOW)
        store_turned(sc, x, keep, send, 0, chunk)

    qkv[...] = (mm(x_out[...], w[...]) + bias[...]).astype(LOW)


def embed_qkv(sc, tokens, spots, fill, w_qkv, bias, n_seq):
    rows, width = tokens.shape
    out = w_qkv.shape[1]
    block = 512
    chunk = width // n_seq
    turned = (n_seq // 2, chunk, rows)
    whole = lambda j, sc: (0, 0)
    return call(
        functools.partial(qkv_body, chunk),
        (out // block,),
        [
            spec((rows, width), whole),
            spec(spots.shape, whole),
            spec(fill.shape, whole),
            spec((width, block), lambda j, sc: (0, j)),
            spec((1, block), lambda j, sc: (0, j)),
        ],
        [
            spec((rows, width), whole),
            spec(turned, lambda j, sc: (0, 0, 0)),
            spec(turned, lambda j, sc: (0, 0, 0)),
            spec((rows, block), lambda j, sc: (0, j)),
        ],
        [shape((rows, width), LOW), far(turned, LOW), far(turned, LOW), shape((rows, out), LOW)],
        weight=1,
    )(sc, tokens, spots, fill, w_qkv, bias)


def head_masks(width, size, factor):
    lane = lax.broadcasted_iota(jnp.int32, (1, width), 1)
    return [jnp.where(lane // size == n, factor, 0.0).astype(LOW) for n in range(width // size)]


def attend_body(chunk, size, scale, sc, q, k, v, att, keep, send, logs):
    rows, width = q.shape
    pair = 2 * size
    masks = head_masks(pair, size, scale)
    lane = lax.broadcasted_iota(jnp.int32, (1, pair), 1)
    place_first = pl.program_id(0) * width
    for first in range(0, width, pair):
        columns = slice(first, first + pair)
        mixed, stats = [], []
        for mask in masks:
            scores = mm_nt(q[:, columns] * mask, k[:, columns])
            peak = jnp.max(scores, axis=1, keepdims=True) * LOG2E
            expo = jnp.exp2(scores * LOG2E - peak)
            total = jnp.sum(expo, axis=1, keepdims=True)
            mixed.append(mm(expo.astype(LOW), v[:, columns]) * (1.0 / total))
            stats.append(peak + jnp.log2(total))
        both = jnp.where(lane < size, mixed[0], mixed[1])
        att[:, columns] = both.astype(LOW)
        logs[:, columns] = jnp.where(lane < size, stats[0], stats[1])
        store_turned(sc, both, keep, send, place_first + first, chunk)


def attend(sc, qkv, n_seq):
    rows = qkv.shape[0]
    width = qkv.shape[1] // 3
    size = width // H
    block = 4 * size
    steps = width // block
    chunk = width // n_seq
    turned = (n_seq // 2, chunk, rows)
    whole = lambda j, sc: (0, 0, 0)
    tile = spec((rows, block), lambda j, sc: (0, j))
    return call(
        functools.partial(attend_body, chunk, size, size ** (-0.5)),
        (steps,),
        [
            tile,
            spec((rows, block), lambda j, sc: (0, steps + j)),
            spec((rows, block), lambda j, sc: (0, 2 * steps + j)),
        ],
        [tile, spec(turned, whole), spec(turned, whole), tile],
        [shape((rows, width), LOW), far(turned, LOW), far(turned, LOW), shape((rows, width), F32)],
        weight=1,
    )(sc, qkv, qkv, qkv)


def norm_one_body(chunk, sc, att, w, x, b, gain, shift, hat, inv, low, keep, send):
    value = x[...].astype(F32) + mm(att[...], w[...]) + b[...]
    centre = value - jnp.mean(value, axis=-1, keepdims=True)
    spread = jnp.mean(centre * centre, axis=-1, keepdims=True)
    inverse = lax.rsqrt(spread + epsilon)
    scaled = centre * inverse
    hat[...] = scaled
    inv[...] = inverse
    normed = scaled * gain[...] + shift[...]
    low[...] = normed.astype(LOW)
    store_turned(sc, normed, keep, send, 0, chunk)


def norm_one(sc, att, w_out, x, b_out, gain, shift, n_seq):
    rows, width = x.shape
    block = 512
    chunk = width // n_seq
    turned = (n_seq // 2, chunk, rows)
    row = lambda i, sc: (i, 0)
    whole = lambda i, sc: (0, 0)
    vector = spec((1, width), whole)
    return call(
        functools.partial(norm_one_body, chunk),
        (rows // block,),
        [spec((block, width), row), spec((width, width), whole), spec((block, width), row), vector, vector, vector],
        [
            spec((block, width), row),
            spec((block, 1), row),
            spec((block, width), row),
            spec((n_seq // 2, chunk, block), lambda i, sc: (0, 0, i)),
            spec((n_seq // 2, chunk, block), lambda i, sc: (0, 0, i)),
        ],
        [
            far((rows, width), F32),
            shape((rows, 1), F32),
            shape((rows, width), LOW),
            far(turned, LOW),
            far(turned, LOW),
        ],
        weight=1,
    )(sc, att, w_out, x, b_out, gain, shift)


TAIL = tuple(0.5 * c for c in (0.254829592, -0.284496736, 1.421413741, -1.453152027, 1.061405429))
TAIL_P = 0.3275911 * 0.7071067811865476


def gelu_both(x):
    t = 1.0 / (1.0 + TAIL_P * jnp.abs(x))
    bell = jnp.exp2(x * x * (-0.5 * LOG2E))
    poly = TAIL[4]
    for c in TAIL[3::-1]:
        poly = poly * t + c
    tail = poly * t * bell
    mass = jnp.where(x < 0.0, tail, 1.0 - tail)
    return x * mass, mass + x * bell * 0.3989422804014327


def ffn_specs(split, width, part, units):
    if split == "own":
        wide = min(2 * WIDE, units)
        ups = [spec((width, wide), lambda j, sc: (0, j))]
        downs = [spec((wide, width), lambda j, sc: (j, 0))]
        return ups, downs, wide
    if split == "stack":
        ups = [spec((None, width, part), lambda j, sc: (j, 0, 0))]
        downs = [spec((None, part, width), lambda j, sc: (j, 0, 0))]
        return ups, downs, part
    near = lambda j, sc: (jnp.minimum(j, 2), 0, 0)
    far = lambda j, sc: (0, 0, 0)
    ups = [spec((None, width, part), at) for at in (near, near, far, far)]
    downs = [spec((None, part, width), at) for at in (near, near, far, far)]
    return ups, downs, part


def column_block(split):
    if split == "pairs":
        return lambda j, sc: (0, j ^ ((sc[0] // 2) % 4))
    return lambda j, sc: (0, j)


def for_pieces(split, size, sc, ups, downs, work):
    if split != "pairs":
        work([(ups[0], downs[0], 0)])
        return
    core = sc[0] % 2
    places = [pl.multiple_of(core * size, size), pl.multiple_of((1 - core) * size, size)]
    step = pl.program_id(0)
    pl.when(step < 3)(lambda: work(list(zip(ups[:2], downs[:2], places))))
    pl.when(step == 3)(lambda: work(list(zip(ups[2:], downs[2:], places))))


def ffn_fwd_body(split, size, n, first, sc, *refs):
    low, bias = refs[:2]
    ups, downs = refs[2 : 2 + n], refs[2 + n : 2 + 2 * n]
    rest = refs[2 + 2 * n :]
    start = None
    if not first:
        start, rest = rest[0], rest[1:]
    hidden, slope, total = rest
    @pl.when(pl.program_id(0) == 0)
    def _():
        total[...] = jnp.zeros_like(total) if first else start[...]

    def work(pieces):
        mixed = None
        for up, down, offset in pieces:
            columns = pl.ds(offset, size)
            pre = mm(low[...], up[...]) + bias[:, columns]
            act, grad = gelu_both(pre)
            act = act.astype(LOW)
            hidden[:, columns] = act
            slope[:, columns] = grad.astype(LOW)
            product = mm(act, down[...])
            mixed = product if mixed is None else mixed + product
        total[...] += mixed

    for_pieces(split, size, sc, ups, downs, work)


def ffn_fwd(sc, low, bias, ups, downs, split, start=None):
    rows, width = low.shape
    units = bias.shape[1]
    part = ups[0].shape[-1]
    up_specs, down_specs, size = ffn_specs(split, width, part, units)
    step = 2 * part if split == "pairs" else size
    whole = lambda j, sc: (0, 0)
    column = column_block(split)
    total = spec((rows, width), whole)
    first = start is None
    return call(
        functools.partial(ffn_fwd_body, split, size, len(ups), first),
        (units // step,),
        [total, spec((1, step), column)] + up_specs + down_specs + ([] if first else [total]),
        [spec((rows, step), column), spec((rows, step), column), total],
        [shape((rows, units), LOW), shape((rows, units), LOW), shape((rows, width), F32)],
        weight=1,
    )(sc, low, bias, *ups, *downs, *([] if first else [start]))


def ffn_bwd_body(split, size, n, first, sc, *refs):
    low, slope = refs[:2]
    ups, downs = refs[2 : 2 + n], refs[2 + n : 2 + 2 * n]
    rest = refs[2 + 2 * n :]
    start = None
    if not first:
        start, rest = rest[0], rest[1:]
    g_low, sums, total = rest
    @pl.when(pl.program_id(0) == 0)
    def _():
        total[...] = jnp.zeros_like(total) if first else start[...]

    def work(pieces):
        mixed = None
        for up, down, offset in pieces:
            columns = pl.ds(offset, size)
            g_pre = mm_nt(low[...], down[...]) * slope[:, columns].astype(F32)
            sums[:, columns] = jnp.sum(g_pre, axis=0, keepdims=True)
            rounded = g_pre.astype(LOW)
            g_low[:, columns] = rounded
            product = mm_nt(rounded, up[...])
            mixed = product if mixed is None else mixed + product
        total[...] += mixed

    for_pieces(split, size, sc, ups, downs, work)


def ffn_bwd(sc, low, slope, ups, downs, split, start=None):
    rows, width = low.shape
    units = slope.shape[1]
    part = ups[0].shape[-1]
    up_specs, down_specs, size = ffn_specs(split, width, part, units)
    step = 2 * part if split == "pairs" else size
    whole = lambda j, sc: (0, 0)
    column = column_block(split)
    total = spec((rows, width), whole)
    first = start is None
    return call(
        functools.partial(ffn_bwd_body, split, size, len(ups), first),
        (units // step,),
        [total, spec((rows, step), column)] + up_specs + down_specs + ([] if first else [total]),
        [spec((rows, step), column), spec((1, step), column), total],
        [shape((rows, units), LOW), shape((1, units), F32), shape((rows, width), F32)],
    )(sc, low, slope, *ups, *downs, *([] if first else [start]))


def ffn_both_body(size, sc, low, slope_oth, slope_own, *refs):
    ups, downs, (up, down) = refs[:4], refs[4:8], refs[8:10]
    g_oth, g_own, sums_oth, sums_own, total = refs[10:]
    core = sc[0] % 2
    places = [pl.multiple_of(core * size, size), pl.multiple_of((1 - core) * size, size)]
    step = pl.program_id(0)

    def work(pieces, slope, g_low, sums):
        mixed = None
        for up_ref, down_ref, offset, span in pieces:
            columns = pl.ds(offset, span)
            g_pre = mm_nt(low[...], down_ref[...]) * slope[:, columns].astype(F32)
            sums[:, columns] = jnp.sum(g_pre, axis=0, keepdims=True)
            rounded = g_pre.astype(LOW)
            g_low[:, columns] = rounded
            product = mm_nt(rounded, up_ref[...])
            mixed = product if mixed is None else mixed + product

        @pl.when(step == 0)
        def _():
            total[...] = mixed

        @pl.when(step > 0)
        def _():
            total[...] += mixed

    other = lambda group: [(u, d, place, size) for u, d, place in zip(ups[group], downs[group], places)]
    pl.when(step < 3)(lambda: work(other(slice(0, 2)), slope_oth, g_oth, sums_oth))
    pl.when(step == 3)(lambda: work(other(slice(2, 4)), slope_oth, g_oth, sums_oth))
    pl.when(step > 3)(lambda: work([(up, down, 0, down.shape[0])], slope_own, g_own, sums_own))


def ffn_both(sc, low, slope_oth, slope_own, ups, downs, up, down):
    rows, width = low.shape
    units = slope_own.shape[1]
    part = ups[0].shape[-1]
    wide = 2 * part
    own_wide = min(2 * WIDE, units)
    steps = units // own_wide
    whole = lambda j, sc: (0, 0)
    near = lambda j, sc: (jnp.minimum(j, 2), 0, 0)
    away = lambda j, sc: (0, 0, 0)
    oth = lambda j, sc: (0, jnp.minimum(j, 3) ^ ((sc[0] // 2) % 4))
    own = lambda j, sc: (0, jnp.maximum(j - 4, 0))
    own_row = lambda j, sc: (jnp.maximum(j - 4, 0), 0)
    return call(
        functools.partial(ffn_both_body, part),
        (4 + steps,),
        [spec((rows, width), whole), spec((rows, wide), oth), spec((rows, own_wide), own)]
        + [spec((None, width, part), at) for at in (near, near, away, away)]
        + [spec((None, part, width), at) for at in (near, near, away, away)]
        + [spec((width, own_wide), own), spec((own_wide, width), own_row)],
        [
            spec((rows, wide), oth),
            spec((rows, own_wide), own),
            spec((1, wide), oth),
            spec((1, own_wide), own),
            spec((rows, width), whole),
        ],
        [far((rows, units), LOW), far((rows, units), LOW), shape((1, units), F32), shape((1, units), F32), shape((rows, width), F32)],
        weight=0,
    )(sc, low, slope_oth, slope_own, *ups, *downs, up, down)


def norm_back(hat, inverse, gain, grad):
    inner = grad * gain
    mean = jnp.mean(inner, axis=-1, keepdims=True)
    along = jnp.mean(inner * hat, axis=-1, keepdims=True)
    return inverse * (inner - mean - hat * along)


def add_sums(sums, rows):
    @pl.when(pl.program_id(0) == 0)
    def _():
        sums[...] = jnp.zeros_like(sums)

    for n, value in enumerate(rows):
        sums[n : n + 1, :] += jnp.sum(value, axis=0, keepdims=True)


def norm_two_body(chunk, sc, mixed, hat_one, gain_one, shift_one, b_down, gain, shift, spots, cot, out, grad, low, keep, send, sums):
    rows = mixed.shape[0]
    value = hat_one[...] * gain_one[...] + shift_one[...] + mixed[...] + b_down[...]
    centre = value - jnp.mean(value, axis=-1, keepdims=True)
    spread = jnp.mean(centre * centre, axis=-1, keepdims=True)
    inverse = lax.rsqrt(spread + epsilon)
    hat = centre * inverse
    out[...] = (hat * gain[...] + shift[...]).astype(LOW)
    placed = one_hot_rows(sc, spots[...], pl.program_id(0) * rows, rows)
    out_grad = mm(placed.astype(LOW), cot[...])
    result = norm_back(hat, inverse, gain[...], out_grad)
    grad[...] = result
    low[...] = result.astype(LOW)
    store_turned(sc, result, keep, send, 0, chunk)
    add_sums(sums, (out_grad * hat, out_grad, result))


def norm_two(sc, mixed, hat_one, gain_one, shift_one, b_down, gain, shift, spots, cot, n_seq):
    rows, width = mixed.shape
    block = 512
    chunk = width // n_seq
    turned = (n_seq // 2, chunk, rows)
    row = lambda i, sc: (i, 0)
    whole = lambda i, sc: (0, 0)
    vector = spec((1, width), whole)
    tile = spec((block, width), row)
    return call(
        functools.partial(norm_two_body, chunk),
        (rows // block,),
        [tile, tile, vector, vector, vector, vector, vector, spec(spots.shape, whole), spec(cot.shape, whole)],
        [
            tile,
            tile,
            tile,
            spec((n_seq // 2, chunk, block), lambda i, sc: (0, 0, i)),
            spec((n_seq // 2, chunk, block), lambda i, sc: (0, 0, i)),
            spec((8, width), whole),
        ],
        [
            shape((rows, width), LOW),
            shape((rows, width), F32),
            shape((rows, width), LOW),
            far(turned, LOW),
            far(turned, LOW),
            shape((8, width), F32),
        ],
        weight=1,
    )(sc, mixed, hat_one, gain_one, shift_one, b_down, gain, shift, spots, cot)


def norm_one_back_body(sc, grad_two, ffn, hat, inv, gain, w, grad, low, g_att, sums):
    g_normed = grad_two[...] + ffn[...]
    result = norm_back(hat[...], inv[...], gain[...], g_normed)
    grad[...] = result
    rounded = result.astype(LOW)
    low[...] = rounded
    g_att[...] = mm_nt(rounded, w[...]).astype(LOW)
    add_sums(sums, (g_normed * hat[...], g_normed, result))


def norm_one_back(sc, grad_two, ffn, hat, inv, gain, w_out):
    rows, width = hat.shape
    block = 512
    row = lambda i, sc: (i, 0)
    whole = lambda i, sc: (0, 0)
    tile = spec((block, width), row)
    return call(
        norm_one_back_body,
        (rows // block,),
        [tile, tile, tile, spec((block, 1), row), spec((1, width), whole), spec((width, width), whole)],
        [tile, tile, tile, spec((8, width), whole)],
        [shape((rows, width), F32), shape((rows, width), LOW), shape((rows, width), LOW), shape((8, width), F32)],
        weight=0,
    )(sc, grad_two, ffn, hat, inv, gain, w_out)


def mm_tn(left, right):
    return lax.dot_general(left, right, (((0,), (0,)), ((), ())), preferred_element_type=F32)


def attend_back_body(size, scale, sc, q, k, v, att, g_att, logs, g_qkv, sums):
    rows, width = q.shape
    pair = 2 * size
    ones = head_masks(pair, size, 1.0)
    halves = head_masks(pair, size, scale)
    lane = lax.broadcasted_iota(jnp.int32, (1, pair), 1)
    for first in range(0, width, pair):
        columns = slice(first, first + pair)
        q_pair, k_pair, v_pair, g_pair = q[:, columns], k[:, columns], v[:, columns], g_att[:, columns]
        q_scaled = q_pair * jnp.asarray(scale, LOW)
        k_scaled = k_pair * jnp.asarray(scale, LOW)
        product = att[:, columns].astype(F32) * g_pair.astype(F32)
        log_pair = logs[:, columns]
        turned_v, turned_k, g_q = [], [], []
        for n in range(2):
            rows_of = slice(n * size, (n + 1) * size)
            scores = mm_nt(q_pair * halves[n], k_pair)
            probs = jnp.exp2(scores * LOG2E - log_pair[:, n * size : n * size + 1])
            g_probs = mm_nt(g_pair * ones[n], v_pair)
            level = jnp.sum(jnp.where(lane // size == n, product, 0.0), axis=1, keepdims=True)
            g_scores = (probs * (g_probs - level)).astype(LOW)
            turned_v.append(mm_tn(g_pair, probs.astype(LOW))[rows_of])
            turned_k.append(mm_tn(q_scaled, g_scores)[rows_of])
            g_q.append(mm(g_scores, k_scaled))
        query = jnp.where(lane < size, g_q[0], g_q[1]).astype(LOW)
        value = jnp.transpose(jnp.concatenate(turned_v, axis=0)).astype(LOW)
        g_qkv[0, :, columns] = query
        g_qkv[1, :, columns] = jnp.transpose(jnp.concatenate(turned_k, axis=0)).astype(LOW)
        g_qkv[2, :, columns] = value
        sums[0:1, columns] = jnp.sum(query.astype(F32), axis=0, keepdims=True)
        sums[1:2, columns] = jnp.sum(value.astype(F32), axis=0, keepdims=True)


def attend_back(sc, qkv, att, g_att, logs):
    rows, width = att.shape
    size = width // H
    block = 4 * size
    steps = width // block
    tile = spec((rows, block), lambda j, sc: (0, j))
    return call(
        functools.partial(attend_back_body, size, size ** (-0.5)),
        (steps,),
        [
            tile,
            spec((rows, block), lambda j, sc: (0, steps + j)),
            spec((rows, block), lambda j, sc: (0, 2 * steps + j)),
            tile,
            tile,
            tile,
        ],
        [spec((3, rows, block), lambda j, sc: (0, 0, j)), spec((2, block), lambda j, sc: (0, j))],
        [far((3, rows, width), LOW), shape((2, width), F32)],
        weight=0,
    )(sc, qkv, qkv, qkv, att, g_att, logs)


def token_grads_body(sc, g_qkv, w, base, spots, spots_column, tokens_out, fill_out):
    rows = base.shape[0]
    width = g_qkv.shape[2]
    grad = base[...]
    for n in range(3):
        grad = grad + mm_nt(g_qkv[n], w[:, n * width : (n + 1) * width])
    placed = one_hot_rows(sc, spots[...], 0, rows)
    kept = 1.0 - jnp.sum(placed, axis=1, keepdims=True)
    tokens_out[...] = (grad * kept).astype(LOW)
    slots = spots_column.shape[0]
    place = lax.broadcasted_iota(jnp.int32, (slots, rows), 1)
    slot = lax.broadcasted_iota(jnp.int32, (slots, rows), 0)
    hit = (place == spots_column[...]) & (slot < sc[2])
    fill_out[...] = mm(jnp.where(hit, 1.0, 0.0).astype(LOW), grad.astype(LOW)).astype(LOW)


def token_grads(sc, g_qkv, w_qkv, base, spots, slots):
    rows, width = base.shape
    block = 512
    column = lambda i, sc: (0, i)
    whole = lambda i, sc: (0, 0)
    tile = spec((rows, block), column)
    return call(
        token_grads_body,
        (width // block,),
        [
            spec(g_qkv.shape, lambda i, sc: (0, 0, 0)),
            spec((block, w_qkv.shape[1]), lambda i, sc: (i, 0)),
            tile,
            spec(spots.shape, whole),
            spec((slots, 1), whole),
        ],
        [tile, spec((slots, block), column)],
        [shape((rows, width), LOW), shape((slots, width), LOW)],
        weight=0.35,
    )(sc, g_qkv, w_qkv, base, spots, spots.reshape(slots, 1))


def weight_body(plan, lefts, sc, *refs):
    left_refs, refs = refs[: 2 * lefts], refs[2 * lefts :]
    ins, outs = refs[: 2 * len(plan)], refs[2 * len(plan) :]
    step = pl.program_id(0)
    first = 0
    for n, (count, matrix, targets) in enumerate(plan):
        left, left_other = left_refs[2 * matrix : 2 * matrix + 2]
        mine, other = ins[2 * n], ins[2 * n + 1]

        def work(left=left, left_other=left_other, mine=mine, other=other, targets=targets):
            places, _, depth = left.shape
            rows_of = lambda ref: ref[...].reshape(-1, depth)
            total = mm(rows_of(left), mine[...]) + mm(rows_of(left_other), other[...])
            total = total.astype(LOW).reshape(places, -1, total.shape[-1])
            share = places // len(targets)
            for block in range(total.shape[-1] // WIDE):
                columns = total[:, :, block * WIDE : (block + 1) * WIDE]
                for part, target in enumerate(targets):
                    outs[target][block * share : (block + 1) * share] = columns[part * share : (part + 1) * share]

        if len(plan) == 1:
            work()
        else:
            pl.when((step >= first) & (step < first + count))(work)
        first += count


def weight_grad(sc, lefts, segments, group=1):
    places, chunk, depth = lefts[0][0].shape
    left_spec = spec((places, chunk, depth), lambda j, sc: (0, 0, 0))
    in_specs = [left_spec] * (2 * len(lefts))
    operands = [value for pair in lefts for value in pair]
    spans, plan, first = {}, [], 0
    for mine, other, count, index, matrix, names in segments:
        def at(j, sc, first=first, count=count, index=index):
            return index(jnp.clip(j - first, 0, count - 1), sc)

        block = (depth, group * WIDE) if mine.ndim == 2 else (None, depth, group * WIDE)
        in_specs += [spec(block, at), spec(block, at)]
        operands += [mine, other]
        for name in names:
            begin = spans.setdefault(name, [first, first, places // len(names)])
            begin[1] = first + count
        first += count
    order = list(spans)
    for _, _, count, _, matrix, names in segments:
        plan.append((count, matrix, tuple(order.index(name) for name in names)))
    out_specs, out_shapes = [], []
    for begin, end, kept in spans.values():
        at = lambda j, sc, begin=begin, end=end: (jnp.clip(j, begin, end - 1) - begin, 0, 0)
        out_specs.append(spec((group * kept, chunk, WIDE), at))
        out_shapes.append(far(((end - begin) * group * kept, chunk, WIDE), LOW))
    found = call(
        functools.partial(weight_body, tuple(plan), len(lefts)),
        (first,),
        in_specs,
        out_specs,
        out_shapes,
        weight=0,
    )(sc, *operands)
    return dict(zip(order, found))


def add_body(count, plan, sc, *refs):
    outs = refs[2 * count :]
    for source, start, (outer, inner), target, place in plan:
        span = pl.ds(start, outer * 2 * inner)
        total = refs[2 * source][span].astype(F32) + refs[2 * source + 1][span].astype(F32)
        total = total.astype(LOW).reshape((outer, 2, inner) + total.shape[1:])
        for half in range(2):
            part = total[:, half]
            outs[2 * target + half][pl.ds(place, outer * inner)] = part.reshape((outer * inner,) + part.shape[2:])


def add_halves(sc, arrays, plan, sizes, weight):
    tile = WIDE // 2
    chunk = arrays[0][0].shape[1]
    column = lambda j, sc: (0, 0, j)
    operands = [value for pair in arrays for value in pair]
    found = call(
        functools.partial(add_body, len(arrays), tuple(plan)),
        (WIDE // tile,),
        [spec(value.shape[:2] + (tile,), column) for value in operands],
        [spec((size, chunk, tile), column) for size in sizes for _ in range(2)],
        [far((size, chunk, WIDE), LOW) for size in sizes for _ in range(2)],
        weight=weight,
    )(sc, *operands)
    return [(found[2 * n], found[2 * n + 1]) for n in range(len(sizes))]


def last_body(count, plan, sc, *refs):
    for source, place, target, at, turned in plan:
        total = refs[2 * source][place].astype(F32) + refs[2 * source + 1][place].astype(F32)
        out = refs[2 * count + target]
        if turned:
            out[at : at + WIDE, :] = jnp.transpose(total)
        else:
            out[:, at : at + WIDE] = total


def add_last(sc, arrays, plan, outs):
    whole = lambda n: (lambda j, sc: (0,) * n)
    operands = [value for pair in arrays for value in pair]
    return call(
        functools.partial(last_body, len(arrays), tuple(plan)),
        (1,),
        [spec(value.shape, whole(3)) for value in operands],
        [spec(dims, whole(2)) for dims in outs],
        [shape(dims, F32) for dims in outs],
    )(sc, *operands)


def stack_body(sc, *refs):
    out = refs[-1]
    for n, ref in enumerate(refs[:-1]):
        out[n] = ref[...]


def stack(sc, *values):
    rows, columns = values[0].shape
    steps = 2
    return call(
        stack_body,
        (steps,),
        [spec((rows // steps, columns), lambda j, sc: (j, 0))] * len(values),
        spec((len(values), rows // steps, columns), lambda j, sc: (0, j, 0)),
        far((len(values),) + values[0].shape, LOW),
        weight=1,
    )(sc, *values)


def swap(value, axis, bit):
    size = lax.axis_size(axis)
    return lax.ppermute(value, axis, [(n, n ^ bit) for n in range(size)])


def halves(value, bits, step):
    shards, blocks, places, chunk, wide = value.shape
    axis, bit = step
    if axis == "ffn":
        return value[: shards // 2], value[shards // 2 :], bits
    at = bits.index(bit)
    low = 1 << (len(bits) - 1 - at)
    parts = value.reshape(shards, blocks, places // (2 * low), 2, low, chunk, wide)
    dims = (shards, blocks, places // 2, chunk, wide)
    return (
        parts[:, :, :, 0].reshape(dims),
        parts[:, :, :, 1].reshape(dims),
        bits[:at] + bits[at + 1 :],
    )


class Line:
    def __init__(self):
        self.last = ()

    def put(self, *values):
        if self.last:
            values = lax.optimization_barrier(self.last + values)[len(self.last) :]
        return values if len(values) > 1 else values[0]

    def mark(self, value):
        self.last = (value,)

    def need(self, *values):
        self.last += values


class Stream:
    def __init__(self, line, bits, steps, whole=None, keep=None, send=None):
        self.line, self.bits, self.steps = line, list(bits), list(steps)
        if keep is None:
            keep, send, self.bits = halves(whole, self.bits, self.steps[0])
        elif self.steps[0][0] == "seq":
            self.bits.remove(self.steps[0][1])
        self.post(keep, send)

    def post(self, keep, send):
        self.keep = keep
        self.got = swap(send, *self.steps.pop(0))

    def advance(self):
        keep, got = self.line.put(self.keep, self.got)
        if self.steps:
            step = self.steps[0]
            keep_a, send_a, left = halves(keep, self.bits, step)
            keep_b, send_b, left = halves(got, self.bits, step)
            self.bits = left
            add = lambda a, b: (a.astype(F32) + b.astype(F32)).astype(LOW)
            send = add(send_a, send_b)
            keep = add(keep_a, keep_b)
            self.line.mark(keep)
            self.post(keep, send)
            return None
        total = keep.astype(F32) + got.astype(F32)
        self.line.mark(total)
        return total

    def finish(self):
        while True:
            total = self.advance()
            if total is not None:
                return total


class Group:
    def __init__(self, sc, line, parts):
        self.sc, self.line = sc, line
        self.arrays = []
        self.parts = []
        for n, (axes, keep, send, step) in enumerate(parts):
            self.arrays.append((keep, swap(send, *step)))
            self.parts.append((n, 0, list(axes)))

    def tied(self):
        flat = self.line.put(*[value for pair in self.arrays for value in pair])
        return [(flat[2 * n], flat[2 * n + 1]) for n in range(len(self.arrays))]

    def advance(self, *steps, weight=0):
        steps = steps * len(self.parts) if len(steps) == 1 else steps
        order = list(dict.fromkeys(steps))
        plan, sizes, parts = [], [0] * len(order), []
        for (array, start, axes), step in zip(self.parts, steps):
            at = [name for name, _ in axes].index(step)
            outer = inner = 1
            for _, size in axes[:at]:
                outer *= size
            for _, size in axes[at + 1 :]:
                inner *= size
            target = order.index(step)
            plan.append((array, start, (outer, inner), target, sizes[target]))
            parts.append((target, sizes[target], axes[:at] + axes[at + 1 :]))
            sizes[target] += outer * inner
        found = add_halves(self.sc, self.tied(), plan, sizes, weight)
        self.line.mark(found[0][0])
        self.arrays = [(keep, swap(send, *step)) for (keep, send), step in zip(found, order)]
        self.parts = parts

    def finish(self, targets, outs):
        plan = []
        for (array, start, _), places in zip(self.parts, targets):
            for n, place in enumerate(places):
                plan.append((array, start + n) + place)
        found = add_last(self.sc, self.tied(), plan, outs)
        self.line.mark(found[0])
        return found


def pack_body(sc, two, one, own, other, att, out):
    out[...] = jnp.zeros_like(out)
    out[0:3, :] = two[0:3, :]
    out[3:6, :] = one[0:3, :]
    width = out.shape[1]
    count = own.shape[1] // width
    for n in range(count):
        columns = slice(n * width, (n + 1) * width)
        first = sc[1] == 0
        out[6 + n : 7 + n, :] = jnp.where(first, own[:, columns], other[:, columns])
        out[6 + count + n : 7 + count + n, :] = jnp.where(first, other[:, columns], own[:, columns])
    out[6 + 2 * count : 8 + 2 * count, :] = att[...]


def pack(sc, *values):
    width = values[0].shape[1]
    rows = 8 + 2 * values[2].shape[1] // width
    rows += -rows % 8
    whole = lambda j, sc: (0, 0)
    return call(
        pack_body,
        (1,),
        [spec(v.shape, whole) for v in values],
        spec((rows, width), whole),
        far((rows, width), F32),
        weight=0,
    )(sc, *values)


def cut_body(sc, *refs):
    for ref, out in zip(refs[:4], refs[4:]):
        out[...] = ref[...]


def cut(sc, w_up, w_down):
    width, units = w_up.shape
    part = units // 8
    steps = 2
    place = lambda sc, away: (((sc[0] // 2) % 4) ^ away) * 2 + sc[0] % 2
    ups = [spec((width // steps, part), lambda j, sc, n=n: (j, place(sc, n))) for n in (0, 3)]
    downs = [spec((part // steps, width), lambda j, sc, n=n: (place(sc, n) * steps + j, 0)) for n in (0, 3)]
    row = lambda j, sc: (j, 0)
    return call(
        cut_body,
        (steps,),
        ups + downs,
        [spec((width // steps, part), row)] * 2 + [spec((part // steps, width), row)] * 2,
        [far((width, part), LOW)] * 2 + [far((part, width), LOW)] * 2,
        weight=1,
    )(sc, w_up, w_up, w_down, w_down)


def all_sum(line, value, n_seq, n_ffn):
    for axis, size in (("seq", n_seq), ("ffn", n_ffn)):
        for bit in bits_of(size):
            value = value + line.put(swap(value, axis, bit))
            line.mark(value)
            yield value


def bits_of(size):
    found = []
    bit = 1
    while bit < size:
        found.append(bit)
        bit *= 2
    return found


def columns_of(found):
    found = found.reshape((-1,) + found.shape[3:])
    return jnp.transpose(found, (1, 0, 2)).reshape(found.shape[1], -1)


def on_device(
    tokens,
    spots,
    counts,
    fill,
    cot,
    w_qkv,
    b_q,
    b_v,
    w_out,
    b_out,
    gain_one,
    shift_one,
    w_up,
    b_up,
    w_down,
    b_down,
    gain_two,
    shift_two,
):
    n_seq, n_ffn = lax.axis_size("seq"), lax.axis_size("ffn")
    seq, ffn = lax.axis_index("seq"), lax.axis_index("ffn")
    rows, width = tokens.shape
    slots = spots.shape[1]
    units = w_up.shape[1]
    sc = jnp.stack([seq.astype(jnp.int32), ffn.astype(jnp.int32), counts[0]])
    fill, cot = fill[0], cot[0]
    vector = lambda v: v.astype(F32).reshape(1, -1)
    gain_a, shift_a, gain_b, shift_b = (vector(v) for v in (gain_one, shift_one, gain_two, shift_two))
    bias_qkv = vector(jnp.concatenate([b_q, jnp.zeros_like(b_q), b_v]))

    order = ffn ^ jnp.arange(n_ffn)
    line = Line()
    pairs = n_ffn == 2
    if pairs:
        split = "pairs"
        w_up, w_down, w_qkv = in_hbm(w_up, w_down, w_qkv)
        up_own, up_far, down_own, down_far = cut(sc, w_up, w_down)
        up_own = swap(up_own, "ffn", 1)
        b_other = swap(b_up, "ffn", 1)
        down_own = swap(down_own, "ffn", 1)
        up_far = swap(up_far, "ffn", 1)
        down_far = swap(down_far, "ffn", 1)
    else:
        split = "stack"
        ups = (jnp.take(lax.all_gather(w_up, "ffn"), order[1:], axis=0),)
        downs = (jnp.take(lax.all_gather(w_down, "ffn"), order[1:], axis=0),)
        b_other = jnp.take(lax.all_gather(b_up, "ffn"), order[1:], axis=0)

    x, x_keep, x_send, qkv = embed_qkv(sc, tokens, spots, fill, w_qkv, bias_qkv, n_seq)
    line.mark(qkv)
    if pairs:
        line.need(up_own, b_other)
        up_y, up_z = swap(line.put(up_own), "seq", 2), swap(line.put(up_own), "seq", 4)
    att, att_keep, att_send, logs = attend(sc, line.put(qkv), n_seq)
    line.mark(att)
    if pairs:
        up_near = stack(sc, *line.put(up_own, up_y, up_z))
        line.mark(up_near)
        line.need(down_own)
        down_y, down_z = swap(line.put(down_own), "seq", 2), swap(line.put(down_own), "seq", 4)
        up_near_other = swap(up_near, "seq", 1)
    hat, inv, low, n_keep, n_send = norm_one(sc, line.put(att), w_out, x, vector(b_out), gain_a, shift_a, n_seq)
    line.mark(low)
    if pairs:
        line.need(up_near_other, up_far)
    x_get = swap(line.put(x_send), "seq", 1)
    att_get = swap(line.put(att_send), "seq", 1)
    hid_own, slope_own, total = ffn_fwd(sc, line.put(low), vector(b_up), (w_up,), (w_down,), "own")
    line.mark(hid_own)
    if pairs:
        line.need(x_get, att_get, down_far)
        up_far, down_far = line.put(up_far)[None], line.put(down_far)[None]
        up_far_other, down_far_other = swap(up_far, "seq", 1), swap(down_far, "seq", 1)
        down_near = stack(sc, *line.put(down_own, down_y, down_z))
        line.mark(down_near)
        down_near_other = swap(down_near, "seq", 1)
        ups = (up_near, up_near_other, up_far, up_far_other)
        downs = (down_near, down_near_other, down_far, down_far_other)
    n_get = swap(line.put(n_send), "seq", 1)
    hid_own_get = swap(line.put(hid_own), "seq", 1)
    hid_oth, slope_oth, total = ffn_fwd(sc, line.put(low), vector(b_other), ups, downs, split, total)
    line.mark(hid_oth)
    line.need(n_get)
    hid_oth_get = swap(hid_oth, "seq", 1)

    output, g_two, g_down, d_keep, d_send, sums_two = norm_two(
        sc, line.put(total), hat, gain_a, shift_a, vector(b_down), gain_b, shift_b, spots, cot, n_seq
    )
    line.mark(g_down)
    line.need(hid_own_get, hid_oth_get)
    d_get = swap(d_send, "seq", 1)

    found_bits = bits_of(n_seq)
    seq_bits = [2] + found_bits[2:][::-1]
    x_step = ("ffn", 1)
    y_step = ("seq", 2)
    z_steps = [("seq", b) for b in found_bits[2:]]
    x_first = [("ffn", b) for b in bits_of(n_ffn)[::-1]] + z_steps + [y_step]
    z_axes = [(step, 2) for step in z_steps[::-1]]
    per = units // WIDE
    half = per // 2
    chunk = width // n_seq
    shards = lambda v, n, places: v.reshape(n, -1, places, chunk, WIDE)
    column = lambda start: (lambda b, sc: (0, start + b))
    d_left, n_left = (d_keep, d_get), (n_keep, n_get)

    def streams(found, blocks_a, blocks_b):
        a = [("block", blocks_a), (y_step, 2)] + z_axes
        b = [(x_step, 2), ("block", blocks_b)] + z_axes
        return Group(sc, line, [
            (a, found["keep_a"], found["send_a"], x_step),
            (b, found["keep_b"], found["send_b"], y_step),
        ])

    def big(left, own, own_get, oth, oth_get):
        left = (line.put(left[0]), left[1])
        found = weight_grad(sc, [left], [
            (oth, oth_get, half // 2, column(0), 0, ("send_a",)),
            (own, own_get, half // 2, column(half // 2), 0, ("keep_b", "send_b")),
            (oth, oth_get, half // 2, column(half // 2), 0, ("keep_b", "send_b")),
            (own, own_get, half // 2, column(0), 0, ("keep_a",)),
        ], 2)
        line.mark(found["keep_a"])
        return streams(found, half, per - half)

    def big_whole(left, own, own_get, oth, oth_get):
        n_oth = oth.shape[1] // WIDE
        left = (line.put(left[0]), left[1])
        found = weight_grad(sc, [left], [
            (own, own_get, per, column(0), 0, ("all",)), (oth, oth_get, n_oth, column(0), 0, ("all",))
        ])["all"]
        line.mark(found)
        return Stream(line, seq_bits, x_first, whole=shards(found, n_ffn, n_seq // 2))

    def narrow(mine, other, first, count, matrix, names):
        per_row = mine.shape[-1] // WIDE
        each = per_row * (mine.shape[0] if mine.ndim == 3 else 1) // n_ffn

        def segment(shard):
            def index(b, sc):
                block = (shard ^ sc[1]) * each + first + b
                return (0, block) if mine.ndim == 2 else (block // per_row, 0, block % per_row)

            return (mine, other, count, index, matrix, names)

        return segment

    def narrow_whole(left, mine, other):
        per_row = mine.shape[-1] // WIDE
        blocks = per_row * (mine.shape[0] if mine.ndim == 3 else 1)
        index = (lambda b, sc: (0, b)) if mine.ndim == 2 else (lambda b, sc: (b // per_row, 0, b % per_row))
        whole = weight_grad(sc, [(line.put(left[0]), left[1])], [(mine, other, blocks, index, 0, ("all",))])["all"]
        line.mark(whole)
        share = blocks * WIDE // n_ffn
        whole = whole.reshape(blocks, n_seq // 2, chunk, WIDE)
        whole = jnp.transpose(whole, (1, 2, 0, 3)).reshape(n_seq // 2, chunk, n_ffn, share)
        whole = jnp.take(jnp.transpose(whole, (2, 0, 1, 3)), order, axis=0)[:, None]
        return Stream(line, seq_bits, x_first, whole=whole)

    ways = {} if not pairs else {"z": [(z_steps[0],), (z_steps[1],), (y_step, x_step)], "y": [(y_step, x_step), (z_steps[0],), (z_steps[1],)]}
    way_d, way_u = list(ways.get("z", ())), list(ways.get("z", ()))
    if pairs:
        held = in_hbm(*ups, *downs)
        ups, downs = held[:4], held[4:]
    columns = lambda count, first, target=0, turned=False: [
        (target, (first + n) * WIDE, turned) for n in range(count)
    ]
    if pairs:
        ops = {}

        def wg_d():
            ops["D"] = big(d_left, hid_own, hid_own_get, hid_oth, hid_oth_get)

        def ffn_back():
            gp_oth, gp_own, bs_oth, bs_own, total = ffn_both(
                sc, line.put(g_down), slope_oth, slope_own, ups, downs, w_up, w_down
            )
            line.mark(gp_own)
            ops["gp"] = (gp_own, swap(gp_own, "seq", 1), gp_oth, swap(gp_oth, "seq", 1))
            ops["bs"] = (bs_own, bs_oth)
            ops["total"] = total

        def norm_back_one():
            ops["one"] = norm_one_back(sc, line.put(g_two), ops["total"], hat, inv, gain_a, w_out)
            line.mark(ops["one"][2])
            ops["low"] = (ops["one"][1], swap(ops["one"][1], "seq", 1))

        def wg_u():
            line.need(ops["gp"][1], ops["gp"][3])
            ops["U"] = big(n_left, *ops["gp"])
            line.need(ops["low"][1])

        def back():
            g_qkv, sums_att = attend_back(sc, line.put(qkv), att, ops["one"][2], logs)
            line.mark(g_qkv)
            ops["qkv"] = (g_qkv, swap(g_qkv, "seq", 1))
            ops["sums_att"] = sums_att

        def wg_q():
            q = ops["qkv"]
            lefts = [(line.put(x_keep), x_get), (att_keep, att_get)]
            q_a = narrow(*q, 0, 2, 0, ("send_a",))
            q_b = narrow(*q, 2, 1, 0, ("keep_b", "send_b"))
            o_b = narrow(*ops["low"], 0, 1, 1, ("keep_b", "send_b"))
            ops["found"] = weight_grad(sc, lefts, [q_a(1), q_b(0), o_b(0), q_b(1), o_b(1)])
            line.mark(ops["found"]["keep_b"])

        def wg_q_rest():
            q_keep = narrow(*ops["qkv"], 0, 2, 0, ("keep_a",))
            found = dict(ops["found"])
            found.update(weight_grad(sc, [(line.put(x_keep), x_get)], [q_keep(0)]))
            line.mark(found["keep_a"])
            ops["Q"] = streams(found, 2, 2)

        def tokens_back():
            ops["tokens"] = token_grads(sc, line.put(ops["qkv"][0]), w_qkv, ops["one"][0], spots, slots)
            line.mark(ops["tokens"][0])

        def sums_start():
            bs_own, bs_oth = ops["bs"]
            ops["sums"] = pack(line.put(sc), sums_two, ops["one"][3], bs_own, bs_oth, ops["sums_att"])
            line.mark(ops["sums"])
            ops["sum_steps"] = [("seq", 1), ("seq", 2), ("ffn", 1)] + [("seq", b) for b in bits_of(n_seq)[2:]]
            sums_post()

        def sums_post():
            step = ops["sum_steps"].pop(0)
            ops["got"] = swap(line.put(ops["sums"]), *step)

        def sums_add():
            mine, got = line.put(ops["sums"], ops["got"])
            ops["sums"] = mine + got
            line.mark(ops["sums"])
            if ops["sum_steps"]:
                sums_post()

        def step_of(name, way, weight=0):
            return lambda: ops[name].advance(*way.pop(0), weight=weight)

        def end_d():
            ops["down"] = ops["D"].finish(
                [columns(half, 0, turned=True), columns(per - half, half, turned=True)], [(units, chunk)]
            )

        def end_u():
            ops["up"] = ops["U"].finish([columns(half, 0), columns(per - half, half)], [(chunk, units)])

        def end_q():
            ops["last"] = ops["Q"].finish(
                [columns(2, 0), columns(1, 2) + columns(1, 0, 1)], [(chunk, 3 * WIDE), (chunk, WIDE)]
            )

        way_q = [(y_step, x_step), (z_steps[0],), (z_steps[1],)]
        steps = {
            "gD": wg_d, "B": ffn_back, "N": norm_back_one, "gU": wg_u, "A": back, "G": wg_q, "H": wg_q_rest,
            "T": tokens_back, "P": sums_start, "S": sums_add, "D": step_of("D", way_d), "D!": step_of("D", way_d, 0.5), "U!": step_of("U", way_u, 1), "U": step_of("U", way_u),
            "Q": step_of("Q", way_q), "eD": end_d, "eU": end_u, "eQ": end_q,
        }
        for name in SEQUENCE:
            steps[name]()
        grad_tokens, grad_fill = ops["tokens"]
        (grad_down,), (grad_up,) = ops["down"], ops["up"]
        grad_qkv, grad_out = ops["last"]
        total_sums = ops["sums"].reshape(-1)
    else:
        down_a = big_whole(d_left, hid_own, hid_own_get, hid_oth, hid_oth_get)
        gp_oth, bs_oth, g_total = ffn_bwd(sc, line.put(g_down), slope_oth, ups, downs, split)
        line.mark(gp_oth)
        gp_oth_get = swap(gp_oth, "seq", 1)
        gp_own, bs_own, g_total = ffn_bwd(sc, line.put(g_down), slope_own, (w_up,), (w_down,), "own", g_total)
        line.mark(gp_own)
        gp_own_get = swap(gp_own, "seq", 1)
        g_one, g_att_low, g_att, sums_one = norm_one_back(sc, line.put(g_two), g_total, hat, inv, gain_a, w_out)
        line.mark(g_att)
        g_att_get = swap(g_att_low, "seq", 1)
        up_a = big_whole(n_left, gp_own, gp_own_get, gp_oth, gp_oth_get)
        g_qkv, sums_att = attend_back(sc, line.put(qkv), att, g_att, logs)
        line.mark(g_qkv)
        g_qkv_get = swap(g_qkv, "seq", 1)
        b_up_sums = jnp.concatenate([bs_own.reshape(1, units), bs_oth.reshape(n_ffn - 1, units)])
        b_up_sums = jnp.take(b_up_sums, order, axis=0).reshape(-1)
        sums = jnp.concatenate(
            [sums_two[:3].reshape(-1), sums_one[:3].reshape(-1), b_up_sums, sums_att.reshape(-1)]
        )
        grad_tokens, grad_fill = token_grads(sc, line.put(g_qkv), w_qkv, g_one, spots, slots)
        line.mark(grad_tokens)
        out = narrow_whole((att_keep, att_get), g_att_low, g_att_get)
        qkv_a = narrow_whole((x_keep, x_get), g_qkv, g_qkv_get)
        (*_, total_sums) = all_sum(line, sums, n_seq, n_ffn)
        grad_down, grad_up = columns_of(down_a.finish()).T, columns_of(up_a.finish())
        grad_out, grad_qkv = columns_of(out.finish()), columns_of(qkv_a.finish())
    hidden_units = n_ffn * units

    part = lambda v, n: v[n * width : (n + 1) * width]
    return (
        output,
        grad_tokens,
        grad_fill[None],
        grad_qkv,
        total_sums[6 * width + hidden_units : 7 * width + hidden_units],
        total_sums[7 * width + hidden_units : 8 * width + hidden_units],
        grad_out,
        part(total_sums, 5),
        part(total_sums, 3),
        part(total_sums, 4),
        grad_up,
        total_sums[6 * width : 6 * width + hidden_units],
        grad_down,
        part(total_sums, 2),
        part(total_sums, 0),
        part(total_sums, 1),
    )


def solution(mesh):
    rows = ("seq", "ffn")
    in_specs = (
        P(rows, None),
        P(rows, None),
        P(rows),
        P(rows, None, None),
        P(rows, None, None),
        P(),
        P(),
        P(),
        P(),
        P(),
        P(),
        P(),
        P(None, "ffn"),
        P("ffn"),
        P("ffn", None),
        P(),
        P(),
        P(),
    )
    out_specs = (
        P(rows, None),
        P(rows, None),
        P(rows, None, None),
        P("seq", "ffn"),
        P(),
        P(),
        P("seq", "ffn"),
        P(),
        P(),
        P(),
        P("seq", "ffn"),
        P(),
        P("ffn", "seq"),
        P(),
        P(),
        P(),
    )
    return jax.shard_map(on_device, mesh=mesh, in_specs=in_specs, out_specs=out_specs, check_vma=False)
```

```python
import functools

import jax
import jax.numpy as jnp
from jax import lax
from jax.experimental import pallas as pl
from jax.experimental.pallas import tpu as pltpu
from jax.sharding import PartitionSpec as P

H = 16
F32 = jnp.float32
LOW = jnp.bfloat16
epsilon = 1e-12
LOG2E = 1.4426950408889634
NT = (((1,), (1,)), ((), ()))
WIDE = 512
SEQUENCE = ("gD", "B", "N", "D!", "gU", "A", "D", "P", "S", "U!", "S", "G", "S", "H", "D", "T", "Q", "U", "S", "Q", "eD", "U", "S", "Q", "eU", "eQ")
STEP = 3 * 10**10


def mm(left, right):
    return jnp.dot(left, right, preferred_element_type=F32)


def mm_nt(left, right):
    return lax.dot_general(left, right, NT, preferred_element_type=F32)


def call(body, grid, in_specs, out_specs, out_shape, scratch=(), prefetch=1, mib=32, weight=0):
    return pl.pallas_call(
        body,
        grid_spec=pltpu.PrefetchScalarGridSpec(
            num_scalar_prefetch=prefetch,
            grid=grid,
            in_specs=in_specs,
            out_specs=out_specs,
            scratch_shapes=list(scratch),
        ),
        out_shape=out_shape,
        compiler_params=pltpu.CompilerParams(
            dimension_semantics=("arbitrary",) * len(grid), vmem_limit_bytes=mib << 20
        ),
        cost_estimate=pl.CostEstimate(flops=int(1 + weight * STEP), bytes_accessed=1, transcendentals=0),
    )


def far(dims, dtype):
    return pltpu.HBM(dims, dtype)


def in_hbm(*values):
    return [pltpu.with_memory_space_constraint(value, pltpu.HBM) for value in values]


def spec(shape, index):
    return pl.BlockSpec(shape, index)


def shape(dims, dtype):
    return jax.ShapeDtypeStruct(dims, dtype)


def one_hot_rows(sc, spots, first, rows):
    slots = spots.shape[1]
    place = lax.broadcasted_iota(jnp.int32, (rows, slots), 0) + first
    slot = lax.broadcasted_iota(jnp.int32, (rows, slots), 1)
    hit = (place == spots) & (slot < sc[2])
    return jnp.where(hit, 1.0, 0.0)


def store_turned(sc, value, keep_ref, send_ref, first_column, chunk):
    columns = value.shape[1]
    for block in range(0, columns, 128):
        turned = jnp.transpose(value[:, block : block + 128]).astype(LOW)
        for part in range(0, 128, chunk):
            place = ((first_column + block + part) // chunk) ^ sc[0]
            piece = turned[part : part + chunk]
            at = ((place // 2) % 2) * (keep_ref.shape[0] // 2) + place // 4

            @pl.when(place % 2 == 0)
            def _():
                keep_ref[at] = piece

            @pl.when(place % 2 == 1)
            def _():
                send_ref[at] = piece


def qkv_body(chunk, sc, tokens, spots, fill, w, bias, x_out, keep, send, qkv):
    @pl.when(pl.program_id(0) == 0)
    def _():
        placed = one_hot_rows(sc, spots[...], 0, tokens.shape[0])
        kept = 1.0 - jnp.sum(placed, axis=1, keepdims=True)
        x = tokens[...].astype(F32) * kept + mm(placed.astype(LOW), fill[...])
        x_out[...] = x.astype(LOW)
        store_turned(sc, x, keep, send, 0, chunk)

    qkv[...] = (mm(x_out[...], w[...]) + bias[...]).astype(LOW)


def embed_qkv(sc, tokens, spots, fill, w_qkv, bias, n_seq):
    rows, width = tokens.shape
    out = w_qkv.shape[1]
    block = 1536
    chunk = width // n_seq
    turned = (n_seq // 2, chunk, rows)
    whole = lambda j, sc: (0, 0)
    return call(
        functools.partial(qkv_body, chunk),
        (out // block,),
        [
            spec((rows, width), whole),
            spec(spots.shape, whole),
            spec(fill.shape, whole),
            spec((width, block), lambda j, sc: (0, j)),
            spec((1, block), lambda j, sc: (0, j)),
        ],
        [
            spec((rows, width), whole),
            spec(turned, lambda j, sc: (0, 0, 0)),
            spec(turned, lambda j, sc: (0, 0, 0)),
            spec((rows, block), lambda j, sc: (0, j)),
        ],
        [shape((rows, width), LOW), far(turned, LOW), far(turned, LOW), shape((rows, out), LOW)],
        weight=1,
    )(sc, tokens, spots, fill, w_qkv, bias)


def head_masks(width, size, factor):
    lane = lax.broadcasted_iota(jnp.int32, (1, width), 1)
    return [jnp.where(lane // size == n, factor, 0.0).astype(LOW) for n in range(width // size)]


def attend_body(chunk, size, scale, sc, q, k, v, att, keep, send, logs):
    rows, width = q.shape
    pair = 2 * size
    masks = head_masks(pair, size, scale)
    lane = lax.broadcasted_iota(jnp.int32, (1, pair), 1)
    place_first = pl.program_id(0) * width
    for first in range(0, width, pair):
        columns = slice(first, first + pair)
        mixed, stats = [], []
        for mask in masks:
            scores = mm_nt(q[:, columns] * mask, k[:, columns])
            peak = jnp.max(scores, axis=1, keepdims=True) * LOG2E
            expo = jnp.exp2(scores * LOG2E - peak)
            total = jnp.sum(expo, axis=1, keepdims=True)
            mixed.append(mm(expo.astype(LOW), v[:, columns]) * (1.0 / total))
            stats.append(peak + jnp.log2(total))
        both = jnp.where(lane < size, mixed[0], mixed[1])
        att[:, columns] = both.astype(LOW)
        logs[:, columns] = jnp.where(lane < size, stats[0], stats[1])
        store_turned(sc, both, keep, send, place_first + first, chunk)


def attend(sc, qkv, n_seq):
    rows = qkv.shape[0]
    width = qkv.shape[1] // 3
    size = width // H
    block = 8 * size
    steps = width // block
    chunk = width // n_seq
    turned = (n_seq // 2, chunk, rows)
    whole = lambda j, sc: (0, 0, 0)
    tile = spec((rows, block), lambda j, sc: (0, j))
    return call(
        functools.partial(attend_body, chunk, size, size ** (-0.5)),
        (steps,),
        [
            tile,
            spec((rows, block), lambda j, sc: (0, steps + j)),
            spec((rows, block), lambda j, sc: (0, 2 * steps + j)),
        ],
        [tile, spec(turned, whole), spec(turned, whole), tile],
        [shape((rows, width), LOW), far(turned, LOW), far(turned, LOW), shape((rows, width), F32)],
        weight=1,
    )(sc, qkv, qkv, qkv)


def norm_one_body(chunk, sc, att, w, x, b, gain, shift, hat, inv, low, keep, send):
    value = x[...].astype(F32) + mm(att[...], w[...]) + b[...]
    centre = value - jnp.mean(value, axis=-1, keepdims=True)
    spread = jnp.mean(centre * centre, axis=-1, keepdims=True)
    inverse = lax.rsqrt(spread + epsilon)
    scaled = centre * inverse
    hat[...] = scaled
    inv[...] = inverse
    normed = scaled * gain[...] + shift[...]
    low[...] = normed.astype(LOW)
    store_turned(sc, normed, keep, send, 0, chunk)


def norm_one(sc, att, w_out, x, b_out, gain, shift, n_seq):
    rows, width = x.shape
    block = 512
    chunk = width // n_seq
    turned = (n_seq // 2, chunk, rows)
    row = lambda i, sc: (i, 0)
    whole = lambda i, sc: (0, 0)
    vector = spec((1, width), whole)
    return call(
        functools.partial(norm_one_body, chunk),
        (rows // block,),
        [spec((block, width), row), spec((width, width), whole), spec((block, width), row), vector, vector, vector],
        [
            spec((block, width), row),
            spec((block, 1), row),
            spec((block, width), row),
            spec((n_seq // 2, chunk, block), lambda i, sc: (0, 0, i)),
            spec((n_seq // 2, chunk, block), lambda i, sc: (0, 0, i)),
        ],
        [
            far((rows, width), F32),
            shape((rows, 1), F32),
            shape((rows, width), LOW),
            far(turned, LOW),
            far(turned, LOW),
        ],
        weight=1,
    )(sc, att, w_out, x, b_out, gain, shift)


TAIL = tuple(0.5 * c for c in (0.254829592, -0.284496736, 1.421413741, -1.453152027, 1.061405429))
TAIL_P = 0.3275911 * 0.7071067811865476


def gelu_both(x):
    t = 1.0 / (1.0 + TAIL_P * jnp.abs(x))
    bell = jnp.exp2(x * x * (-0.5 * LOG2E))
    poly = TAIL[4]
    for c in TAIL[3::-1]:
        poly = poly * t + c
    tail = poly * t * bell
    mass = jnp.where(x < 0.0, tail, 1.0 - tail)
    return x * mass, mass + x * bell * 0.3989422804014327


def ffn_specs(split, width, part, units):
    if split == "own":
        wide = min(2 * WIDE, units)
        ups = [spec((width, wide), lambda j, sc: (0, j))]
        downs = [spec((wide, width), lambda j, sc: (j, 0))]
        return ups, downs, wide
    if split == "stack":
        ups = [spec((None, width, part), lambda j, sc: (j, 0, 0))]
        downs = [spec((None, part, width), lambda j, sc: (j, 0, 0))]
        return ups, downs, part
    near = lambda j, sc: (jnp.minimum(j, 2), 0, 0)
    far = lambda j, sc: (0, 0, 0)
    ups = [spec((None, width, part), at) for at in (near, near, far, far)]
    downs = [spec((None, part, width), at) for at in (near, near, far, far)]
    return ups, downs, part


def column_block(split):
    if split == "pairs":
        return lambda j, sc: (0, j ^ ((sc[0] // 2) % 4))
    return lambda j, sc: (0, j)


def for_pieces(split, size, sc, ups, downs, work):
    if split != "pairs":
        work([(ups[0], downs[0], 0)])
        return
    core = sc[0] % 2
    places = [pl.multiple_of(core * size, size), pl.multiple_of((1 - core) * size, size)]
    step = pl.program_id(0)
    pl.when(step < 3)(lambda: work(list(zip(ups[:2], downs[:2], places))))
    pl.when(step == 3)(lambda: work(list(zip(ups[2:], downs[2:], places))))


def ffn_fwd_body(split, size, n, first, sc, *refs):
    low, bias = refs[:2]
    ups, downs = refs[2 : 2 + n], refs[2 + n : 2 + 2 * n]
    rest = refs[2 + 2 * n :]
    start = None
    if not first:
        start, rest = rest[0], rest[1:]
    hidden, slope, total = rest
    @pl.when(pl.program_id(0) == 0)
    def _():
        total[...] = jnp.zeros_like(total) if first else start[...]

    def work(pieces):
        mixed = None
        for up, down, offset in pieces:
            columns = pl.ds(offset, size)
            pre = mm(low[...], up[...]) + bias[:, columns]
            act, grad = gelu_both(pre)
            act = act.astype(LOW)
            hidden[:, columns] = act
            slope[:, columns] = grad.astype(LOW)
            product = mm(act, down[...])
            mixed = product if mixed is None else mixed + product
        total[...] += mixed

    for_pieces(split, size, sc, ups, downs, work)


def ffn_fwd(sc, low, bias, ups, downs, split, start=None):
    rows, width = low.shape
    units = bias.shape[1]
    part = ups[0].shape[-1]
    up_specs, down_specs, size = ffn_specs(split, width, part, units)
    step = 2 * part if split == "pairs" else size
    whole = lambda j, sc: (0, 0)
    column = column_block(split)
    total = spec((rows, width), whole)
    first = start is None
    return call(
        functools.partial(ffn_fwd_body, split, size, len(ups), first),
        (units // step,),
        [total, spec((1, step), column)] + up_specs + down_specs + ([] if first else [total]),
        [spec((rows, step), column), spec((rows, step), column), total],
        [shape((rows, units), LOW), shape((rows, units), LOW), shape((rows, width), F32)],
        weight=1,
    )(sc, low, bias, *ups, *downs, *([] if first else [start]))


def ffn_bwd_body(split, size, n, first, sc, *refs):
    low, slope = refs[:2]
    ups, downs = refs[2 : 2 + n], refs[2 + n : 2 + 2 * n]
    rest = refs[2 + 2 * n :]
    start = None
    if not first:
        start, rest = rest[0], rest[1:]
    g_low, sums, total = rest
    @pl.when(pl.program_id(0) == 0)
    def _():
        total[...] = jnp.zeros_like(total) if first else start[...]

    def work(pieces):
        mixed = None
        for up, down, offset in pieces:
            columns = pl.ds(offset, size)
            g_pre = mm_nt(low[...], down[...]) * slope[:, columns].astype(F32)
            sums[:, columns] = jnp.sum(g_pre, axis=0, keepdims=True)
            rounded = g_pre.astype(LOW)
            g_low[:, columns] = rounded
            product = mm_nt(rounded, up[...])
            mixed = product if mixed is None else mixed + product
        total[...] += mixed

    for_pieces(split, size, sc, ups, downs, work)


def ffn_bwd(sc, low, slope, ups, downs, split, start=None):
    rows, width = low.shape
    units = slope.shape[1]
    part = ups[0].shape[-1]
    up_specs, down_specs, size = ffn_specs(split, width, part, units)
    step = 2 * part if split == "pairs" else size
    whole = lambda j, sc: (0, 0)
    column = column_block(split)
    total = spec((rows, width), whole)
    first = start is None
    return call(
        functools.partial(ffn_bwd_body, split, size, len(ups), first),
        (units // step,),
        [total, spec((rows, step), column)] + up_specs + down_specs + ([] if first else [total]),
        [spec((rows, step), column), spec((1, step), column), total],
        [shape((rows, units), LOW), shape((1, units), F32), shape((rows, width), F32)],
    )(sc, low, slope, *ups, *downs, *([] if first else [start]))


def ffn_both_body(size, sc, low, slope_oth, slope_own, *refs):
    ups, downs, (up, down) = refs[:4], refs[4:8], refs[8:10]
    g_oth, g_own, sums_oth, sums_own, total = refs[10:]
    core = sc[0] % 2
    places = [pl.multiple_of(core * size, size), pl.multiple_of((1 - core) * size, size)]
    step = pl.program_id(0)

    def work(pieces, slope, g_low, sums):
        mixed = None
        for up_ref, down_ref, offset, span in pieces:
            columns = pl.ds(offset, span)
            g_pre = mm_nt(low[...], down_ref[...]) * slope[:, columns].astype(F32)
            sums[:, columns] = jnp.sum(g_pre, axis=0, keepdims=True)
            rounded = g_pre.astype(LOW)
            g_low[:, columns] = rounded
            product = mm_nt(rounded, up_ref[...])
            mixed = product if mixed is None else mixed + product

        @pl.when(step == 0)
        def _():
            total[...] = mixed

        @pl.when(step > 0)
        def _():
            total[...] += mixed

    other = lambda group: [(u, d, place, size) for u, d, place in zip(ups[group], downs[group], places)]
    pl.when(step < 3)(lambda: work(other(slice(0, 2)), slope_oth, g_oth, sums_oth))
    pl.when(step == 3)(lambda: work(other(slice(2, 4)), slope_oth, g_oth, sums_oth))
    pl.when(step > 3)(lambda: work([(up, down, 0, down.shape[0])], slope_own, g_own, sums_own))


def ffn_both(sc, low, slope_oth, slope_own, ups, downs, up, down):
    rows, width = low.shape
    units = slope_own.shape[1]
    part = ups[0].shape[-1]
    wide = 2 * part
    own_wide = min(2 * WIDE, units)
    steps = units // own_wide
    whole = lambda j, sc: (0, 0)
    near = lambda j, sc: (jnp.minimum(j, 2), 0, 0)
    away = lambda j, sc: (0, 0, 0)
    oth = lambda j, sc: (0, jnp.minimum(j, 3) ^ ((sc[0] // 2) % 4))
    own = lambda j, sc: (0, jnp.maximum(j - 4, 0))
    own_row = lambda j, sc: (jnp.maximum(j - 4, 0), 0)
    return call(
        functools.partial(ffn_both_body, part),
        (4 + steps,),
        [spec((rows, width), whole), spec((rows, wide), oth), spec((rows, own_wide), own)]
        + [spec((None, width, part), at) for at in (near, near, away, away)]
        + [spec((None, part, width), at) for at in (near, near, away, away)]
        + [spec((width, own_wide), own), spec((own_wide, width), own_row)],
        [
            spec((rows, wide), oth),
            spec((rows, own_wide), own),
            spec((1, wide), oth),
            spec((1, own_wide), own),
            spec((rows, width), whole),
        ],
        [far((rows, units), LOW), far((rows, units), LOW), shape((1, units), F32), shape((1, units), F32), shape((rows, width), F32)],
        weight=0,
    )(sc, low, slope_oth, slope_own, *ups, *downs, up, down)


def norm_back(hat, inverse, gain, grad):
    inner = grad * gain
    mean = jnp.mean(inner, axis=-1, keepdims=True)
    along = jnp.mean(inner * hat, axis=-1, keepdims=True)
    return inverse * (inner - mean - hat * along)


def add_sums(sums, rows):
    @pl.when(pl.program_id(0) == 0)
    def _():
        sums[...] = jnp.zeros_like(sums)

    for n, value in enumerate(rows):
        sums[n : n + 1, :] += jnp.sum(value, axis=0, keepdims=True)


def norm_two_body(chunk, sc, mixed, hat_one, gain_one, shift_one, b_down, gain, shift, spots, cot, out, grad, low, keep, send, sums):
    rows = mixed.shape[0]
    value = hat_one[...] * gain_one[...] + shift_one[...] + mixed[...] + b_down[...]
    centre = value - jnp.mean(value, axis=-1, keepdims=True)
    spread = jnp.mean(centre * centre, axis=-1, keepdims=True)
    inverse = lax.rsqrt(spread + epsilon)
    hat = centre * inverse
    out[...] = (hat * gain[...] + shift[...]).astype(LOW)
    placed = one_hot_rows(sc, spots[...], pl.program_id(0) * rows, rows)
    out_grad = mm(placed.astype(LOW), cot[...])
    result = norm_back(hat, inverse, gain[...], out_grad)
    grad[...] = result
    low[...] = result.astype(LOW)
    store_turned(sc, result, keep, send, 0, chunk)
    add_sums(sums, (out_grad * hat, out_grad, result))


def norm_two(sc, mixed, hat_one, gain_one, shift_one, b_down, gain, shift, spots, cot, n_seq):
    rows, width = mixed.shape
    block = 512
    chunk = width // n_seq
    turned = (n_seq // 2, chunk, rows)
    row = lambda i, sc: (i, 0)
    whole = lambda i, sc: (0, 0)
    vector = spec((1, width), whole)
    tile = spec((block, width), row)
    return call(
        functools.partial(norm_two_body, chunk),
        (rows // block,),
        [tile, tile, vector, vector, vector, vector, vector, spec(spots.shape, whole), spec(cot.shape, whole)],
        [
            tile,
            tile,
            tile,
            spec((n_seq // 2, chunk, block), lambda i, sc: (0, 0, i)),
            spec((n_seq // 2, chunk, block), lambda i, sc: (0, 0, i)),
            spec((8, width), whole),
        ],
        [
            shape((rows, width), LOW),
            shape((rows, width), F32),
            shape((rows, width), LOW),
            far(turned, LOW),
            far(turned, LOW),
            shape((8, width), F32),
        ],
        weight=1,
    )(sc, mixed, hat_one, gain_one, shift_one, b_down, gain, shift, spots, cot)


def norm_one_back_body(sc, grad_two, ffn, hat, inv, gain, w, grad, low, g_att, sums):
    g_normed = grad_two[...] + ffn[...]
    result = norm_back(hat[...], inv[...], gain[...], g_normed)
    grad[...] = result
    rounded = result.astype(LOW)
    low[...] = rounded
    g_att[...] = mm_nt(rounded, w[...]).astype(LOW)
    add_sums(sums, (g_normed * hat[...], g_normed, result))


def norm_one_back(sc, grad_two, ffn, hat, inv, gain, w_out):
    rows, width = hat.shape
    block = 512
    row = lambda i, sc: (i, 0)
    whole = lambda i, sc: (0, 0)
    tile = spec((block, width), row)
    return call(
        norm_one_back_body,
        (rows // block,),
        [tile, tile, tile, spec((block, 1), row), spec((1, width), whole), spec((width, width), whole)],
        [tile, tile, tile, spec((8, width), whole)],
        [shape((rows, width), F32), shape((rows, width), LOW), shape((rows, width), LOW), shape((8, width), F32)],
        weight=0,
    )(sc, grad_two, ffn, hat, inv, gain, w_out)


def mm_tn(left, right):
    return lax.dot_general(left, right, (((0,), (0,)), ((), ())), preferred_element_type=F32)


def attend_back_body(size, scale, sc, q, k, v, att, g_att, logs, g_qkv, sums):
    rows, width = q.shape
    pair = 2 * size
    ones = head_masks(pair, size, 1.0)
    halves = head_masks(pair, size, scale)
    lane = lax.broadcasted_iota(jnp.int32, (1, pair), 1)
    for first in range(0, width, pair):
        columns = slice(first, first + pair)
        q_pair, k_pair, v_pair, g_pair = q[:, columns], k[:, columns], v[:, columns], g_att[:, columns]
        q_scaled = q_pair * jnp.asarray(scale, LOW)
        k_scaled = k_pair * jnp.asarray(scale, LOW)
        product = att[:, columns].astype(F32) * g_pair.astype(F32)
        log_pair = logs[:, columns]
        turned_v, turned_k, g_q = [], [], []
        for n in range(2):
            rows_of = slice(n * size, (n + 1) * size)
            scores = mm_nt(q_pair * halves[n], k_pair)
            probs = jnp.exp2(scores * LOG2E - log_pair[:, n * size : n * size + 1])
            g_probs = mm_nt(g_pair * ones[n], v_pair)
            level = jnp.sum(jnp.where(lane // size == n, product, 0.0), axis=1, keepdims=True)
            g_scores = (probs * (g_probs - level)).astype(LOW)
            turned_v.append(mm_tn(g_pair, probs.astype(LOW))[rows_of])
            turned_k.append(mm_tn(q_scaled, g_scores)[rows_of])
            g_q.append(mm(g_scores, k_scaled))
        query = jnp.where(lane < size, g_q[0], g_q[1]).astype(LOW)
        value = jnp.transpose(jnp.concatenate(turned_v, axis=0)).astype(LOW)
        g_qkv[0, :, columns] = query
        g_qkv[1, :, columns] = jnp.transpose(jnp.concatenate(turned_k, axis=0)).astype(LOW)
        g_qkv[2, :, columns] = value
        sums[0:1, columns] = jnp.sum(query.astype(F32), axis=0, keepdims=True)
        sums[1:2, columns] = jnp.sum(value.astype(F32), axis=0, keepdims=True)


def attend_back(sc, qkv, att, g_att, logs):
    rows, width = att.shape
    size = width // H
    block = 4 * size
    steps = width // block
    tile = spec((rows, block), lambda j, sc: (0, j))
    return call(
        functools.partial(attend_back_body, size, size ** (-0.5)),
        (steps,),
        [
            tile,
            spec((rows, block), lambda j, sc: (0, steps + j)),
            spec((rows, block), lambda j, sc: (0, 2 * steps + j)),
            tile,
            tile,
            tile,
        ],
        [spec((3, rows, block), lambda j, sc: (0, 0, j)), spec((2, block), lambda j, sc: (0, j))],
        [far((3, rows, width), LOW), shape((2, width), F32)],
        weight=0,
    )(sc, qkv, qkv, qkv, att, g_att, logs)


def token_grads_body(sc, g_qkv, w, base, spots, spots_column, tokens_out, fill_out):
    rows = base.shape[0]
    width = g_qkv.shape[2]
    grad = base[...]
    for n in range(3):
        grad = grad + mm_nt(g_qkv[n], w[:, n * width : (n + 1) * width])
    placed = one_hot_rows(sc, spots[...], 0, rows)
    kept = 1.0 - jnp.sum(placed, axis=1, keepdims=True)
    tokens_out[...] = (grad * kept).astype(LOW)
    slots = spots_column.shape[0]
    place = lax.broadcasted_iota(jnp.int32, (slots, rows), 1)
    slot = lax.broadcasted_iota(jnp.int32, (slots, rows), 0)
    hit = (place == spots_column[...]) & (slot < sc[2])
    fill_out[...] = mm(jnp.where(hit, 1.0, 0.0).astype(LOW), grad.astype(LOW)).astype(LOW)


def token_grads(sc, g_qkv, w_qkv, base, spots, slots):
    rows, width = base.shape
    block = 512
    column = lambda i, sc: (0, i)
    whole = lambda i, sc: (0, 0)
    tile = spec((rows, block), column)
    return call(
        token_grads_body,
        (width // block,),
        [
            spec(g_qkv.shape, lambda i, sc: (0, 0, 0)),
            spec((block, w_qkv.shape[1]), lambda i, sc: (i, 0)),
            tile,
            spec(spots.shape, whole),
            spec((slots, 1), whole),
        ],
        [tile, spec((slots, block), column)],
        [shape((rows, width), LOW), shape((slots, width), LOW)],
        weight=0.35,
    )(sc, g_qkv, w_qkv, base, spots, spots.reshape(slots, 1))


def weight_body(plan, lefts, sc, *refs):
    left_refs, refs = refs[: 2 * lefts], refs[2 * lefts :]
    ins, outs = refs[: 2 * len(plan)], refs[2 * len(plan) :]
    step = pl.program_id(0)
    first = 0
    for n, (count, matrix, targets) in enumerate(plan):
        left, left_other = left_refs[2 * matrix : 2 * matrix + 2]
        mine, other = ins[2 * n], ins[2 * n + 1]

        def work(left=left, left_other=left_other, mine=mine, other=other, targets=targets):
            places, _, depth = left.shape
            rows_of = lambda ref: ref[...].reshape(-1, depth)
            total = mm(rows_of(left), mine[...]) + mm(rows_of(left_other), other[...])
            total = total.astype(LOW).reshape(places, -1, total.shape[-1])
            share = places // len(targets)
            for block in range(total.shape[-1] // WIDE):
                columns = total[:, :, block * WIDE : (block + 1) * WIDE]
                for part, target in enumerate(targets):
                    outs[target][block * share : (block + 1) * share] = columns[part * share : (part + 1) * share]

        if len(plan) == 1:
            work()
        else:
            pl.when((step >= first) & (step < first + count))(work)
        first += count


def weight_grad(sc, lefts, segments, group=1):
    places, chunk, depth = lefts[0][0].shape
    left_spec = spec((places, chunk, depth), lambda j, sc: (0, 0, 0))
    in_specs = [left_spec] * (2 * len(lefts))
    operands = [value for pair in lefts for value in pair]
    spans, plan, first = {}, [], 0
    for mine, other, count, index, matrix, names in segments:
        def at(j, sc, first=first, count=count, index=index):
            return index(jnp.clip(j - first, 0, count - 1), sc)

        block = (depth, group * WIDE) if mine.ndim == 2 else (None, depth, group * WIDE)
        in_specs += [spec(block, at), spec(block, at)]
        operands += [mine, other]
        for name in names:
            begin = spans.setdefault(name, [first, first, places // len(names)])
            begin[1] = first + count
        first += count
    order = list(spans)
    for _, _, count, _, matrix, names in segments:
        plan.append((count, matrix, tuple(order.index(name) for name in names)))
    out_specs, out_shapes = [], []
    for begin, end, kept in spans.values():
        at = lambda j, sc, begin=begin, end=end: (jnp.clip(j, begin, end - 1) - begin, 0, 0)
        out_specs.append(spec((group * kept, chunk, WIDE), at))
        out_shapes.append(far(((end - begin) * group * kept, chunk, WIDE), LOW))
    found = call(
        functools.partial(weight_body, tuple(plan), len(lefts)),
        (first,),
        in_specs,
        out_specs,
        out_shapes,
        weight=0,
    )(sc, *operands)
    return dict(zip(order, found))


def add_body(count, plan, sc, *refs):
    outs = refs[2 * count :]
    for source, start, (outer, inner), target, place in plan:
        span = pl.ds(start, outer * 2 * inner)
        total = refs[2 * source][span].astype(F32) + refs[2 * source + 1][span].astype(F32)
        total = total.astype(LOW).reshape((outer, 2, inner) + total.shape[1:])
        for half in range(2):
            part = total[:, half]
            outs[2 * target + half][pl.ds(place, outer * inner)] = part.reshape((outer * inner,) + part.shape[2:])


def add_halves(sc, arrays, plan, sizes, weight):
    tile = WIDE // 2
    chunk = arrays[0][0].shape[1]
    column = lambda j, sc: (0, 0, j)
    operands = [value for pair in arrays for value in pair]
    found = call(
        functools.partial(add_body, len(arrays), tuple(plan)),
        (WIDE // tile,),
        [spec(value.shape[:2] + (tile,), column) for value in operands],
        [spec((size, chunk, tile), column) for size in sizes for _ in range(2)],
        [far((size, chunk, WIDE), LOW) for size in sizes for _ in range(2)],
        weight=weight,
    )(sc, *operands)
    return [(found[2 * n], found[2 * n + 1]) for n in range(len(sizes))]


def last_body(count, plan, sc, *refs):
    for source, place, target, at, turned in plan:
        total = refs[2 * source][place].astype(F32) + refs[2 * source + 1][place].astype(F32)
        out = refs[2 * count + target]
        if turned:
            out[at : at + WIDE, :] = jnp.transpose(total)
        else:
            out[:, at : at + WIDE] = total


def add_last(sc, arrays, plan, outs):
    whole = lambda n: (lambda j, sc: (0,) * n)
    operands = [value for pair in arrays for value in pair]
    return call(
        functools.partial(last_body, len(arrays), tuple(plan)),
        (1,),
        [spec(value.shape, whole(3)) for value in operands],
        [spec(dims, whole(2)) for dims in outs],
        [shape(dims, F32) for dims in outs],
    )(sc, *operands)


def stack_body(sc, *refs):
    out = refs[-1]
    for n, ref in enumerate(refs[:-1]):
        out[n] = ref[...]


def stack(sc, *values):
    rows, columns = values[0].shape
    steps = 2
    return call(
        stack_body,
        (steps,),
        [spec((rows // steps, columns), lambda j, sc: (j, 0))] * len(values),
        spec((len(values), rows // steps, columns), lambda j, sc: (0, j, 0)),
        far((len(values),) + values[0].shape, LOW),
        weight=1,
    )(sc, *values)


def swap(value, axis, bit):
    size = lax.axis_size(axis)
    return lax.ppermute(value, axis, [(n, n ^ bit) for n in range(size)])


def halves(value, bits, step):
    shards, blocks, places, chunk, wide = value.shape
    axis, bit = step
    if axis == "ffn":
        return value[: shards // 2], value[shards // 2 :], bits
    at = bits.index(bit)
    low = 1 << (len(bits) - 1 - at)
    parts = value.reshape(shards, blocks, places // (2 * low), 2, low, chunk, wide)
    dims = (shards, blocks, places // 2, chunk, wide)
    return (
        parts[:, :, :, 0].reshape(dims),
        parts[:, :, :, 1].reshape(dims),
        bits[:at] + bits[at + 1 :],
    )


class Line:
    def __init__(self):
        self.last = ()

    def put(self, *values):
        if self.last:
            values = lax.optimization_barrier(self.last + values)[len(self.last) :]
        return values if len(values) > 1 else values[0]

    def mark(self, value):
        self.last = (value,)

    def need(self, *values):
        self.last += values


class Stream:
    def __init__(self, line, bits, steps, whole=None, keep=None, send=None):
        self.line, self.bits, self.steps = line, list(bits), list(steps)
        if keep is None:
            keep, send, self.bits = halves(whole, self.bits, self.steps[0])
        elif self.steps[0][0] == "seq":
            self.bits.remove(self.steps[0][1])
        self.post(keep, send)

    def post(self, keep, send):
        self.keep = keep
        self.got = swap(send, *self.steps.pop(0))

    def advance(self):
        keep, got = self.line.put(self.keep, self.got)
        if self.steps:
            step = self.steps[0]
            keep_a, send_a, left = halves(keep, self.bits, step)
            keep_b, send_b, left = halves(got, self.bits, step)
            self.bits = left
            add = lambda a, b: (a.astype(F32) + b.astype(F32)).astype(LOW)
            send = add(send_a, send_b)
            keep = add(keep_a, keep_b)
            self.line.mark(keep)
            self.post(keep, send)
            return None
        total = keep.astype(F32) + got.astype(F32)
        self.line.mark(total)
        return total

    def finish(self):
        while True:
            total = self.advance()
            if total is not None:
                return total


class Group:
    def __init__(self, sc, line, parts):
        self.sc, self.line = sc, line
        self.arrays = []
        self.parts = []
        for n, (axes, keep, send, step) in enumerate(parts):
            self.arrays.append((keep, swap(send, *step)))
            self.parts.append((n, 0, list(axes)))

    def tied(self):
        flat = self.line.put(*[value for pair in self.arrays for value in pair])
        return [(flat[2 * n], flat[2 * n + 1]) for n in range(len(self.arrays))]

    def advance(self, *steps, weight=0):
        steps = steps * len(self.parts) if len(steps) == 1 else steps
        order = list(dict.fromkeys(steps))
        plan, sizes, parts = [], [0] * len(order), []
        for (array, start, axes), step in zip(self.parts, steps):
            at = [name for name, _ in axes].index(step)
            outer = inner = 1
            for _, size in axes[:at]:
                outer *= size
            for _, size in axes[at + 1 :]:
                inner *= size
            target = order.index(step)
            plan.append((array, start, (outer, inner), target, sizes[target]))
            parts.append((target, sizes[target], axes[:at] + axes[at + 1 :]))
            sizes[target] += outer * inner
        found = add_halves(self.sc, self.tied(), plan, sizes, weight)
        self.line.mark(found[0][0])
        self.arrays = [(keep, swap(send, *step)) for (keep, send), step in zip(found, order)]
        self.parts = parts

    def finish(self, targets, outs):
        plan = []
        for (array, start, _), places in zip(self.parts, targets):
            for n, place in enumerate(places):
                plan.append((array, start + n) + place)
        found = add_last(self.sc, self.tied(), plan, outs)
        self.line.mark(found[0])
        return found


def pack_body(sc, two, one, own, other, att, out):
    out[...] = jnp.zeros_like(out)
    out[0:3, :] = two[0:3, :]
    out[3:6, :] = one[0:3, :]
    width = out.shape[1]
    count = own.shape[1] // width
    for n in range(count):
        columns = slice(n * width, (n + 1) * width)
        first = sc[1] == 0
        out[6 + n : 7 + n, :] = jnp.where(first, own[:, columns], other[:, columns])
        out[6 + count + n : 7 + count + n, :] = jnp.where(first, other[:, columns], own[:, columns])
    out[6 + 2 * count : 8 + 2 * count, :] = att[...]


def pack(sc, *values):
    width = values[0].shape[1]
    rows = 8 + 2 * values[2].shape[1] // width
    rows += -rows % 8
    whole = lambda j, sc: (0, 0)
    return call(
        pack_body,
        (1,),
        [spec(v.shape, whole) for v in values],
        spec((rows, width), whole),
        far((rows, width), F32),
        weight=0,
    )(sc, *values)


def cut_body(sc, *refs):
    for ref, out in zip(refs[:4], refs[4:]):
        out[...] = ref[...]


def cut(sc, w_up, w_down):
    width, units = w_up.shape
    part = units // 8
    steps = 2
    place = lambda sc, away: (((sc[0] // 2) % 4) ^ away) * 2 + sc[0] % 2
    ups = [spec((width // steps, part), lambda j, sc, n=n: (j, place(sc, n))) for n in (0, 3)]
    downs = [spec((part // steps, width), lambda j, sc, n=n: (place(sc, n) * steps + j, 0)) for n in (0, 3)]
    row = lambda j, sc: (j, 0)
    return call(
        cut_body,
        (steps,),
        ups + downs,
        [spec((width // steps, part), row)] * 2 + [spec((part // steps, width), row)] * 2,
        [far((width, part), LOW)] * 2 + [far((part, width), LOW)] * 2,
        weight=1,
    )(sc, w_up, w_up, w_down, w_down)


def all_sum(line, value, n_seq, n_ffn):
    for axis, size in (("seq", n_seq), ("ffn", n_ffn)):
        for bit in bits_of(size):
            value = value + line.put(swap(value, axis, bit))
            line.mark(value)
            yield value


def bits_of(size):
    found = []
    bit = 1
    while bit < size:
        found.append(bit)
        bit *= 2
    return found


def columns_of(found):
    found = found.reshape((-1,) + found.shape[3:])
    return jnp.transpose(found, (1, 0, 2)).reshape(found.shape[1], -1)


def on_device(
    tokens,
    spots,
    counts,
    fill,
    cot,
    w_qkv,
    b_q,
    b_v,
    w_out,
    b_out,
    gain_one,
    shift_one,
    w_up,
    b_up,
    w_down,
    b_down,
    gain_two,
    shift_two,
):
    n_seq, n_ffn = lax.axis_size("seq"), lax.axis_size("ffn")
    seq, ffn = lax.axis_index("seq"), lax.axis_index("ffn")
    rows, width = tokens.shape
    slots = spots.shape[1]
    units = w_up.shape[1]
    sc = jnp.stack([seq.astype(jnp.int32), ffn.astype(jnp.int32), counts[0]])
    fill, cot = fill[0], cot[0]
    vector = lambda v: v.astype(F32).reshape(1, -1)
    gain_a, shift_a, gain_b, shift_b = (vector(v) for v in (gain_one, shift_one, gain_two, shift_two))
    bias_qkv = vector(jnp.concatenate([b_q, jnp.zeros_like(b_q), b_v]))

    order = ffn ^ jnp.arange(n_ffn)
    line = Line()
    pairs = n_ffn == 2
    if pairs:
        split = "pairs"
        w_up, w_down, w_qkv = in_hbm(w_up, w_down, w_qkv)
        up_own, up_far, down_own, down_far = cut(sc, w_up, w_down)
        up_own = swap(up_own, "ffn", 1)
        b_other = swap(b_up, "ffn", 1)
        down_own = swap(down_own, "ffn", 1)
        up_far = swap(up_far, "ffn", 1)
        down_far = swap(down_far, "ffn", 1)
    else:
        split = "stack"
        ups = (jnp.take(lax.all_gather(w_up, "ffn"), order[1:], axis=0),)
        downs = (jnp.take(lax.all_gather(w_down, "ffn"), order[1:], axis=0),)
        b_other = jnp.take(lax.all_gather(b_up, "ffn"), order[1:], axis=0)

    x, x_keep, x_send, qkv = embed_qkv(sc, tokens, spots, fill, w_qkv, bias_qkv, n_seq)
    line.mark(qkv)
    if pairs:
        line.need(up_own, b_other)
        up_y, up_z = swap(line.put(up_own), "seq", 2), swap(line.put(up_own), "seq", 4)
    att, att_keep, att_send, logs = attend(sc, line.put(qkv), n_seq)
    line.mark(att)
    if pairs:
        up_near = stack(sc, *line.put(up_own, up_y, up_z))
        line.mark(up_near)
        line.need(down_own)
        down_y, down_z = swap(line.put(down_own), "seq", 2), swap(line.put(down_own), "seq", 4)
        up_near_other = swap(up_near, "seq", 1)
    hat, inv, low, n_keep, n_send = norm_one(sc, line.put(att), w_out, x, vector(b_out), gain_a, shift_a, n_seq)
    line.mark(low)
    if pairs:
        line.need(up_near_other, up_far)
    x_get = swap(line.put(x_send), "seq", 1)
    att_get = swap(line.put(att_send), "seq", 1)
    hid_own, slope_own, total = ffn_fwd(sc, line.put(low), vector(b_up), (w_up,), (w_down,), "own")
    line.mark(hid_own)
    if pairs:
        line.need(x_get, att_get, down_far)
        up_far, down_far = line.put(up_far)[None], line.put(down_far)[None]
        up_far_other, down_far_other = swap(up_far, "seq", 1), swap(down_far, "seq", 1)
        down_near = stack(sc, *line.put(down_own, down_y, down_z))
        line.mark(down_near)
        down_near_other = swap(down_near, "seq", 1)
        ups = (up_near, up_near_other, up_far, up_far_other)
        downs = (down_near, down_near_other, down_far, down_far_other)
    n_get = swap(line.put(n_send), "seq", 1)
    hid_own_get = swap(line.put(hid_own), "seq", 1)
    hid_oth, slope_oth, total = ffn_fwd(sc, line.put(low), vector(b_other), ups, downs, split, total)
    line.mark(hid_oth)
    line.need(n_get)
    hid_oth_get = swap(hid_oth, "seq", 1)

    output, g_two, g_down, d_keep, d_send, sums_two = norm_two(
        sc, line.put(total), hat, gain_a, shift_a, vector(b_down), gain_b, shift_b, spots, cot, n_seq
    )
    line.mark(g_down)
    line.need(hid_own_get, hid_oth_get)
    d_get = swap(d_send, "seq", 1)

    found_bits = bits_of(n_seq)
    seq_bits = [2] + found_bits[2:][::-1]
    x_step = ("ffn", 1)
    y_step = ("seq", 2)
    z_steps = [("seq", b) for b in found_bits[2:]]
    x_first = [("ffn", b) for b in bits_of(n_ffn)[::-1]] + z_steps + [y_step]
    z_axes = [(step, 2) for step in z_steps[::-1]]
    per = units // WIDE
    half = per // 2
    chunk = width // n_seq
    shards = lambda v, n, places: v.reshape(n, -1, places, chunk, WIDE)
    column = lambda start: (lambda b, sc: (0, start + b))
    d_left, n_left = (d_keep, d_get), (n_keep, n_get)

    def streams(found, blocks_a, blocks_b):
        a = [("block", blocks_a), (y_step, 2)] + z_axes
        b = [(x_step, 2), ("block", blocks_b)] + z_axes
        return Group(sc, line, [
            (a, found["keep_a"], found["send_a"], x_step),
            (b, found["keep_b"], found["send_b"], y_step),
        ])

    def big(left, own, own_get, oth, oth_get):
        left = (line.put(left[0]), left[1])
        found = weight_grad(sc, [left], [
            (oth, oth_get, half // 2, column(0), 0, ("send_a",)),
            (own, own_get, half // 2, column(half // 2), 0, ("keep_b", "send_b")),
            (oth, oth_get, half // 2, column(half // 2), 0, ("keep_b", "send_b")),
            (own, own_get, half // 2, column(0), 0, ("keep_a",)),
        ], 2)
        line.mark(found["keep_a"])
        return streams(found, half, per - half)

    def big_whole(left, own, own_get, oth, oth_get):
        n_oth = oth.shape[1] // WIDE
        left = (line.put(left[0]), left[1])
        found = weight_grad(sc, [left], [
            (own, own_get, per, column(0), 0, ("all",)), (oth, oth_get, n_oth, column(0), 0, ("all",))
        ])["all"]
        line.mark(found)
        return Stream(line, seq_bits, x_first, whole=shards(found, n_ffn, n_seq // 2))

    def narrow(mine, other, first, count, matrix, names):
        per_row = mine.shape[-1] // WIDE
        each = per_row * (mine.shape[0] if mine.ndim == 3 else 1) // n_ffn

        def segment(shard):
            def index(b, sc):
                block = (shard ^ sc[1]) * each + first + b
                return (0, block) if mine.ndim == 2 else (block // per_row, 0, block % per_row)

            return (mine, other, count, index, matrix, names)

        return segment

    def narrow_whole(left, mine, other):
        per_row = mine.shape[-1] // WIDE
        blocks = per_row * (mine.shape[0] if mine.ndim == 3 else 1)
        index = (lambda b, sc: (0, b)) if mine.ndim == 2 else (lambda b, sc: (b // per_row, 0, b % per_row))
        whole = weight_grad(sc, [(line.put(left[0]), left[1])], [(mine, other, blocks, index, 0, ("all",))])["all"]
        line.mark(whole)
        share = blocks * WIDE // n_ffn
        whole = whole.reshape(blocks, n_seq // 2, chunk, WIDE)
        whole = jnp.transpose(whole, (1, 2, 0, 3)).reshape(n_seq // 2, chunk, n_ffn, share)
        whole = jnp.take(jnp.transpose(whole, (2, 0, 1, 3)), order, axis=0)[:, None]
        return Stream(line, seq_bits, x_first, whole=whole)

    ways = {} if not pairs else {"z": [(z_steps[0],), (z_steps[1],), (y_step, x_step)], "y": [(y_step, x_step), (z_steps[0],), (z_steps[1],)]}
    way_d, way_u = list(ways.get("z", ())), list(ways.get("z", ()))
    if pairs:
        held = in_hbm(*ups, *downs)
        ups, downs = held[:4], held[4:]
    columns = lambda count, first, target=0, turned=False: [
        (target, (first + n) * WIDE, turned) for n in range(count)
    ]
    if pairs:
        ops = {}

        def wg_d():
            ops["D"] = big(d_left, hid_own, hid_own_get, hid_oth, hid_oth_get)

        def ffn_back():
            gp_oth, gp_own, bs_oth, bs_own, total = ffn_both(
                sc, line.put(g_down), slope_oth, slope_own, ups, downs, w_up, w_down
            )
            line.mark(gp_own)
            ops["gp"] = (gp_own, swap(gp_own, "seq", 1), gp_oth, swap(gp_oth, "seq", 1))
            ops["bs"] = (bs_own, bs_oth)
            ops["total"] = total

        def norm_back_one():
            ops["one"] = norm_one_back(sc, line.put(g_two), ops["total"], hat, inv, gain_a, w_out)
            line.mark(ops["one"][2])
            ops["low"] = (ops["one"][1], swap(ops["one"][1], "seq", 1))

        def wg_u():
            line.need(ops["gp"][1], ops["gp"][3])
            ops["U"] = big(n_left, *ops["gp"])
            line.need(ops["low"][1])

        def back():
            g_qkv, sums_att = attend_back(sc, line.put(qkv), att, ops["one"][2], logs)
            line.mark(g_qkv)
            ops["qkv"] = (g_qkv, swap(g_qkv, "seq", 1))
            ops["sums_att"] = sums_att

        def wg_q():
            q = ops["qkv"]
            lefts = [(line.put(x_keep), x_get), (att_keep, att_get)]
            q_a = narrow(*q, 0, 2, 0, ("send_a",))
            q_b = narrow(*q, 2, 1, 0, ("keep_b", "send_b"))
            o_b = narrow(*ops["low"], 0, 1, 1, ("keep_b", "send_b"))
            ops["found"] = weight_grad(sc, lefts, [q_a(1), q_b(0), o_b(0), q_b(1), o_b(1)])
            line.mark(ops["found"]["keep_b"])

        def wg_q_rest():
            q_keep = narrow(*ops["qkv"], 0, 2, 0, ("keep_a",))
            found = dict(ops["found"])
            found.update(weight_grad(sc, [(line.put(x_keep), x_get)], [q_keep(0)]))
            line.mark(found["keep_a"])
            ops["Q"] = streams(found, 2, 2)

        def tokens_back():
            ops["tokens"] = token_grads(sc, line.put(ops["qkv"][0]), w_qkv, ops["one"][0], spots, slots)
            line.mark(ops["tokens"][0])

        def sums_start():
            bs_own, bs_oth = ops["bs"]
            ops["sums"] = pack(line.put(sc), sums_two, ops["one"][3], bs_own, bs_oth, ops["sums_att"])
            line.mark(ops["sums"])
            ops["sum_steps"] = [("seq", 1), ("seq", 2), ("ffn", 1)] + [("seq", b) for b in bits_of(n_seq)[2:]]
            sums_post()

        def sums_post():
            step = ops["sum_steps"].pop(0)
            ops["got"] = swap(line.put(ops["sums"]), *step)

        def sums_add():
            mine, got = line.put(ops["sums"], ops["got"])
            ops["sums"] = mine + got
            line.mark(ops["sums"])
            if ops["sum_steps"]:
                sums_post()

        def step_of(name, way, weight=0):
            return lambda: ops[name].advance(*way.pop(0), weight=weight)

        def end_d():
            ops["down"] = ops["D"].finish(
                [columns(half, 0, turned=True), columns(per - half, half, turned=True)], [(units, chunk)]
            )

        def end_u():
            ops["up"] = ops["U"].finish([columns(half, 0), columns(per - half, half)], [(chunk, units)])

        def end_q():
            ops["last"] = ops["Q"].finish(
                [columns(2, 0), columns(1, 2) + columns(1, 0, 1)], [(chunk, 3 * WIDE), (chunk, WIDE)]
            )

        way_q = [(y_step, x_step), (z_steps[0],), (z_steps[1],)]
        steps = {
            "gD": wg_d, "B": ffn_back, "N": norm_back_one, "gU": wg_u, "A": back, "G": wg_q, "H": wg_q_rest,
            "T": tokens_back, "P": sums_start, "S": sums_add, "D": step_of("D", way_d), "D!": step_of("D", way_d, 0.5), "U!": step_of("U", way_u, 1), "U": step_of("U", way_u),
            "Q": step_of("Q", way_q), "eD": end_d, "eU": end_u, "eQ": end_q,
        }
        for name in SEQUENCE:
            steps[name]()
        grad_tokens, grad_fill = ops["tokens"]
        (grad_down,), (grad_up,) = ops["down"], ops["up"]
        grad_qkv, grad_out = ops["last"]
        total_sums = ops["sums"].reshape(-1)
    else:
        down_a = big_whole(d_left, hid_own, hid_own_get, hid_oth, hid_oth_get)
        gp_oth, bs_oth, g_total = ffn_bwd(sc, line.put(g_down), slope_oth, ups, downs, split)
        line.mark(gp_oth)
        gp_oth_get = swap(gp_oth, "seq", 1)
        gp_own, bs_own, g_total = ffn_bwd(sc, line.put(g_down), slope_own, (w_up,), (w_down,), "own", g_total)
        line.mark(gp_own)
        gp_own_get = swap(gp_own, "seq", 1)
        g_one, g_att_low, g_att, sums_one = norm_one_back(sc, line.put(g_two), g_total, hat, inv, gain_a, w_out)
        line.mark(g_att)
        g_att_get = swap(g_att_low, "seq", 1)
        up_a = big_whole(n_left, gp_own, gp_own_get, gp_oth, gp_oth_get)
        g_qkv, sums_att = attend_back(sc, line.put(qkv), att, g_att, logs)
        line.mark(g_qkv)
        g_qkv_get = swap(g_qkv, "seq", 1)
        b_up_sums = jnp.concatenate([bs_own.reshape(1, units), bs_oth.reshape(n_ffn - 1, units)])
        b_up_sums = jnp.take(b_up_sums, order, axis=0).reshape(-1)
        sums = jnp.concatenate(
            [sums_two[:3].reshape(-1), sums_one[:3].reshape(-1), b_up_sums, sums_att.reshape(-1)]
        )
        grad_tokens, grad_fill = token_grads(sc, line.put(g_qkv), w_qkv, g_one, spots, slots)
        line.mark(grad_tokens)
        out = narrow_whole((att_keep, att_get), g_att_low, g_att_get)
        qkv_a = narrow_whole((x_keep, x_get), g_qkv, g_qkv_get)
        (*_, total_sums) = all_sum(line, sums, n_seq, n_ffn)
        grad_down, grad_up = columns_of(down_a.finish()).T, columns_of(up_a.finish())
        grad_out, grad_qkv = columns_of(out.finish()), columns_of(qkv_a.finish())
    hidden_units = n_ffn * units

    part = lambda v, n: v[n * width : (n + 1) * width]
    return (
        output,
        grad_tokens,
        grad_fill[None],
        grad_qkv,
        total_sums[6 * width + hidden_units : 7 * width + hidden_units],
        total_sums[7 * width + hidden_units : 8 * width + hidden_units],
        grad_out,
        part(total_sums, 5),
        part(total_sums, 3),
        part(total_sums, 4),
        grad_up,
        total_sums[6 * width : 6 * width + hidden_units],
        grad_down,
        part(total_sums, 2),
        part(total_sums, 0),
        part(total_sums, 1),
    )


def solution(mesh):
    rows = ("seq", "ffn")
    in_specs = (
        P(rows, None),
        P(rows, None),
        P(rows),
        P(rows, None, None),
        P(rows, None, None),
        P(),
        P(),
        P(),
        P(),
        P(),
        P(),
        P(),
        P(None, "ffn"),
        P("ffn"),
        P("ffn", None),
        P(),
        P(),
        P(),
    )
    out_specs = (
        P(rows, None),
        P(rows, None),
        P(rows, None, None),
        P("seq", "ffn"),
        P(),
        P(),
        P("seq", "ffn"),
        P(),
        P(),
        P(),
        P("seq", "ffn"),
        P(),
        P("ffn", "seq"),
        P(),
        P(),
        P(),
    )
    return jax.shard_map(on_device, mesh=mesh, in_specs=in_specs, out_specs=out_specs, check_vma=False)
```
